512 devices in a mesh: band: 16 (over z), space: 32 (over y, x, core).
Axes of the slice: x: 4, y: 4, z: 16, core: 2. Of those that a mesh axis runs over, the one named last changes fastest.
Arguments:
- orbitals: float32 [2, 64, 96, 9216], P(None, 'band', 'space'), may hold values from -6 to 6
- potential: float32 [96, 9216], P('space'), may hold values from -2 to 4
- occupations: float32 [64], P('band'), may hold values from 0.5 to 2
Outputs:
- propagated: float32 [2, 64, 96, 9216], P(None, 'band', 'space')
- density: float32 [96, 9216], P('space')
- hartree: float32 [96, 9216], P('space')
The draws below stay inside these ranges and needn't reach their ends.
All inputs are finite; a program needn't handle non-finite values.
Results may differ from the reference program's by a relative error of at most 0.0029.
Values may be sent and summed in bfloat16 or wider, within the bound.
A program may use at most 64 MiB of HBM per device.

```python
import math
from functools import partial
import jax
import jax.numpy as jnp
from jax import lax

NX = 96
NY = 96
NZ = 96
ORBITALS = 64


def draw_orbitals(key, part):
    shape = (2, ORBITALS, NX, NY * NZ)
    values = jax.random.normal(jax.random.fold_in(key, 11), shape, jnp.float32)
    return jnp.clip(values, -6.0, 6.0)


def draw_potential(key, part):
    shape = (NX, NY * NZ)
    return jax.random.uniform(jax.random.fold_in(key, 43), shape, jnp.float32, -2.0, 4.0)


def block_levels(own_key, dims, cuts, least, largest):
    def one(position, parts):
        draws = jax.random.uniform(jax.random.fold_in(jax.random.fold_in(own_key, 6), position), (parts,), jnp.float32, least / len(cuts), largest / len(cuts))
        return jnp.repeat(jnp.exp(draws), dims[position] // parts).reshape((-1,) + (1,) * (len(dims) - position - 1))

    factor_of = one(*cuts[0])
    for cut in cuts[1:]:
        factor_of = factor_of * one(*cut)
    return factor_of


def setup_inputs(seed: int = 0) -> dict:
    streams_of = jax.random.split(jax.random.key(seed), 4)
    orbitals = draw_orbitals(jax.random.fold_in(streams_of[3], 71), 0)
    potential = draw_potential(jax.random.fold_in(streams_of[3], 71), 0)
    occupations = jnp.clip(jnp.exp(math.log(2.0) - 1.3862944 * jax.random.uniform(streams_of[2], (ORBITALS,), jnp.float32) ** block_levels(streams_of[2], (ORBITALS,), ((0, 16),), -0.2, 0.2)), 0.5, 2.0)
    return {"orbitals": orbitals, "potential": potential, "occupations": occupations}


stencil_coeffs = (-205.0 / 72.0, 8.0 / 5.0, -1.0 / 5.0, 8.0 / 315.0, -1.0 / 560.0)
energy_shift = 6.0
energy_scale = 8.0
bessel_terms = (0.7651976865579666, 0.44005058574493355, 0.11490348493190049)


def neighbour(padded, dimension, offset, reach_cells, shape):
    starts = [0, reach_cells, reach_cells, reach_cells]
    starts[dimension] = starts[dimension] + offset
    limits = [opening + extent for opening, extent in zip(starts, shape)]
    return lax.slice(padded, starts, limits)


def scaled_operator(center, grid_potential):
    reach_cells = len(stencil_coeffs) - 1
    rounded = lax.optimization_barrier(center.astype(jnp.bfloat16)).astype(jnp.float32)
    widths = ((0, 0), (reach_cells, reach_cells), (reach_cells, reach_cells), (reach_cells, reach_cells))
    padded = jnp.pad(rounded, widths)
    summed = (3.0 * stencil_coeffs[0]) * center
    for offset in range(1, reach_cells + 1):
        for dimension in (1, 2, 3):
            after = neighbour(padded, dimension, offset, reach_cells, center.shape)
            before = neighbour(padded, dimension, -offset, reach_cells, center.shape)
            summed = summed + stencil_coeffs[offset] * (after + before)
    energy = -0.5 * summed + grid_potential * center
    return (energy - energy_shift * center) / energy_scale


def propagate_one(orbital_pair, grid_potential):
    start = orbital_pair.reshape(2, NX, NY, NZ)
    first = scaled_operator(start, grid_potential)
    second = 2.0 * scaled_operator(first, grid_potential) - start
    real_out = bessel_terms[0] * start[0] + 2.0 * bessel_terms[1] * first[1] - 2.0 * bessel_terms[2] * second[0]
    imag_out = bessel_terms[0] * start[1] - 2.0 * bessel_terms[1] * first[0] - 2.0 * bessel_terms[2] * second[1]
    return jnp.stack([real_out, imag_out]).reshape(2, NX, NY * NZ)


def squared_waves(length):
    indices = lax.iota(jnp.int32, length)
    signed = jnp.where(indices < (length + 1) // 2, indices, indices - length).astype(jnp.float32)
    return (2.0 * math.pi / length * signed) ** 2


def reference(orbitals, potential, occupations):
    grid_potential = potential.reshape(NX, NY, NZ)
    moved = jnp.moveaxis(orbitals, 1, 0)
    results = lax.map(partial(propagate_one, grid_potential=grid_potential), moved)
    propagated = jnp.moveaxis(results, 0, 1)
    weights = occupations / ORBITALS
    density = jnp.sum(weights[:, None, None] * (propagated[0] * propagated[0] + propagated[1] * propagated[1]), axis=0)
    squares = squared_waves(NX)[:, None, None] + squared_waves(NY)[None, :, None] + squared_waves(NZ)[None, None, :]
    kernel = jnp.where(squares > 0, 4.0 * math.pi / jnp.where(squares > 0, squares, 1.0), 0.0)
    spectral = jnp.fft.fftn(density.reshape(NX, NY, NZ))
    hartree = jnp.real(jnp.fft.ifftn(spectral * kernel)).reshape(NX, NY * NZ).astype(jnp.float32)
    return propagated, density, hartree
```

```python
import functools
import math

import jax
import jax.numpy as jnp
import ml_dtypes
import numpy as np
from jax import lax
from jax.experimental import pallas as pl
from jax.experimental.pallas import tpu as pltpu
from jax.sharding import PartitionSpec as P

NX = 96
NY = 96
NZ = 96

stencil_coeffs = (-205.0 / 72.0, 8.0 / 5.0, -1.0 / 5.0, 8.0 / 315.0, -1.0 / 560.0)
energy_shift = 6.0
energy_scale = 8.0
bessel_terms = (0.7651976865579666, 0.44005058574493355, 0.11490348493190049)
scaled_coeffs = tuple(c / stencil_coeffs[1] for c in stencil_coeffs)

MESH = pl.DeviceIdType.MESH
PLANES = 3
FIELDS = 8
CELLS = NY * NZ
FOLD = CELLS // 2
BLOCK = 4 * NZ
BLOCKS = CELLS // BLOCK
CHUNKS = 4
CHUNK = FOLD // CHUNKS
PER_CHUNK = CHUNK // BLOCK
WINDOW = 3 * BLOCK
PADDED = FOLD + 2 * BLOCK
SPACE = 32
BAND = 16
OWNERS = 9
ORBITALS = 64


def band_matrix():
    table = np.zeros((WINDOW, BLOCK))
    for cell in range(BLOCK):
        z = cell % NZ
        for offset in range(1, 5):
            c = scaled_coeffs[offset]
            table[BLOCK + cell + offset * NZ, cell] += c
            table[BLOCK + cell - offset * NZ, cell] += c
            if z + offset < NZ:
                table[BLOCK + cell + offset, cell] += c
            if z - offset >= 0:
                table[BLOCK + cell - offset, cell] += c
    return table.astype(ml_dtypes.bfloat16)


def real_basis(length):
    cells = np.arange(length)
    rows = [np.full(length, 1.0 / math.sqrt(length))]
    waves = [0]
    for k in range(1, length // 2):
        phase = 2.0 * math.pi * ((k * cells) % length) / length
        rows.append(math.sqrt(2.0 / length) * np.cos(phase))
        rows.append(math.sqrt(2.0 / length) * np.sin(phase))
        waves += [k, k]
    rows.append(np.where(cells % 2 == 0, 1.0, -1.0) / math.sqrt(length))
    waves.append(length // 2)
    return np.stack(rows), (2.0 * math.pi / length * np.array(waves)) ** 2


def transform_tables():
    basis, squares = real_basis(NY)
    order = np.array([4 * block + r for r in range(4) for block in range(BLOCKS)])
    forward_y = basis[:, order]
    lanes = np.arange(128)
    spread = np.stack([basis[lanes % 64], basis[64 + lanes % 32]])
    forward_z = np.zeros((4, NZ, 4, 2, 128))
    for r in range(4):
        forward_z[r, :, r] = np.transpose(spread, (2, 0, 1))
    forward_z = forward_z.reshape(BLOCK, 1024)
    row = np.arange(72)[:, None]
    mode_y = np.where(row < 48, row + 48 * (lanes >= 64), row - 48 + 24 * (lanes // 32))
    mode_z = np.where(row < 48, lanes % 64, 64 + lanes % 32)
    across = squares[mode_y] + squares[mode_z]
    cells = np.arange(NX)
    signed = np.where(cells < NX // 2, cells, cells - NX)
    along = (2.0 * math.pi / NX * signed) ** 2
    total = along[:, None, None] + across
    kernel = np.where(total > 0, 4.0 * math.pi / np.where(total > 0, total, 1.0), 0.0)
    green = np.real(np.fft.ifft(kernel, axis=0))
    green = green[(np.arange(NX + 2) - 2) % NX]
    green = green.reshape(NX + 2, OWNERS, 8, 128).transpose(1, 0, 2, 3)
    f32 = np.float32
    return (
        forward_z.astype(f32),
        forward_y.astype(f32),
        forward_y.T.copy().astype(f32),
        forward_z.T.copy().astype(f32),
        green.astype(f32),
    )


def exact_dot(a, b):
    return lax.dot_general(
        a,
        b,
        (((1,), (0,)), ((), ())),
        precision=lax.Precision.HIGHEST,
        preferred_element_type=jnp.float32,
    )


def body(
    orb_hbm, pot_ref, occ_ref, band_hbm, fz_hbm, fy_hbm, iy_hbm, iz_hbm, green_hbm,
    prop_hbm, dens_ref, hart_ref,
    field, first, prop, own0, own1, rim0, rim1, lines,
    band_ref, fz_ref, fy_ref, iy_ref, iz_ref, green_ref,
    modes, shares, summed, layer, answer, dens_modes, hart_modes,
    load_sem, table_sem, store_sem, halo_send, halo_recv,
    share_send, share_recv, layer_send, layer_recv, dens_send, dens_recv, hart_send, hart_recv,
):
    s = lax.axis_index("space")
    z = lax.axis_index("band")
    core = lax.rem(s, 2)
    f32 = jnp.float32
    bf16 = jnp.bfloat16

    loads = [
        pltpu.make_async_copy(orb_hbm.at[part], field.at[:, pl.ds(4 * part, 4), :], load_sem.at[part])
        for part in range(2)
    ]
    for copy in loads:
        copy.start()
    owner = (OWNERS * z + BAND - 1) // BAND
    owner_index = jnp.minimum(owner, OWNERS - 1)
    is_owner = (BAND * owner) // OWNERS == z
    tables = [
        pltpu.make_async_copy(src, dst, table_sem.at[i])
        for i, (src, dst) in enumerate(
            [
                (band_hbm, band_ref),
                (fz_hbm, fz_ref),
                (fy_hbm, fy_ref),
                (iy_hbm, iy_ref),
                (iz_hbm, iz_ref),
                (green_hbm.at[owner_index], green_ref),
            ]
        )
    ]
    for copy in tables:
        copy.start()

    barrier = pltpu.get_barrier_semaphore()

    def greet_space(k, carry):
        pl.semaphore_signal(
            barrier, inc=1, device_id={"space": lax.rem(s + k, SPACE)}, device_id_type=MESH
        )
        return carry

    def greet_band(k, carry):
        pl.semaphore_signal(
            barrier, inc=1, device_id={"band": lax.rem(z + k, BAND)}, device_id_type=MESH
        )
        return carry

    lax.fori_loop(1, BAND, greet_band, 0)
    lax.fori_loop(1, SPACE, greet_space, 0)

    def lanes_of(c, extra=0, size=CHUNK):
        return pl.ds(pl.multiple_of(c * CHUNK + extra, 128), size)

    outward = 2 * core - 1
    owns = (own0, own1)
    rims = (rim0, rim1)

    def halo(phase, kind, c):
        own, rim = owns[phase], rims[phase]
        inside = lanes_of(c, BLOCK)
        outside = lanes_of(c)
        if kind == 0:
            src = own.at[:, :, inside]
            dst = rim.at[1 - core, pl.ds(core, 3), :, outside]
            step = outward
        elif kind == 1:
            src = own.at[:, :, inside]
            dst = rim.at[core, pl.ds(1 - core, 3), :, outside]
            step = -outward
        elif kind == 2:
            src = own.at[2 * (1 - core), :, inside]
            dst = rim.at[core, 3 * core, :, outside]
            step = -2 * outward
        else:
            src = rim.at[core, 3 * (1 - core), :, outside]
            dst = rim.at[core, 3 * core, :, outside]
            step = -outward
        return pltpu.make_async_remote_copy(
            src_ref=src,
            dst_ref=dst,
            send_sem=halo_send.at[phase, kind, c],
            recv_sem=halo_recv.at[phase, kind, c],
            device_id={"space": lax.rem(s + step + SPACE, SPACE)},
            device_id_type=MESH,
        )

    def fold_edges(source, own):
        zeros = jnp.zeros((FIELDS, BLOCK), f32)
        for p in range(PLANES):
            own[p, :, 0:BLOCK] = jnp.concatenate(
                [zeros, source[p, :, FOLD - BLOCK : FOLD]], axis=0
            ).astype(bf16)
            own[p, :, PADDED - BLOCK : PADDED] = jnp.concatenate(
                [source[p, :, FOLD : FOLD + BLOCK], zeros], axis=0
            ).astype(bf16)

    for copy in loads:
        copy.wait()
    pl.semaphore_wait(barrier, SPACE + BAND - 2)

    def ship(c, carry):
        for p in range(PLANES):
            own0[p, :, lanes_of(c, BLOCK)] = jnp.concatenate(
                [field[p, :, lanes_of(c)], field[p, :, lanes_of(c, FOLD)]], axis=0
            ).astype(bf16)
        for kind in range(3):
            halo(0, kind, c).start()
        return carry

    lax.fori_loop(0, CHUNKS, ship, 0)
    fold_edges(field, own0)
    tables[0].wait()

    near_left = jnp.where(s >= 1, 1.0, 0.0).astype(f32)
    far_left = jnp.where(s >= 2, 1.0, 0.0).astype(f32)
    near_right = jnp.where(s <= SPACE - 2, 1.0, 0.0).astype(f32)
    far_right = jnp.where(s <= SPACE - 3, 1.0, 0.0).astype(f32)
    left_weights = (far_left, near_left, near_left, near_left)
    right_weights = (near_right, near_right, near_right, far_right)

    gain = stencil_coeffs[1] / (2.0 * energy_scale)
    level = -(energy_shift + 1.5 * stencil_coeffs[0]) / energy_scale

    def arrive(phase, c):
        halo(phase, 0, c).wait_recv()
        halo(phase, 3, c).start()
        for kind in (1, 2, 3):
            halo(phase, kind, c).wait_recv()

    def stencil(phase, source, c, finish):
        own, rim = owns[phase], rims[phase]
        windows = [
            own[p, :, lanes_of(c, b * BLOCK, WINDOW)]
            for p in range(PLANES)
            for b in range(PER_CHUNK)
        ]
        flat = jnp.dot(
            jnp.concatenate(windows, axis=0), band_ref[...], preferred_element_type=f32
        )
        for b in range(PER_CHUNK):
            outside = lanes_of(c, b * BLOCK, BLOCK)
            inside = lanes_of(c, (b + 1) * BLOCK, BLOCK)
            stack = [rim[0, k, :, outside].astype(f32) * left_weights[k] for k in range(4)]
            stack += [own[p, :, inside].astype(f32) for p in range(PLANES)]
            stack += [rim[1, k, :, outside].astype(f32) * right_weights[k] for k in range(4)]
            for p in range(PLANES):
                across = stack[p + 5] + stack[p + 3]
                for offset in range(2, 5):
                    across = across + scaled_coeffs[offset] * (
                        stack[p + 4 + offset] + stack[p + 4 - offset]
                    )
                at = 16 * (p * PER_CHUNK + b)
                across = gain * (across + flat[at : at + 16])
                for half in range(2):
                    lanes = lanes_of(c, half * FOLD + b * BLOCK, BLOCK)
                    centre = source[p, :, lanes]
                    factor = pot_ref[p : p + 1, lanes] * (1.0 / energy_scale) + level
                    value = centre * factor - across[8 * half : 8 * half + 8]
                    finish(p, b, half, lanes, centre, value)

    def first_chunk(c, carry):
        arrive(0, c)
        values = {}

        def finish(p, b, half, lanes, centre, value):
            first[p, :, lanes] = value
            values[p, b, half] = value
            if half == 1:
                own1[p, :, lanes_of(c, (b + 1) * BLOCK, BLOCK)] = jnp.concatenate(
                    [values[p, b, 0], value], axis=0
                ).astype(bf16)

        stencil(0, field, c, finish)
        for kind in range(3):
            halo(1, kind, c).start()
        return carry

    lax.fori_loop(0, CHUNKS, first_chunk, 0)
    fold_edges(first, own1)

    rows = lax.broadcasted_iota(jnp.int32, (FIELDS, BLOCK), 0)
    weight = jnp.zeros((FIELDS, BLOCK), f32)
    for o in range(4):
        weight = jnp.where(lax.rem(rows, 4) == o, occ_ref[o] * (1.0 / ORBITALS), weight)
    sign = jnp.where(rows < 4, 2.0 * bessel_terms[1], -2.0 * bessel_terms[1]).astype(f32)

    def stores(c, half, part):
        lanes = lanes_of(c, half * FOLD)
        return pltpu.make_async_copy(
            prop.at[:, pl.ds(4 * part, 4), lanes],
            prop_hbm.at[part, :, :, lanes],
            store_sem.at[c, half, part],
        )

    def second_chunk(c, carry):
        arrive(1, c)

        def finish(p, b, half, lanes, centre, value):
            swapped = jnp.concatenate([centre[4:8], centre[0:4]], axis=0)
            result = (
                (bessel_terms[0] + 2.0 * bessel_terms[2]) * field[p, :, lanes]
                + sign * swapped
                - (4.0 * bessel_terms[2]) * value
            )
            prop[p, :, lanes] = result
            share = jnp.sum(weight * (result * result), axis=0, keepdims=True)
            lines[pl.ds(p * BLOCKS + half * (BLOCKS // 2) + c * PER_CHUNK + b, 1), :] = share

        stencil(1, first, c, finish)
        for half in range(2):
            for part in range(2):
                stores(c, half, part).start()
        return carry

    lax.fori_loop(0, CHUNKS, second_chunk, 0)

    for copy in tables[1:]:
        copy.wait()
    turned = exact_dot(lines[...], fz_ref[...])
    stacked = jnp.concatenate(
        [
            jnp.concatenate(
                [
                    turned[p * BLOCKS : (p + 1) * BLOCKS, r * 256 : (r + 1) * 256]
                    for r in range(4)
                ],
                axis=0,
            )
            for p in range(PLANES)
        ],
        axis=1,
    )
    spectral = exact_dot(fy_ref[...], stacked)
    lane = lax.broadcasted_iota(jnp.int32, (1, 128), 1)
    for p in range(PLANES):
        wide = spectral[:, p * 256 : p * 256 + 128]
        tail = spectral[:, p * 256 + 128 : (p + 1) * 256]
        head = jnp.where(lane < 64, wide[0:48], wide[48:96])
        rest = tail[0:24]
        for quarter in range(1, 4):
            rest = jnp.where(lane >= 32 * quarter, tail[24 * quarter : 24 * quarter + 24], rest)
        for o in range(6):
            modes[o, p] = head[8 * o : 8 * o + 8]
        for o in range(3):
            modes[6 + o, p] = rest[8 * o : 8 * o + 8]

    def share_copy(o, source):
        return pltpu.make_async_remote_copy(
            src_ref=modes.at[o],
            dst_ref=shares.at[source],
            send_sem=share_send.at[o],
            recv_sem=share_recv.at[source],
            device_id={"band": (BAND * o) // OWNERS},
            device_id_type=MESH,
        )

    for o in range(OWNERS):
        @pl.when((BAND * o) // OWNERS != z)
        def _():
            share_copy(o, z).start()

    def layer_copy(k):
        return pltpu.make_async_remote_copy(
            src_ref=summed,
            dst_ref=layer.at[SPACE - k],
            send_sem=layer_send.at[k],
            recv_sem=layer_recv.at[SPACE - k],
            device_id={"space": lax.rem(s + k, SPACE)},
            device_id_type=MESH,
        )

    def band_copy(src, dst, send, recv, k):
        return pltpu.make_async_remote_copy(
            src_ref=src,
            dst_ref=dst.at[owner_index],
            send_sem=send.at[k],
            recv_sem=recv.at[owner_index],
            device_id={"band": lax.rem(z + k, BAND)},
            device_id_type=MESH,
        )

    @pl.when(is_owner)
    def _():
        def collect(k, total):
            source = lax.rem(z + k, BAND)
            pltpu.make_async_copy(modes.at[0], shares.at[source], share_recv.at[source]).wait()
            return total + shares[source]

        total = lax.fori_loop(1, BAND, collect, modes[owner_index])
        summed[...] = total
        layer[0] = total
        dens_modes[owner_index] = total

        def out_layer(k, carry):
            layer_copy(k).start()
            return carry

        lax.fori_loop(1, SPACE, out_layer, 0)

        def out_dens(k, carry):
            band_copy(summed, dens_modes, dens_send, dens_recv, k).start()
            return carry

        lax.fori_loop(1, BAND, out_dens, 0)

        def apply(r, total):
            out = list(total)
            for q in range(PLANES):
                value = layer[r, q]
                for p in range(PLANES):
                    out[p] = out[p] + green_ref[3 * r + q - p + 2] * value
            return tuple(out)

        def collect_layer(r, total):
            pltpu.make_async_copy(summed, layer.at[r], layer_recv.at[r]).wait()
            return apply(r, total)

        zero = jnp.zeros((8, 128), f32)
        result = lax.fori_loop(1, SPACE, collect_layer, apply(0, (zero, zero, zero)))
        for p in range(PLANES):
            answer[p] = result[p]
            hart_modes[owner_index, p] = result[p]

        def out_hart(k, carry):
            band_copy(answer, hart_modes, hart_send, hart_recv, k).start()
            return carry

        lax.fori_loop(1, BAND, out_hart, 0)

    def back(spec_ref):
        pieces = []
        for p in range(PLANES):
            head = jnp.concatenate([spec_ref[o, p] for o in range(6)], axis=0)
            rest = jnp.concatenate([spec_ref[6 + o, p] for o in range(3)], axis=0)
            upper = jnp.concatenate(
                [jnp.where(lane < 64, head, 0.0), jnp.where(lane >= 64, head, 0.0)], axis=0
            )
            lower = jnp.concatenate(
                [jnp.where(lane // 32 == quarter, rest, 0.0) for quarter in range(4)], axis=0
            )
            pieces += [upper, lower]
        rows_y = exact_dot(iy_ref[...], jnp.concatenate(pieces, axis=1))
        flat = jnp.concatenate(
            [
                jnp.concatenate(
                    [
                        rows_y[r * BLOCKS : (r + 1) * BLOCKS, p * 256 : (p + 1) * 256]
                        for r in range(4)
                    ],
                    axis=1,
                )
                for p in range(PLANES)
            ],
            axis=0,
        )
        return exact_dot(flat, iz_ref[...])

    def put(out_ref, values):
        for p in range(PLANES):
            for block in range(BLOCKS):
                at = p * BLOCKS + block
                out_ref[p : p + 1, block * BLOCK : (block + 1) * BLOCK] = values[at : at + 1]

    def gathered(dst, recv):
        for o in range(OWNERS):
            @pl.when((BAND * o) // OWNERS != z)
            def _():
                pltpu.make_async_copy(summed, dst.at[o], recv.at[o]).wait()

    gathered(dens_modes, dens_recv)
    put(dens_ref, back(dens_modes))
    gathered(hart_modes, hart_recv)
    put(hart_ref, back(hart_modes))

    @pl.when(is_owner)
    def _():
        def drain_layer(k, carry):
            layer_copy(k).wait_send()
            return carry

        lax.fori_loop(1, SPACE, drain_layer, 0)

        def drain_band(k, carry):
            band_copy(summed, dens_modes, dens_send, dens_recv, k).wait_send()
            band_copy(answer, hart_modes, hart_send, hart_recv, k).wait_send()
            return carry

        lax.fori_loop(1, BAND, drain_band, 0)

    for o in range(OWNERS):
        @pl.when((BAND * o) // OWNERS != z)
        def _():
            share_copy(o, z).wait_send()

    def drain(c, carry):
        for phase in range(2):
            for kind in range(4):
                halo(phase, kind, c).wait_send()
        for half in range(2):
            for part in range(2):
                stores(c, half, part).wait()
        return carry

    lax.fori_loop(0, CHUNKS, drain, 0)


def per_device(orbitals, potential, occupations):
    f32 = jnp.float32
    bf16 = jnp.bfloat16
    forward_z, forward_y, inverse_y, inverse_z, green = transform_tables()
    vmem = pltpu.VMEM
    dma = pltpu.SemaphoreType.DMA
    anywhere = pl.BlockSpec(memory_space=pl.ANY)
    whole = pl.BlockSpec(memory_space=pltpu.VMEM)
    prop, dens, hart = pl.pallas_call(
        body,
        out_shape=(
            jax.ShapeDtypeStruct((2, PLANES, 4, CELLS), f32),
            jax.ShapeDtypeStruct((PLANES, CELLS), f32),
            jax.ShapeDtypeStruct((PLANES, CELLS), f32),
        ),
        in_specs=[anywhere, whole, pl.BlockSpec(memory_space=pltpu.SMEM)] + [anywhere] * 6,
        out_specs=(anywhere, whole, whole),
        scratch_shapes=[
            vmem((PLANES, FIELDS, CELLS), f32),
            vmem((PLANES, FIELDS, CELLS), f32),
            vmem((PLANES, FIELDS, CELLS), f32),
            vmem((PLANES, 16, PADDED), bf16),
            vmem((PLANES, 16, PADDED), bf16),
            vmem((2, 4, 16, FOLD), bf16),
            vmem((2, 4, 16, FOLD), bf16),
            vmem((PLANES * BLOCKS, BLOCK), f32),
            vmem((WINDOW, BLOCK), bf16),
            vmem((BLOCK, 1024), f32),
            vmem((NY, NY), f32),
            vmem((NY, NY), f32),
            vmem((1024, BLOCK), f32),
            vmem((NX + 2, 8, 128), f32),
            vmem((OWNERS, PLANES, 8, 128), f32),
            vmem((BAND, PLANES, 8, 128), f32),
            vmem((PLANES, 8, 128), f32),
            vmem((SPACE, PLANES, 8, 128), f32),
            vmem((PLANES, 8, 128), f32),
            vmem((OWNERS, PLANES, 8, 128), f32),
            vmem((OWNERS, PLANES, 8, 128), f32),
            dma((2,)),
            dma((6,)),
            dma((CHUNKS, 2, 2)),
            dma((2, 4, CHUNKS)),
            dma((2, 4, CHUNKS)),
            dma((OWNERS,)),
            dma((BAND,)),
            dma((SPACE,)),
            dma((SPACE,)),
            dma((BAND,)),
            dma((OWNERS,)),
            dma((BAND,)),
            dma((OWNERS,)),
        ],
        compiler_params=pltpu.CompilerParams(
            collective_id=0, has_side_effects=True, vmem_limit_bytes=40 * 2**20
        ),
    )(
        jnp.transpose(orbitals, (0, 2, 1, 3)),
        potential,
        occupations,
        jnp.asarray(band_matrix()),
        jnp.asarray(forward_z),
        jnp.asarray(forward_y),
        jnp.asarray(inverse_y),
        jnp.asarray(inverse_z),
        jnp.asarray(green),
    )
    return jnp.transpose(prop, (0, 2, 1, 3)), dens, hart


def solution(mesh):
    in_specs = (P(None, "band", "space", None), P("space", None), P("band"))
    out_specs = (P(None, "band", "space", None), P("space", None), P("space", None))
    return jax.shard_map(
        per_device, mesh=mesh, in_specs=in_specs, out_specs=out_specs, check_vma=False
    )
```

```python
import functools
import math

import jax
import jax.numpy as jnp
import ml_dtypes
import numpy as np
from jax import lax
from jax.experimental import pallas as pl
from jax.experimental.pallas import tpu as pltpu
from jax.sharding import PartitionSpec as P

NX = 96
NY = 96
NZ = 96

stencil_coeffs = (-205.0 / 72.0, 8.0 / 5.0, -1.0 / 5.0, 8.0 / 315.0, -1.0 / 560.0)
energy_shift = 6.0
energy_scale = 8.0
bessel_terms = (0.7651976865579666, 0.44005058574493355, 0.11490348493190049)
scaled_coeffs = tuple(c / stencil_coeffs[1] for c in stencil_coeffs)

MESH = pl.DeviceIdType.MESH
PLANES = 3
FIELDS = 8
CELLS = NY * NZ
FOLD = CELLS // 2
BLOCK = 4 * NZ
BLOCKS = CELLS // BLOCK
CHUNKS = 4
CHUNK = FOLD // CHUNKS
PER_CHUNK = CHUNK // BLOCK
WINDOW = 3 * BLOCK
PADDED = FOLD + 2 * BLOCK
SPACE = 32
BAND = 16
OWNERS = 9
ORBITALS = 64


def band_matrix():
    table = np.zeros((WINDOW, BLOCK))
    for cell in range(BLOCK):
        z = cell % NZ
        for offset in range(1, 5):
            c = scaled_coeffs[offset]
            table[BLOCK + cell + offset * NZ, cell] += c
            table[BLOCK + cell - offset * NZ, cell] += c
            if z + offset < NZ:
                table[BLOCK + cell + offset, cell] += c
            if z - offset >= 0:
                table[BLOCK + cell - offset, cell] += c
    return table.astype(ml_dtypes.bfloat16)


def real_basis(length):
    cells = np.arange(length)
    rows = [np.full(length, 1.0 / math.sqrt(length))]
    waves = [0]
    for k in range(1, length // 2):
        phase = 2.0 * math.pi * ((k * cells) % length) / length
        rows.append(math.sqrt(2.0 / length) * np.cos(phase))
        rows.append(math.sqrt(2.0 / length) * np.sin(phase))
        waves += [k, k]
    rows.append(np.where(cells % 2 == 0, 1.0, -1.0) / math.sqrt(length))
    waves.append(length // 2)
    return np.stack(rows), (2.0 * math.pi / length * np.array(waves)) ** 2


def split(table):
    high = table.astype(ml_dtypes.bfloat16)
    low = (table - high.astype(np.float64)).astype(ml_dtypes.bfloat16)
    return high, low


def transform_tables():
    basis, squares = real_basis(NY)
    order = np.array([4 * block + r for r in range(4) for block in range(BLOCKS)])
    forward_y = basis[:, order]
    lanes = np.arange(128)
    spread = np.stack([basis[lanes % 64], basis[64 + lanes % 32]])
    forward_z = np.zeros((4, NZ, 4, 2, 128))
    for r in range(4):
        forward_z[r, :, r] = np.transpose(spread, (2, 0, 1))
    forward_z = forward_z.reshape(BLOCK, 1024)
    row = np.arange(72)[:, None]
    mode_y = np.where(row < 48, row + 48 * (lanes >= 64), row - 48 + 24 * (lanes // 32))
    mode_z = np.where(row < 48, lanes % 64, 64 + lanes % 32)
    across = squares[mode_y] + squares[mode_z]
    cells = np.arange(NX)
    signed = np.where(cells < NX // 2, cells, cells - NX)
    along = (2.0 * math.pi / NX * signed) ** 2
    total = along[:, None, None] + across
    kernel = np.where(total > 0, 4.0 * math.pi / np.where(total > 0, total, 1.0), 0.0)
    green = np.real(np.fft.ifft(kernel, axis=0))
    green = green[(np.arange(NX + 5) - 5) % NX]
    green = green.reshape(NX + 5, OWNERS, 8, 128).transpose(1, 0, 2, 3)
    f32 = np.float32
    y_high, y_low = split(forward_y.T)
    z_high, z_low = split(forward_z.T)
    return (
        forward_z.astype(f32),
        forward_y.astype(f32),
        np.concatenate([y_high, y_low], axis=1),
        np.concatenate([z_high, z_low], axis=0),
        green.astype(f32),
    )


def exact_dot(a, b):
    return lax.dot_general(
        a,
        b,
        (((1,), (0,)), ((), ())),
        precision=lax.Precision.HIGHEST,
        preferred_element_type=jnp.float32,
    )


def body(
    orb_hbm, pot_hbm, occ_ref, band_hbm, fz_hbm, fy_hbm, iy_hbm, iz_hbm, green_hbm,
    prop_hbm, dens_ref, hart_ref,
    pot_ref, field, first, prop, own0, own1, rim0, rim1, lines,
    band_ref, fz_ref, fy_ref, iy_ref, iz_ref, green_ref,
    modes, shares, summed, layer, partial, crossed, dens_own, hart_own, dens_modes, hart_modes,
    load_sem, table_sem, store_sem, halo_send, halo_recv, hand,
    share_send, share_recv, layer_send, layer_recv, cross_sem,
    dens_send, dens_recv, hart_send, hart_recv,
):
    s = lax.axis_index("space")
    z = lax.axis_index("band")
    core = lax.rem(s, 2)
    f32 = jnp.float32
    bf16 = jnp.bfloat16

    def lanes_of(c, extra=0, size=CHUNK):
        return pl.ds(pl.multiple_of(c * CHUNK + extra, 128), size)

    def load(c, half, part):
        lanes = lanes_of(c, half * FOLD)
        return pltpu.make_async_copy(
            orb_hbm.at[part, :, :, lanes],
            field.at[:, pl.ds(4 * part, 4), lanes],
            load_sem.at[c, half, part],
        )

    barrier = pltpu.get_barrier_semaphore()

    def greet(sem, axis, me, size, offset):
        for step in (offset, size - offset):
            pl.semaphore_signal(
                sem, inc=1, device_id={axis: lax.rem(me + step, size)}, device_id_type=MESH
            )

    for offset in (1, 2):
        greet(barrier, "space", s, SPACE, offset)
        greet(barrier, "band", z, BAND, offset)
    for c in range(CHUNKS):
        for half in range(2):
            for part in range(2):
                load(c, half, part).start()
    owner = (OWNERS * z + BAND - 1) // BAND
    owner_index = jnp.minimum(owner, OWNERS - 1)
    is_owner = (BAND * owner) // OWNERS == z
    pot_copy = pltpu.make_async_copy(pot_hbm, pot_ref, table_sem.at[6])
    pot_copy.start()
    tables = [
        pltpu.make_async_copy(src, dst, table_sem.at[i])
        for i, (src, dst) in enumerate(
            [
                (band_hbm, band_ref),
                (fz_hbm, fz_ref),
                (fy_hbm, fy_ref),
                (iy_hbm, iy_ref),
                (iz_hbm, iz_ref),
                (green_hbm.at[owner_index], green_ref),
            ]
        )
    ]
    tables[0].start()

    outward = 2 * core - 1
    owns = (own0, own1)
    rims = (rim0, rim1)

    def halo(phase, kind, c):
        own, rim = owns[phase], rims[phase]
        inside = lanes_of(c, BLOCK)
        outside = lanes_of(c)
        if kind == 0:
            src = own.at[:, :, inside]
            dst = rim.at[1 - core, pl.ds(core, 3), :, outside]
            step = outward
        elif kind == 1:
            src = own.at[:, :, inside]
            dst = rim.at[core, pl.ds(1 - core, 3), :, outside]
            step = -outward
        elif kind == 2:
            src = own.at[2 * (1 - core), :, inside]
            dst = rim.at[core, 3 * core, :, outside]
            step = -2 * outward
        else:
            src = rim.at[core, 3 * (1 - core), :, outside]
            dst = rim.at[core, 3 * core, :, outside]
            step = -outward
        return pltpu.make_async_remote_copy(
            src_ref=src,
            dst_ref=dst,
            send_sem=halo_send.at[phase, kind, c],
            recv_sem=halo_recv.at[phase, kind, c],
            device_id={"space": lax.rem(s + step + SPACE, SPACE)},
            device_id_type=MESH,
        )

    def fold_edges(source, own):
        zeros = jnp.zeros((FIELDS, BLOCK), f32)
        for p in range(PLANES):
            own[p, :, 0:BLOCK] = jnp.concatenate(
                [zeros, source[p, :, FOLD - BLOCK : FOLD]], axis=0
            ).astype(bf16)
            own[p, :, PADDED - BLOCK : PADDED] = jnp.concatenate(
                [source[p, :, FOLD : FOLD + BLOCK], zeros], axis=0
            ).astype(bf16)

    def pack(c, carry):
        for half in range(2):
            for part in range(2):
                load(c, half, part).wait()
        for p in range(PLANES):
            own0[p, :, lanes_of(c, BLOCK)] = jnp.concatenate(
                [field[p, :, lanes_of(c)], field[p, :, lanes_of(c, FOLD)]], axis=0
            ).astype(bf16)
        return carry

    lax.fori_loop(0, CHUNKS, pack, 0)
    pl.semaphore_wait(barrier, 8)

    def ship(c, carry):
        for kind in range(3):
            halo(0, kind, c).start()
        return carry

    lax.fori_loop(0, CHUNKS, ship, 0)
    greet(hand.at[0], "band", z, BAND, 2)
    greet(hand.at[1], "space", s, SPACE, 2)
    fold_edges(field, own0)
    for copy in tables[1:]:
        copy.start()
    tables[0].wait()

    pot_copy.wait()
    near_left = jnp.where(s >= 1, 1.0, 0.0).astype(f32)
    far_left = jnp.where(s >= 2, 1.0, 0.0).astype(f32)
    near_right = jnp.where(s <= SPACE - 2, 1.0, 0.0).astype(f32)
    far_right = jnp.where(s <= SPACE - 3, 1.0, 0.0).astype(f32)
    left_weights = (far_left, near_left, near_left, near_left)
    right_weights = (near_right, near_right, near_right, far_right)

    gain = stencil_coeffs[1] / (2.0 * energy_scale)
    level = -(energy_shift + 1.5 * stencil_coeffs[0]) / energy_scale

    def arrive(phase, c):
        halo(phase, 0, c).wait_recv()
        halo(phase, 3, c).start()
        for kind in (1, 2, 3):
            halo(phase, kind, c).wait_recv()

    def stencil(phase, source, c, finish):
        own, rim = owns[phase], rims[phase]
        windows = [
            own[p, :, lanes_of(c, b * BLOCK, WINDOW)]
            for p in range(PLANES)
            for b in range(PER_CHUNK)
        ]
        flat = jnp.dot(
            jnp.concatenate(windows, axis=0), band_ref[...], preferred_element_type=f32
        )
        for b in range(PER_CHUNK):
            outside = lanes_of(c, b * BLOCK, BLOCK)
            inside = lanes_of(c, (b + 1) * BLOCK, BLOCK)
            stack = [rim[0, k, :, outside].astype(f32) * left_weights[k] for k in range(4)]
            stack += [own[p, :, inside].astype(f32) for p in range(PLANES)]
            stack += [rim[1, k, :, outside].astype(f32) * right_weights[k] for k in range(4)]
            for p in range(PLANES):
                across = stack[p + 5] + stack[p + 3]
                for offset in range(2, 5):
                    across = across + scaled_coeffs[offset] * (
                        stack[p + 4 + offset] + stack[p + 4 - offset]
                    )
                at = 16 * (p * PER_CHUNK + b)
                across = gain * (across + flat[at : at + 16])
                for half in range(2):
                    lanes = lanes_of(c, half * FOLD + b * BLOCK, BLOCK)
                    centre = source[p, :, lanes]
                    factor = pot_ref[p : p + 1, lanes] * (1.0 / energy_scale) + level
                    value = centre * factor - across[8 * half : 8 * half + 8]
                    finish(p, b, half, lanes, centre, value)


    def first_chunk(c, carry):
        arrive(0, c)
        values = {}

        def finish(p, b, half, lanes, centre, value):
            first[p, :, lanes] = value
            values[p, b, half] = value
            if half == 1:
                own1[p, :, lanes_of(c, (b + 1) * BLOCK, BLOCK)] = jnp.concatenate(
                    [values[p, b, 0], value], axis=0
                ).astype(bf16)

        stencil(0, field, c, finish)
        for kind in range(3):
            halo(1, kind, c).start()
        return carry

    lax.fori_loop(0, CHUNKS, first_chunk, 0)
    pl.semaphore_wait(hand.at[0], 2)
    greet(hand.at[2], "band", z, BAND, 4)
    pl.semaphore_wait(hand.at[1], 2)
    greet(hand.at[3], "space", s, SPACE, 4)
    fold_edges(first, own1)

    rows = lax.broadcasted_iota(jnp.int32, (FIELDS, BLOCK), 0)
    weight = jnp.zeros((FIELDS, BLOCK), f32)
    for o in range(4):
        weight = jnp.where(lax.rem(rows, 4) == o, occ_ref[o] * (1.0 / ORBITALS), weight)
    sign = jnp.where(rows < 4, 2.0 * bessel_terms[1], -2.0 * bessel_terms[1]).astype(f32)

    def stores(c, half, part):
        lanes = lanes_of(c, half * FOLD)
        return pltpu.make_async_copy(
            prop.at[:, pl.ds(4 * part, 4), lanes],
            prop_hbm.at[part, :, :, lanes],
            store_sem.at[c, half, part],
        )

    def second_chunk(c, carry):
        arrive(1, c)

        def finish(p, b, half, lanes, centre, value):
            swapped = jnp.concatenate([centre[4:8], centre[0:4]], axis=0)
            result = (
                (bessel_terms[0] + 2.0 * bessel_terms[2]) * field[p, :, lanes]
                + sign * swapped
                - (4.0 * bessel_terms[2]) * value
            )
            prop[p, :, lanes] = result
            share = jnp.sum(weight * (result * result), axis=0, keepdims=True)
            lines[pl.ds(p * BLOCKS + half * (BLOCKS // 2) + c * PER_CHUNK + b, 1), :] = share

        stencil(1, first, c, finish)
        for half in range(2):
            for part in range(2):
                stores(c, half, part).start()
        return carry

    lax.fori_loop(0, CHUNKS, second_chunk, 0)
    pl.semaphore_wait(hand.at[2], 2)
    pl.semaphore_wait(hand.at[3], 2)
    greet(hand.at[4], "space", s, SPACE, 8)

    for copy in tables[1:]:
        copy.wait()
    turned = exact_dot(lines[...], fz_ref[...])
    stacked = jnp.concatenate(
        [
            jnp.concatenate(
                [
                    turned[p * BLOCKS : (p + 1) * BLOCKS, r * 256 : (r + 1) * 256]
                    for r in range(4)
                ],
                axis=0,
            )
            for p in range(PLANES)
        ],
        axis=1,
    )
    spectral = exact_dot(fy_ref[...], stacked)
    lane = lax.broadcasted_iota(jnp.int32, (1, 128), 1)
    for p in range(PLANES):
        wide = spectral[:, p * 256 : p * 256 + 128]
        tail = spectral[:, p * 256 + 128 : (p + 1) * 256]
        head = jnp.where(lane < 64, wide[0:48], wide[48:96])
        rest = tail[0:24]
        for quarter in range(1, 4):
            rest = jnp.where(lane >= 32 * quarter, tail[24 * quarter : 24 * quarter + 24], rest)
        for o in range(6):
            modes[o, p] = head[8 * o : 8 * o + 8]
        for o in range(3):
            modes[6 + o, p] = rest[8 * o : 8 * o + 8]


    def share_copy(o, source):
        return pltpu.make_async_remote_copy(
            src_ref=modes.at[o],
            dst_ref=shares.at[source],
            send_sem=share_send.at[o],
            recv_sem=share_recv.at[source],
            device_id={"band": (BAND * o) // OWNERS},
            device_id_type=MESH,
        )

    def by_distance(i, middle):
        return middle + jnp.where(lax.rem(i, 2) == 0, i // 2, -(i + 1) // 2)

    def out_share(i, carry):
        target = lax.rem(z + by_distance(i, BAND // 2), BAND)
        o = (OWNERS * target + BAND - 1) // BAND

        @pl.when((BAND * o) // OWNERS == target)
        def _():
            share_copy(o, z).start()

        return carry

    lax.fori_loop(0, BAND - 1, out_share, 0)
    pl.semaphore_wait(hand.at[4], 2)

    def layer_copy(k):
        return pltpu.make_async_remote_copy(
            src_ref=summed,
            dst_ref=layer.at[SPACE // 2 - k],
            send_sem=layer_send.at[k],
            recv_sem=layer_recv.at[SPACE // 2 - k],
            device_id={"space": lax.rem(s + 2 * k, SPACE)},
            device_id_type=MESH,
        )

    partner_copy = pltpu.make_async_remote_copy(
        src_ref=partial,
        dst_ref=crossed,
        send_sem=cross_sem.at[0],
        recv_sem=cross_sem.at[1],
        device_id={"space": s - outward},
        device_id_type=MESH,
    )

    def band_copy(src, dst, send, recv, k):
        return pltpu.make_async_remote_copy(
            src_ref=src,
            dst_ref=dst.at[owner_index],
            send_sem=send.at[k],
            recv_sem=recv.at[owner_index],
            device_id={"band": lax.rem(z + k, BAND)},
            device_id_type=MESH,
        )

    def keep(values, ref, gathered_ref):
        upper = jnp.concatenate([values[0], values[1]], axis=0).astype(bf16)
        lower = jnp.concatenate([values[2], jnp.zeros((8, 128), f32)], axis=0).astype(bf16)
        for out in (ref, gathered_ref.at[owner_index]):
            out[0] = upper
            out[1] = lower

    @pl.when(is_owner)
    def _():
        def collect(k, total):
            source = lax.rem(z + k, BAND)
            pltpu.make_async_copy(modes.at[0], shares.at[source], share_recv.at[source]).wait()
            return total + shares[source]

        total = lax.fori_loop(1, BAND, collect, modes[owner_index])
        summed[...] = total
        layer[0] = total

        def out_layer(i, carry):
            layer_copy(by_distance(i, SPACE // 4)).start()
            return carry

        lax.fori_loop(0, SPACE // 2 - 1, out_layer, 0)
        keep([total[p] for p in range(PLANES)], dens_own, dens_modes)

        def out_dens(i, carry):
            band_copy(dens_own, dens_modes, dens_send, dens_recv, by_distance(i, BAND // 2)).start()
            return carry

        lax.fori_loop(0, BAND - 1, out_dens, 0)

        def apply(r, total):
            out = list(total)
            for q in range(PLANES):
                value = layer[r, q]
                for p in range(PLANES):
                    at = 6 * r + q - p + 5
                    out[p] = out[p] + green_ref[at] * value
                    out[PLANES + p] = out[PLANES + p] + green_ref[at + 3 * outward] * value
            return tuple(out)

        def collect_layer(r, total):
            pltpu.make_async_copy(summed, layer.at[r], layer_recv.at[r]).wait()
            return apply(r, total)

        zero = jnp.zeros((8, 128), f32)
        result = lax.fori_loop(1, SPACE // 2, collect_layer, apply(0, (zero,) * (2 * PLANES)))
        for p in range(PLANES):
            partial[p] = result[PLANES + p]
        partner_copy.start()
        partner_copy.wait()
        keep([result[p] + crossed[p] for p in range(PLANES)], hart_own, hart_modes)

        def out_hart(i, carry):
            band_copy(hart_own, hart_modes, hart_send, hart_recv, by_distance(i, BAND // 2)).start()
            return carry

        lax.fori_loop(0, BAND - 1, out_hart, 0)

    def back(spec_ref):
        halves = [[spec_ref[o, i].astype(f32) for i in range(2)] for o in range(OWNERS)]
        pieces = []
        for p in range(PLANES):
            at = 8 * (p % 2)
            blocks = [halves[o][p // 2][at : at + 8] for o in range(OWNERS)]
            head = jnp.concatenate(blocks[:6], axis=0)
            rest = jnp.concatenate(blocks[6:], axis=0)
            upper = [jnp.where(lane < 64, head, 0.0), jnp.where(lane >= 64, head, 0.0)]
            lower = [jnp.where(lane // 32 == quarter, rest, 0.0) for quarter in range(4)]
            pieces += [jnp.concatenate(upper, axis=0), jnp.concatenate(lower, axis=0)]
        spread = jnp.concatenate(pieces, axis=1).astype(bf16)
        rows_y = jnp.dot(
            iy_ref[...], jnp.concatenate([spread, spread], axis=0), preferred_element_type=f32
        )
        flat = jnp.concatenate(
            [
                jnp.concatenate(
                    [
                        rows_y[r * BLOCKS : (r + 1) * BLOCKS, p * 256 : (p + 1) * 256]
                        for r in range(4)
                    ],
                    axis=1,
                )
                for p in range(PLANES)
            ],
            axis=0,
        )
        high = flat.astype(bf16)
        low = (flat - high.astype(f32)).astype(bf16)
        z_high = iz_ref[0:1024]
        return (
            jnp.dot(high, z_high, preferred_element_type=f32)
            + jnp.dot(low, z_high, preferred_element_type=f32)
            + jnp.dot(high, iz_ref[1024:2048], preferred_element_type=f32)
        )

    def put(out_ref, values):
        for p in range(PLANES):
            for block in range(BLOCKS):
                at = p * BLOCKS + block
                out_ref[p : p + 1, block * BLOCK : (block + 1) * BLOCK] = values[at : at + 1]

    def gathered(dst, recv):
        for o in range(OWNERS):
            @pl.when((BAND * o) // OWNERS != z)
            def _():
                pltpu.make_async_copy(dens_own, dst.at[o], recv.at[o]).wait()

    gathered(dens_modes, dens_recv)
    put(dens_ref, back(dens_modes))
    gathered(hart_modes, hart_recv)
    put(hart_ref, back(hart_modes))

    @pl.when(is_owner)
    def _():
        def drain_layer(k, carry):
            layer_copy(k).wait_send()
            return carry

        lax.fori_loop(1, SPACE // 2, drain_layer, 0)

        def drain_band(k, carry):
            band_copy(dens_own, dens_modes, dens_send, dens_recv, k).wait_send()
            band_copy(hart_own, hart_modes, hart_send, hart_recv, k).wait_send()
            return carry

        lax.fori_loop(1, BAND, drain_band, 0)

    for o in range(OWNERS):
        @pl.when((BAND * o) // OWNERS != z)
        def _():
            share_copy(o, z).wait_send()

    def drain(c, carry):
        for phase in range(2):
            for kind in range(4):
                halo(phase, kind, c).wait_send()
        for half in range(2):
            for part in range(2):
                stores(c, half, part).wait()
        return carry

    lax.fori_loop(0, CHUNKS, drain, 0)


def settle(prop_in, dens_in, hart_in, prop_out, dens_out, hart_out, prop_at, dens_at, hart_at, in_sem, out_sem):
    routes = [(dens_in, dens_at, dens_out), (hart_in, hart_at, hart_out)]
    for part in range(2):
        for p in range(PLANES):
            routes.append((prop_in.at[part, p], prop_at.at[part, p], prop_out.at[part, p]))
    inward = [pltpu.make_async_copy(r[0], r[1], in_sem.at[i]) for i, r in enumerate(routes)]
    outward = [pltpu.make_async_copy(r[1], r[2], out_sem.at[i]) for i, r in enumerate(routes)]
    for copy in inward:
        copy.start()
    for i in range(len(routes)):
        inward[i].wait()
        outward[i].start()
    for copy in outward:
        copy.wait()


def per_device(orbitals, potential, occupations):
    f32 = jnp.float32
    bf16 = jnp.bfloat16
    forward_z, forward_y, inverse_y, inverse_z, green = transform_tables()
    vmem = pltpu.VMEM
    dma = pltpu.SemaphoreType.DMA
    anywhere = pl.BlockSpec(memory_space=pl.ANY)
    whole = pl.BlockSpec(memory_space=pltpu.VMEM)
    in_hbm = pl.BlockSpec(memory_space=pltpu.HBM)
    raw = pl.pallas_call(
        body,
        out_shape=(
            jax.ShapeDtypeStruct((2, PLANES, 4, CELLS), f32),
            jax.ShapeDtypeStruct((PLANES, CELLS), f32),
            jax.ShapeDtypeStruct((PLANES, CELLS), f32),
        ),
        in_specs=[in_hbm, in_hbm, pl.BlockSpec(memory_space=pltpu.SMEM)] + [in_hbm] * 6,
        out_specs=(anywhere, whole, whole),
        scratch_shapes=[
            vmem((PLANES, CELLS), f32),
            vmem((PLANES, FIELDS, CELLS), f32),
            vmem((PLANES, FIELDS, CELLS), f32),
            vmem((PLANES, FIELDS, CELLS), f32),
            vmem((PLANES, 16, PADDED), bf16),
            vmem((PLANES, 16, PADDED), bf16),
            vmem((2, 4, 16, FOLD), bf16),
            vmem((2, 4, 16, FOLD), bf16),
            vmem((PLANES * BLOCKS, BLOCK), f32),
            vmem((WINDOW, BLOCK), bf16),
            vmem((BLOCK, 1024), f32),
            vmem((NY, NY), f32),
            vmem((NY, 2 * NY), bf16),
            vmem((2048, BLOCK), bf16),
            vmem((NX + 5, 8, 128), f32),
            vmem((OWNERS, PLANES, 8, 128), f32),
            vmem((BAND, PLANES, 8, 128), f32),
            vmem((PLANES, 8, 128), f32),
            vmem((SPACE // 2, PLANES, 8, 128), f32),
            vmem((PLANES, 8, 128), f32),
            vmem((PLANES, 8, 128), f32),
            vmem((2, 16, 128), bf16),
            vmem((2, 16, 128), bf16),
            vmem((OWNERS, 2, 16, 128), bf16),
            vmem((OWNERS, 2, 16, 128), bf16),
            dma((CHUNKS, 2, 2)),
            dma((7,)),
            dma((CHUNKS, 2, 2)),
            dma((2, 4, CHUNKS)),
            dma((2, 4, CHUNKS)),
            pltpu.SemaphoreType.REGULAR((5,)),
            dma((OWNERS,)),
            dma((BAND,)),
            dma((SPACE // 2,)),
            dma((SPACE // 2,)),
            dma((2,)),
            dma((BAND,)),
            dma((OWNERS,)),
            dma((BAND,)),
            dma((OWNERS,)),
        ],
        compiler_params=pltpu.CompilerParams(
            collective_id=0, has_side_effects=True, vmem_limit_bytes=62 * 2**20
        ),
    )(
        jnp.transpose(orbitals, (0, 2, 1, 3)),
        potential,
        occupations,
        jnp.asarray(band_matrix()),
        jnp.asarray(forward_z),
        jnp.asarray(forward_y),
        jnp.asarray(inverse_y),
        jnp.asarray(inverse_z),
        jnp.asarray(green),
    )
    prop, dens, hart = pl.pallas_call(
        settle,
        out_shape=[jax.ShapeDtypeStruct(r.shape, r.dtype) for r in raw],
        in_specs=[anywhere] * 3,
        out_specs=[anywhere] * 3,
        scratch_shapes=[vmem(r.shape, r.dtype) for r in raw] + [dma((8,)), dma((8,))],
        compiler_params=pltpu.CompilerParams(vmem_limit_bytes=62 * 2**20),
    )(*raw)
    return jnp.transpose(prop, (0, 2, 1, 3)), dens, hart


def solution(mesh):
    in_specs = (P(None, "band", "space", None), P("space", None), P("band"))
    out_specs = (P(None, "band", "space", None), P("space", None), P("space", None))
    return jax.shard_map(
        per_device, mesh=mesh, in_specs=in_specs, out_specs=out_specs, check_vma=False
    )
```

```python
import functools
import math

import jax
import jax.numpy as jnp
import ml_dtypes
import numpy as np
from jax import lax
from jax.experimental import pallas as pl
from jax.experimental.pallas import tpu as pltpu
from jax.sharding import PartitionSpec as P

NX = 96
NY = 96
NZ = 96

stencil_coeffs = (-205.0 / 72.0, 8.0 / 5.0, -1.0 / 5.0, 8.0 / 315.0, -1.0 / 560.0)
energy_shift = 6.0
energy_scale = 8.0
bessel_terms = (0.7651976865579666, 0.44005058574493355, 0.11490348493190049)
scaled_coeffs = tuple(c / stencil_coeffs[1] for c in stencil_coeffs)

MESH = pl.DeviceIdType.MESH
PLANES = 3
FIELDS = 8
CELLS = NY * NZ
FOLD = CELLS // 2
BLOCK = 4 * NZ
BLOCKS = CELLS // BLOCK
CHUNKS = 4
CHUNK = FOLD // CHUNKS
PER_CHUNK = CHUNK // BLOCK
WINDOW = 3 * BLOCK
PADDED = FOLD + 2 * BLOCK
SPACE = 32
BAND = 16
OWNERS = 9
ORBITALS = 64


def band_matrix():
    table = np.zeros((WINDOW, BLOCK))
    for cell in range(BLOCK):
        z = cell % NZ
        for offset in range(1, 5):
            c = scaled_coeffs[offset]
            table[BLOCK + cell + offset * NZ, cell] += c
            table[BLOCK + cell - offset * NZ, cell] += c
            if z + offset < NZ:
                table[BLOCK + cell + offset, cell] += c
            if z - offset >= 0:
                table[BLOCK + cell - offset, cell] += c
    return table.astype(ml_dtypes.bfloat16)


def real_basis(length):
    cells = np.arange(length)
    rows = [np.full(length, 1.0 / math.sqrt(length))]
    waves = [0]
    for k in range(1, length // 2):
        phase = 2.0 * math.pi * ((k * cells) % length) / length
        rows.append(math.sqrt(2.0 / length) * np.cos(phase))
        rows.append(math.sqrt(2.0 / length) * np.sin(phase))
        waves += [k, k]
    rows.append(np.where(cells % 2 == 0, 1.0, -1.0) / math.sqrt(length))
    waves.append(length // 2)
    return np.stack(rows), (2.0 * math.pi / length * np.array(waves)) ** 2


def split(table):
    high = table.astype(ml_dtypes.bfloat16)
    low = (table - high.astype(np.float64)).astype(ml_dtypes.bfloat16)
    return high, low


def transform_tables():
    basis, squares = real_basis(NY)
    order = np.array([4 * block + r for r in range(4) for block in range(BLOCKS)])
    forward_y = basis[:, order]
    lanes = np.arange(128)
    spread = np.stack([basis[lanes % 64], basis[64 + lanes % 32]])
    forward_z = np.zeros((4, NZ, 4, 2, 128))
    for r in range(4):
        forward_z[r, :, r] = np.transpose(spread, (2, 0, 1))
    forward_z = forward_z.reshape(BLOCK, 1024)
    row = np.arange(72)[:, None]
    mode_y = np.where(row < 48, row + 48 * (lanes >= 64), row - 48 + 24 * (lanes // 32))
    mode_z = np.where(row < 48, lanes % 64, 64 + lanes % 32)
    across = squares[mode_y] + squares[mode_z]
    cells = np.arange(NX)
    signed = np.where(cells < NX // 2, cells, cells - NX)
    along = (2.0 * math.pi / NX * signed) ** 2
    total = along[:, None, None] + across
    kernel = np.where(total > 0, 4.0 * math.pi / np.where(total > 0, total, 1.0), 0.0)
    green = np.real(np.fft.ifft(kernel, axis=0))
    green = green[(np.arange(NX + 5) - 5) % NX]
    green = green.reshape(NX + 5, OWNERS, 8, 128).transpose(1, 0, 2, 3)
    f32 = np.float32
    y_high, y_low = split(forward_y.T)
    z_high, z_low = split(forward_z.T)
    return (
        forward_z.astype(f32),
        forward_y.astype(f32),
        np.concatenate([y_high, y_low], axis=1),
        np.concatenate([z_high, z_low], axis=0),
        green.astype(f32),
    )


def exact_dot(a, b):
    return lax.dot_general(
        a,
        b,
        (((1,), (0,)), ((), ())),
        precision=lax.Precision.HIGHEST,
        preferred_element_type=jnp.float32,
    )


def body(
    orb_hbm, pot_hbm, occ_hbm, band_hbm, fz_hbm, fy_hbm, iy_hbm, iz_hbm, green_hbm,
    prop_hbm, dens_hbm, hart_hbm,
    pot_ref, occ_ref, dens_ref, hart_ref, field, first, prop, own0, own1, rim0, rim1, lines,
    band_ref, fz_ref, fy_ref, iy_ref, iz_ref, green_ref,
    modes, shares, summed, layer, partial, crossed, dens_own, hart_own, dens_modes, hart_modes,
    load_sem, table_sem, store_sem, halo_send, halo_recv, hand,
    share_send, share_recv, layer_send, layer_recv, cross_sem,
    dens_send, dens_recv, hart_send, hart_recv,
):
    s = lax.axis_index("space")
    z = lax.axis_index("band")
    core = lax.rem(s, 2)
    f32 = jnp.float32
    bf16 = jnp.bfloat16

    def lanes_of(c, extra=0, size=CHUNK):
        return pl.ds(pl.multiple_of(c * CHUNK + extra, 128), size)

    def load(c, half, part):
        lanes = lanes_of(c, half * FOLD)
        return pltpu.make_async_copy(
            orb_hbm.at[part, :, :, lanes],
            field.at[:, pl.ds(4 * part, 4), lanes],
            load_sem.at[c, half, part],
        )

    barrier = pltpu.get_barrier_semaphore()

    def greet(sem, axis, me, size, offset):
        for step in (offset, size - offset):
            pl.semaphore_signal(
                sem, inc=1, device_id={axis: lax.rem(me + step, size)}, device_id_type=MESH
            )

    for offset in (1, 2):
        greet(barrier, "space", s, SPACE, offset)
        greet(barrier, "band", z, BAND, offset)
    for c in range(CHUNKS):
        for half in range(2):
            for part in range(2):
                load(c, half, part).start()
    owner = (OWNERS * z + BAND - 1) // BAND
    owner_index = jnp.minimum(owner, OWNERS - 1)
    is_owner = (BAND * owner) // OWNERS == z
    pot_copy = pltpu.make_async_copy(pot_hbm, pot_ref, table_sem.at[6])
    pot_copy.start()
    occ_copy = pltpu.make_async_copy(occ_hbm, occ_ref, table_sem.at[7])
    occ_copy.start()
    tables = [
        pltpu.make_async_copy(src, dst, table_sem.at[i])
        for i, (src, dst) in enumerate(
            [
                (band_hbm, band_ref),
                (fz_hbm, fz_ref),
                (fy_hbm, fy_ref),
                (iy_hbm, iy_ref),
                (iz_hbm, iz_ref),
                (green_hbm.at[owner_index], green_ref),
            ]
        )
    ]
    tables[0].start()

    outward = 2 * core - 1
    owns = (own0, own1)
    rims = (rim0, rim1)

    def halo(phase, kind, c):
        own, rim = owns[phase], rims[phase]
        inside = lanes_of(c, BLOCK)
        outside = lanes_of(c)
        if kind == 0:
            src = own.at[:, :, inside]
            dst = rim.at[1 - core, pl.ds(core, 3), :, outside]
            step = outward
        elif kind == 1:
            src = own.at[:, :, inside]
            dst = rim.at[core, pl.ds(1 - core, 3), :, outside]
            step = -outward
        elif kind == 2:
            src = own.at[2 * (1 - core), :, inside]
            dst = rim.at[core, 3 * core, :, outside]
            step = -2 * outward
        else:
            src = rim.at[core, 3 * (1 - core), :, outside]
            dst = rim.at[core, 3 * core, :, outside]
            step = -outward
        return pltpu.make_async_remote_copy(
            src_ref=src,
            dst_ref=dst,
            send_sem=halo_send.at[phase, kind, c],
            recv_sem=halo_recv.at[phase, kind, c],
            device_id={"space": lax.rem(s + step + SPACE, SPACE)},
            device_id_type=MESH,
        )

    def fold_edges(source, own):
        zeros = jnp.zeros((FIELDS, BLOCK), f32)
        for p in range(PLANES):
            own[p, :, 0:BLOCK] = jnp.concatenate(
                [zeros, source[p, :, FOLD - BLOCK : FOLD]], axis=0
            ).astype(bf16)
            own[p, :, PADDED - BLOCK : PADDED] = jnp.concatenate(
                [source[p, :, FOLD : FOLD + BLOCK], zeros], axis=0
            ).astype(bf16)

    def pack(c, carry):
        for half in range(2):
            for part in range(2):
                load(c, half, part).wait()
        for p in range(PLANES):
            own0[p, :, lanes_of(c, BLOCK)] = jnp.concatenate(
                [field[p, :, lanes_of(c)], field[p, :, lanes_of(c, FOLD)]], axis=0
            ).astype(bf16)
        return carry

    lax.fori_loop(0, CHUNKS, pack, 0)
    pl.semaphore_wait(barrier, 8)

    def ship(c, carry):
        for kind in range(3):
            halo(0, kind, c).start()
        return carry

    lax.fori_loop(0, CHUNKS, ship, 0)
    greet(hand.at[0], "band", z, BAND, 2)
    greet(hand.at[1], "space", s, SPACE, 2)
    fold_edges(field, own0)
    for copy in tables[1:]:
        copy.start()
    tables[0].wait()

    pot_copy.wait()
    occ_copy.wait()
    edge = (s - core) // 2
    before = jnp.where(edge >= 1, 1.0, 0.0).astype(f32)
    after = jnp.where(edge <= SPACE // 2 - 2, 1.0, 0.0).astype(f32)
    outer_weight = jnp.where(core == 0, before, after)
    inner_weight = jnp.where(core == 0, after, before)

    gain = stencil_coeffs[1] / (2.0 * energy_scale)
    level = -(energy_shift + 1.5 * stencil_coeffs[0]) / energy_scale

    def mirrored(position, last):
        return position + core * (last - 2 * position)

    def stencil(phase, source, c, finish):
        own, rim = owns[phase], rims[phase]
        windows = [
            own[mirrored(q, 2), :, lanes_of(c, b * BLOCK, WINDOW)]
            for q in range(PLANES)
            for b in range(PER_CHUNK)
        ]
        flat = jnp.dot(
            jnp.concatenate(windows, axis=0), band_ref[...], preferred_element_type=f32
        )
        halo(phase, 0, c).wait_recv()
        halo(phase, 3, c).start()
        for kind in (1, 2):
            halo(phase, kind, c).wait_recv()
        for targets in ((0, 1), (2,)):
            if 2 in targets:
                halo(phase, 3, c).wait_recv()
            for b in range(PER_CHUNK):
                outside = lanes_of(c, b * BLOCK, BLOCK)
                inside = lanes_of(c, (b + 1) * BLOCK, BLOCK)
                stack = {}
                for at in range(targets[0], targets[-1] + 9):
                    if at < 4:
                        plane = rim[core, mirrored(at, 3), :, outside].astype(f32) * outer_weight
                    elif at < 7:
                        plane = own[mirrored(at - 4, 2), :, inside].astype(f32)
                    else:
                        plane = rim[1 - core, mirrored(at - 7, 3), :, outside].astype(f32)
                    stack[at] = plane * inner_weight if at == 10 else plane
                for q in targets:
                    p = mirrored(q, 2)
                    across = stack[q + 5] + stack[q + 3]
                    for offset in range(2, 5):
                        across = across + scaled_coeffs[offset] * (
                            stack[q + 4 + offset] + stack[q + 4 - offset]
                        )
                    at = 16 * (q * PER_CHUNK + b)
                    across = gain * (across + flat[at : at + 16])
                    for half in range(2):
                        lanes = lanes_of(c, half * FOLD + b * BLOCK, BLOCK)
                        centre = source[p, :, lanes]
                        factor = pot_ref[pl.ds(p, 1), lanes] * (1.0 / energy_scale) + level
                        value = centre * factor - across[8 * half : 8 * half + 8]
                        finish(p, b, half, lanes, centre, value)


    def first_chunk(c, carry):
        values = []

        def finish(p, b, half, lanes, centre, value):
            first[p, :, lanes] = value
            values.append(value)
            if half == 1:
                own1[p, :, lanes_of(c, (b + 1) * BLOCK, BLOCK)] = jnp.concatenate(
                    values[-2:], axis=0
                ).astype(bf16)

        stencil(0, field, c, finish)
        for kind in range(3):
            halo(1, kind, c).start()
        return carry

    lax.fori_loop(0, CHUNKS, first_chunk, 0)
    pl.semaphore_wait(hand.at[0], 2)
    greet(hand.at[2], "band", z, BAND, 4)
    pl.semaphore_wait(hand.at[1], 2)
    greet(hand.at[3], "space", s, SPACE, 4)
    fold_edges(first, own1)

    rows = lax.broadcasted_iota(jnp.int32, (FIELDS, BLOCK), 0)
    weight = jnp.zeros((FIELDS, BLOCK), f32)
    for o in range(4):
        weight = jnp.where(lax.rem(rows, 4) == o, occ_ref[o] * (1.0 / ORBITALS), weight)
    sign = jnp.where(rows < 4, 2.0 * bessel_terms[1], -2.0 * bessel_terms[1]).astype(f32)

    def stores(c, half, part):
        lanes = lanes_of(c, half * FOLD)
        return pltpu.make_async_copy(
            prop.at[:, pl.ds(4 * part, 4), lanes],
            prop_hbm.at[part, :, :, lanes],
            store_sem.at[c, half, part],
        )

    def second_chunk(c, carry):
        def finish(p, b, half, lanes, centre, value):
            swapped = jnp.concatenate([centre[4:8], centre[0:4]], axis=0)
            result = (
                (bessel_terms[0] + 2.0 * bessel_terms[2]) * field[p, :, lanes]
                + sign * swapped
                - (4.0 * bessel_terms[2]) * value
            )
            prop[p, :, lanes] = result
            share = jnp.sum(weight * (result * result), axis=0, keepdims=True)
            lines[pl.ds(p * BLOCKS + half * (BLOCKS // 2) + c * PER_CHUNK + b, 1), :] = share

        stencil(1, first, c, finish)
        for half in range(2):
            for part in range(2):
                stores(c, half, part).start()
        return carry

    lax.fori_loop(0, CHUNKS, second_chunk, 0)
    pl.semaphore_wait(hand.at[2], 2)
    pl.semaphore_wait(hand.at[3], 2)
    greet(hand.at[4], "space", s, SPACE, 8)

    for copy in tables[1:]:
        copy.wait()
    turned = exact_dot(lines[...], fz_ref[...])
    stacked = jnp.concatenate(
        [
            jnp.concatenate(
                [
                    turned[p * BLOCKS : (p + 1) * BLOCKS, r * 256 : (r + 1) * 256]
                    for r in range(4)
                ],
                axis=0,
            )
            for p in range(PLANES)
        ],
        axis=1,
    )
    spectral = exact_dot(fy_ref[...], stacked)
    lane = lax.broadcasted_iota(jnp.int32, (1, 128), 1)
    for p in range(PLANES):
        wide = spectral[:, p * 256 : p * 256 + 128]
        tail = spectral[:, p * 256 + 128 : (p + 1) * 256]
        head = jnp.where(lane < 64, wide[0:48], wide[48:96])
        rest = tail[0:24]
        for quarter in range(1, 4):
            rest = jnp.where(lane >= 32 * quarter, tail[24 * quarter : 24 * quarter + 24], rest)
        for o in range(6):
            modes[o, p] = head[8 * o : 8 * o + 8]
        for o in range(3):
            modes[6 + o, p] = rest[8 * o : 8 * o + 8]


    def share_copy(o, source):
        return pltpu.make_async_remote_copy(
            src_ref=modes.at[o],
            dst_ref=shares.at[source],
            send_sem=share_send.at[o],
            recv_sem=share_recv.at[source],
            device_id={"band": (BAND * o) // OWNERS},
            device_id_type=MESH,
        )

    def by_distance(i, middle):
        return middle + jnp.where(lax.rem(i, 2) == 0, i // 2, -(i + 1) // 2)

    def out_share(i, carry):
        target = lax.rem(z + by_distance(i, BAND // 2), BAND)
        o = (OWNERS * target + BAND - 1) // BAND

        @pl.when((BAND * o) // OWNERS == target)
        def _():
            share_copy(o, z).start()

        return carry

    lax.fori_loop(0, BAND - 1, out_share, 0)
    pl.semaphore_wait(hand.at[4], 2)

    def layer_copy(k):
        return pltpu.make_async_remote_copy(
            src_ref=summed,
            dst_ref=layer.at[SPACE // 2 - k],
            send_sem=layer_send.at[k],
            recv_sem=layer_recv.at[SPACE // 2 - k],
            device_id={"space": lax.rem(s + 2 * k, SPACE)},
            device_id_type=MESH,
        )

    partner_copy = pltpu.make_async_remote_copy(
        src_ref=partial,
        dst_ref=crossed,
        send_sem=cross_sem.at[0],
        recv_sem=cross_sem.at[1],
        device_id={"space": s - outward},
        device_id_type=MESH,
    )

    def band_copy(src, dst, send, recv, k):
        return pltpu.make_async_remote_copy(
            src_ref=src,
            dst_ref=dst.at[owner_index],
            send_sem=send.at[k],
            recv_sem=recv.at[owner_index],
            device_id={"band": lax.rem(z + k, BAND)},
            device_id_type=MESH,
        )

    def keep(values, ref, gathered_ref):
        upper = jnp.concatenate([values[0], values[1]], axis=0).astype(bf16)
        lower = jnp.concatenate([values[2], jnp.zeros((8, 128), f32)], axis=0).astype(bf16)
        for out in (ref, gathered_ref.at[owner_index]):
            out[0] = upper
            out[1] = lower

    @pl.when(is_owner)
    def _():
        def collect(k, total):
            source = lax.rem(z + k, BAND)
            pltpu.make_async_copy(modes.at[0], shares.at[source], share_recv.at[source]).wait()
            return total + shares[source]

        total = lax.fori_loop(1, BAND, collect, modes[owner_index])
        summed[...] = total
        layer[0] = total

        def out_layer(i, carry):
            layer_copy(by_distance(i, SPACE // 4)).start()
            return carry

        lax.fori_loop(0, SPACE // 2 - 1, out_layer, 0)
        keep([total[p] for p in range(PLANES)], dens_own, dens_modes)

        def out_dens(i, carry):
            band_copy(dens_own, dens_modes, dens_send, dens_recv, by_distance(i, BAND // 2)).start()
            return carry

        lax.fori_loop(0, BAND - 1, out_dens, 0)

        def apply(r, total):
            out = list(total)
            for q in range(PLANES):
                value = layer[r, q]
                for p in range(PLANES):
                    at = 6 * r + q - p + 5
                    out[p] = out[p] + green_ref[at] * value
                    out[PLANES + p] = out[PLANES + p] + green_ref[at + 3 * outward] * value
            return tuple(out)

        def collect_layer(r, total):
            pltpu.make_async_copy(summed, layer.at[r], layer_recv.at[r]).wait()
            return apply(r, total)

        zero = jnp.zeros((8, 128), f32)
        result = lax.fori_loop(1, SPACE // 2, collect_layer, apply(0, (zero,) * (2 * PLANES)))
        for p in range(PLANES):
            partial[p] = result[PLANES + p]
        partner_copy.start()
        partner_copy.wait()
        keep([result[p] + crossed[p] for p in range(PLANES)], hart_own, hart_modes)

        def out_hart(i, carry):
            band_copy(hart_own, hart_modes, hart_send, hart_recv, by_distance(i, BAND // 2)).start()
            return carry

        lax.fori_loop(0, BAND - 1, out_hart, 0)

    def back(spec_ref):
        halves = [[spec_ref[o, i].astype(f32) for i in range(2)] for o in range(OWNERS)]
        pieces = []
        for p in range(PLANES):
            at = 8 * (p % 2)
            blocks = [halves[o][p // 2][at : at + 8] for o in range(OWNERS)]
            head = jnp.concatenate(blocks[:6], axis=0)
            rest = jnp.concatenate(blocks[6:], axis=0)
            upper = [jnp.where(lane < 64, head, 0.0), jnp.where(lane >= 64, head, 0.0)]
            lower = [jnp.where(lane // 32 == quarter, rest, 0.0) for quarter in range(4)]
            pieces += [jnp.concatenate(upper, axis=0), jnp.concatenate(lower, axis=0)]
        spread = jnp.concatenate(pieces, axis=1).astype(bf16)
        rows_y = jnp.dot(
            iy_ref[...], jnp.concatenate([spread, spread], axis=0), preferred_element_type=f32
        )
        flat = jnp.concatenate(
            [
                jnp.concatenate(
                    [
                        rows_y[r * BLOCKS : (r + 1) * BLOCKS, p * 256 : (p + 1) * 256]
                        for r in range(4)
                    ],
                    axis=1,
                )
                for p in range(PLANES)
            ],
            axis=0,
        )
        high = flat.astype(bf16)
        low = (flat - high.astype(f32)).astype(bf16)
        z_high = iz_ref[0:1024]
        return (
            jnp.dot(high, z_high, preferred_element_type=f32)
            + jnp.dot(low, z_high, preferred_element_type=f32)
            + jnp.dot(high, iz_ref[1024:2048], preferred_element_type=f32)
        )

    def put(out_ref, values):
        for p in range(PLANES):
            for block in range(BLOCKS):
                at = p * BLOCKS + block
                out_ref[p : p + 1, block * BLOCK : (block + 1) * BLOCK] = values[at : at + 1]

    def gathered(dst, recv):
        for o in range(OWNERS):
            @pl.when((BAND * o) // OWNERS != z)
            def _():
                pltpu.make_async_copy(dens_own, dst.at[o], recv.at[o]).wait()

    dens_copy = pltpu.make_async_copy(dens_ref, dens_hbm, table_sem.at[8])
    hart_copy = pltpu.make_async_copy(hart_ref, hart_hbm, table_sem.at[9])
    gathered(dens_modes, dens_recv)
    put(dens_ref, back(dens_modes))
    dens_copy.start()
    gathered(hart_modes, hart_recv)
    put(hart_ref, back(hart_modes))
    hart_copy.start()

    @pl.when(is_owner)
    def _():
        def drain_layer(k, carry):
            layer_copy(k).wait_send()
            return carry

        lax.fori_loop(1, SPACE // 2, drain_layer, 0)

        def drain_band(k, carry):
            band_copy(dens_own, dens_modes, dens_send, dens_recv, k).wait_send()
            band_copy(hart_own, hart_modes, hart_send, hart_recv, k).wait_send()
            return carry

        lax.fori_loop(1, BAND, drain_band, 0)

    for o in range(OWNERS):
        @pl.when((BAND * o) // OWNERS != z)
        def _():
            share_copy(o, z).wait_send()

    def drain(c, carry):
        for phase in range(2):
            for kind in range(4):
                halo(phase, kind, c).wait_send()
        for half in range(2):
            for part in range(2):
                stores(c, half, part).wait()
        return carry

    lax.fori_loop(0, CHUNKS, drain, 0)
    dens_copy.wait()
    hart_copy.wait()


def settle(prop_in, dens_in, hart_in, prop_out, dens_out, hart_out, prop_at, dens_at, hart_at, in_sem, out_sem):
    routes = [(dens_in, dens_at, dens_out), (hart_in, hart_at, hart_out)]
    for part in range(2):
        for p in range(PLANES):
            routes.append((prop_in.at[part, p], prop_at.at[part, p], prop_out.at[part, p]))
    inward = [pltpu.make_async_copy(r[0], r[1], in_sem.at[i]) for i, r in enumerate(routes)]
    outward = [pltpu.make_async_copy(r[1], r[2], out_sem.at[i]) for i, r in enumerate(routes)]
    for copy in inward:
        copy.start()
    for i in range(len(routes)):
        inward[i].wait()
        outward[i].start()
    for copy in outward:
        copy.wait()


def per_device(orbitals, potential, occupations):
    f32 = jnp.float32
    bf16 = jnp.bfloat16
    forward_z, forward_y, inverse_y, inverse_z, green = transform_tables()
    vmem = pltpu.VMEM
    dma = pltpu.SemaphoreType.DMA
    anywhere = pl.BlockSpec(memory_space=pl.ANY)
    raw = pl.pallas_call(
        body,
        out_shape=(
            jax.ShapeDtypeStruct((2, PLANES, 4, CELLS), f32),
            jax.ShapeDtypeStruct((PLANES, CELLS), f32),
            jax.ShapeDtypeStruct((PLANES, CELLS), f32),
        ),
        in_specs=[anywhere] * 9,
        out_specs=(anywhere, anywhere, anywhere),
        scratch_shapes=[
            vmem((PLANES, CELLS), f32),
            pltpu.SMEM((4,), f32),
            vmem((PLANES, CELLS), f32),
            vmem((PLANES, CELLS), f32),
            vmem((PLANES, FIELDS, CELLS), f32),
            vmem((PLANES, FIELDS, CELLS), f32),
            vmem((PLANES, FIELDS, CELLS), f32),
            vmem((PLANES, 16, PADDED), bf16),
            vmem((PLANES, 16, PADDED), bf16),
            vmem((2, 4, 16, FOLD), bf16),
            vmem((2, 4, 16, FOLD), bf16),
            vmem((PLANES * BLOCKS, BLOCK), f32),
            vmem((WINDOW, BLOCK), bf16),
            vmem((BLOCK, 1024), f32),
            vmem((NY, NY), f32),
            vmem((NY, 2 * NY), bf16),
            vmem((2048, BLOCK), bf16),
            vmem((NX + 5, 8, 128), f32),
            vmem((OWNERS, PLANES, 8, 128), f32),
            vmem((BAND, PLANES, 8, 128), f32),
            vmem((PLANES, 8, 128), f32),
            vmem((SPACE // 2, PLANES, 8, 128), f32),
            vmem((PLANES, 8, 128), f32),
            vmem((PLANES, 8, 128), f32),
            vmem((2, 16, 128), bf16),
            vmem((2, 16, 128), bf16),
            vmem((OWNERS, 2, 16, 128), bf16),
            vmem((OWNERS, 2, 16, 128), bf16),
            dma((CHUNKS, 2, 2)),
            dma((10,)),
            dma((CHUNKS, 2, 2)),
            dma((2, 4, CHUNKS)),
            dma((2, 4, CHUNKS)),
            pltpu.SemaphoreType.REGULAR((5,)),
            dma((OWNERS,)),
            dma((BAND,)),
            dma((SPACE // 2,)),
            dma((SPACE // 2,)),
            dma((2,)),
            dma((BAND,)),
            dma((OWNERS,)),
            dma((BAND,)),
            dma((OWNERS,)),
        ],
        compiler_params=pltpu.CompilerParams(
            collective_id=0, has_side_effects=True, vmem_limit_bytes=62 * 2**20
        ),
    )(
        jnp.transpose(orbitals, (0, 2, 1, 3)),
        potential,
        occupations,
        jnp.asarray(band_matrix()),
        jnp.asarray(forward_z),
        jnp.asarray(forward_y),
        jnp.asarray(inverse_y),
        jnp.asarray(inverse_z),
        jnp.asarray(green),
    )
    prop, dens, hart = pl.pallas_call(
        settle,
        out_shape=[jax.ShapeDtypeStruct(r.shape, r.dtype) for r in raw],
        in_specs=[anywhere] * 3,
        out_specs=[anywhere] * 3,
        scratch_shapes=[vmem(r.shape, r.dtype) for r in raw] + [dma((8,)), dma((8,))],
        compiler_params=pltpu.CompilerParams(vmem_limit_bytes=62 * 2**20),
    )(*raw)
    return jnp.transpose(prop, (0, 2, 1, 3)), dens, hart


def solution(mesh):
    in_specs = (P(None, "band", "space", None), P("space", None), P("band"))
    out_specs = (P(None, "band", "space", None), P("space", None), P("space", None))
    return jax.shard_map(
        per_device, mesh=mesh, in_specs=in_specs, out_specs=out_specs, check_vma=False
    )
```

```python
import functools
import math

import jax
import jax.numpy as jnp
import ml_dtypes
import numpy as np
from jax import lax
from jax.experimental import pallas as pl
from jax.experimental.pallas import tpu as pltpu
from jax.sharding import PartitionSpec as P

NX = 96
NY = 96
NZ = 96

stencil_coeffs = (-205.0 / 72.0, 8.0 / 5.0, -1.0 / 5.0, 8.0 / 315.0, -1.0 / 560.0)
energy_shift = 6.0
energy_scale = 8.0
bessel_terms = (0.7651976865579666, 0.44005058574493355, 0.11490348493190049)
scaled_coeffs = tuple(c / stencil_coeffs[1] for c in stencil_coeffs)

MESH = pl.DeviceIdType.MESH
PLANES = 3
FIELDS = 8
CELLS = NY * NZ
FOLD = CELLS // 2
BLOCK = 4 * NZ
BLOCKS = CELLS // BLOCK
CHUNKS = 4
CHUNK = FOLD // CHUNKS
PER_CHUNK = CHUNK // BLOCK
WINDOW = 3 * BLOCK
PADDED = FOLD + 2 * BLOCK
SPACE = 32
BAND = 16
OWNERS = 9
ORBITALS = 64


def band_matrix():
    table = np.zeros((WINDOW, BLOCK))
    for cell in range(BLOCK):
        z = cell % NZ
        for offset in range(1, 5):
            c = scaled_coeffs[offset]
            table[BLOCK + cell + offset * NZ, cell] += c
            table[BLOCK + cell - offset * NZ, cell] += c
            if z + offset < NZ:
                table[BLOCK + cell + offset, cell] += c
            if z - offset >= 0:
                table[BLOCK + cell - offset, cell] += c
    return table.astype(ml_dtypes.bfloat16)


def real_basis(length):
    cells = np.arange(length)
    rows = [np.full(length, 1.0 / math.sqrt(length))]
    waves = [0]
    for k in range(1, length // 2):
        phase = 2.0 * math.pi * ((k * cells) % length) / length
        rows.append(math.sqrt(2.0 / length) * np.cos(phase))
        rows.append(math.sqrt(2.0 / length) * np.sin(phase))
        waves += [k, k]
    rows.append(np.where(cells % 2 == 0, 1.0, -1.0) / math.sqrt(length))
    waves.append(length // 2)
    return np.stack(rows), (2.0 * math.pi / length * np.array(waves)) ** 2


def split(table):
    high = table.astype(ml_dtypes.bfloat16)
    low = (table - high.astype(np.float64)).astype(ml_dtypes.bfloat16)
    return high, low


def transform_tables():
    basis, squares = real_basis(NY)
    order = np.array([4 * block + r for r in range(4) for block in range(BLOCKS)])
    forward_y = basis[:, order]
    lanes = np.arange(128)
    spread = np.stack([basis[lanes % 64], basis[64 + lanes % 32]])
    forward_z = np.zeros((4, NZ, 4, 2, 128))
    for r in range(4):
        forward_z[r, :, r] = np.transpose(spread, (2, 0, 1))
    forward_z = forward_z.reshape(BLOCK, 1024)
    row = np.arange(72)[:, None]
    mode_y = np.where(row < 48, row + 48 * (lanes >= 64), row - 48 + 24 * (lanes // 32))
    mode_z = np.where(row < 48, lanes % 64, 64 + lanes % 32)
    across = squares[mode_y] + squares[mode_z]
    cells = np.arange(NX)
    signed = np.where(cells < NX // 2, cells, cells - NX)
    along = (2.0 * math.pi / NX * signed) ** 2
    total = along[:, None, None] + across
    kernel = np.where(total > 0, 4.0 * math.pi / np.where(total > 0, total, 1.0), 0.0)
    green = np.real(np.fft.ifft(kernel, axis=0))
    green = green[(np.arange(NX + 5) - 5) % NX]
    green = green.reshape(NX + 5, OWNERS, 8, 128).transpose(1, 0, 2, 3)
    f32 = np.float32
    y_high, y_low = split(forward_y.T)
    z_high, z_low = split(forward_z.T)
    return (
        np.concatenate([forward_z, np.pad(forward_y, ((0, 0), (0, 1024 - NY)))]).astype(f32),
        np.concatenate([z_high, z_low, np.pad(np.concatenate([y_high, y_low], axis=1), ((0, 0), (0, BLOCK - 2 * NY)))]),
        green.astype(f32),
    )


def exact_dot(a, b):
    return lax.dot_general(
        a,
        b,
        (((1,), (0,)), ((), ())),
        precision=lax.Precision.HIGHEST,
        preferred_element_type=jnp.float32,
    )


def body(
    orb_hbm, pot_hbm, occ_hbm, band_hbm, forward_hbm, inverse_hbm, green_hbm,
    prop_hbm, dens_hbm, hart_hbm,
    pot_ref, occ_ref, dens_ref, hart_ref, flat, field, first, prop, own0, own1, rim0, rim1, lines,
    band_ref, forward_ref, inverse_ref, green_ref,
    modes, shares, summed, layer, partial, crossed, dens_own, hart_own, dens_modes, hart_modes,
    load_sem, table_sem, store_sem, halo_send, halo_recv, hand,
    share_send, share_recv, layer_send, layer_recv, cross_sem,
    dens_send, dens_recv, hart_send, hart_recv,
):
    s = lax.axis_index("space")
    z = lax.axis_index("band")
    core = lax.rem(s, 2)
    f32 = jnp.float32
    bf16 = jnp.bfloat16

    def lanes_of(c, extra=0, size=CHUNK):
        return pl.ds(pl.multiple_of(c * CHUNK + extra, 128), size)

    def load(c, half, part):
        lanes = lanes_of(c, half * FOLD)
        return pltpu.make_async_copy(
            orb_hbm.at[part, :, :, lanes],
            field.at[:, pl.ds(4 * part, 4), lanes],
            load_sem.at[c, half, part],
        )

    barrier = pltpu.get_barrier_semaphore()

    def greet(sem, axis, me, size, offset):
        for step in (offset, size - offset):
            pl.semaphore_signal(
                sem, inc=1, device_id={axis: lax.rem(me + step, size)}, device_id_type=MESH
            )

    for offset in (1, 2):
        greet(barrier, "space", s, SPACE, offset)
        greet(barrier, "band", z, BAND, offset)
    for c in range(CHUNKS):
        for half in range(2):
            for part in range(2):
                load(c, half, part).start()
    owner = (OWNERS * z + BAND - 1) // BAND
    owner_index = jnp.minimum(owner, OWNERS - 1)
    is_owner = (BAND * owner) // OWNERS == z
    pot_copy = pltpu.make_async_copy(pot_hbm, pot_ref, table_sem.at[4])
    pot_copy.start()
    occ_copy = pltpu.make_async_copy(occ_hbm, occ_ref, table_sem.at[5])
    occ_copy.start()
    tables = [
        pltpu.make_async_copy(src, dst, table_sem.at[i])
        for i, (src, dst) in enumerate(
            [
                (band_hbm, band_ref),
                (forward_hbm, forward_ref),
                (inverse_hbm, inverse_ref),
                (green_hbm.at[owner_index], green_ref),
            ]
        )
    ]
    tables[0].start()

    outward = 2 * core - 1
    owns = (own0, own1)
    rims = (rim0, rim1)

    def halo(phase, kind, c):
        own, rim = owns[phase], rims[phase]
        inside = lanes_of(c, BLOCK)
        outside = lanes_of(c)
        if kind == 0:
            src = own.at[:, :, inside]
            dst = rim.at[1 - core, pl.ds(core, 3), :, outside]
            step = outward
        elif kind == 1:
            src = own.at[:, :, inside]
            dst = rim.at[core, pl.ds(1 - core, 3), :, outside]
            step = -outward
        elif kind == 2:
            src = own.at[2 * (1 - core), :, inside]
            dst = rim.at[core, 3 * core, :, outside]
            step = -2 * outward
        else:
            src = rim.at[core, 3 * (1 - core), :, outside]
            dst = rim.at[core, 3 * core, :, outside]
            step = -outward
        return pltpu.make_async_remote_copy(
            src_ref=src,
            dst_ref=dst,
            send_sem=halo_send.at[phase, kind, c],
            recv_sem=halo_recv.at[phase, kind, c],
            device_id={"space": lax.rem(s + step + SPACE, SPACE)},
            device_id_type=MESH,
        )

    def fold_edges(source, own):
        zeros = jnp.zeros((FIELDS, BLOCK), f32)
        for p in range(PLANES):
            own[p, :, 0:BLOCK] = jnp.concatenate(
                [zeros, source[p, :, FOLD - BLOCK : FOLD]], axis=0
            ).astype(bf16)
            own[p, :, PADDED - BLOCK : PADDED] = jnp.concatenate(
                [source[p, :, FOLD : FOLD + BLOCK], zeros], axis=0
            ).astype(bf16)

    def pack(c, carry):
        for half in range(2):
            for part in range(2):
                load(c, half, part).wait()
        for p in range(PLANES):
            own0[p, :, lanes_of(c, BLOCK)] = jnp.concatenate(
                [field[p, :, lanes_of(c)], field[p, :, lanes_of(c, FOLD)]], axis=0
            ).astype(bf16)
        return carry

    lax.fori_loop(0, CHUNKS, pack, 0)
    pl.semaphore_wait(barrier, 8)

    def ship(c, carry):
        for kind in range(3):
            halo(0, kind, c).start()
        return carry

    lax.fori_loop(0, CHUNKS, ship, 0)
    greet(hand.at[0], "band", z, BAND, 2)
    greet(hand.at[1], "space", s, SPACE, 2)
    fold_edges(field, own0)
    for copy in tables[1:]:
        copy.start()
    tables[0].wait()

    pot_copy.wait()
    occ_copy.wait()
    edge = (s - core) // 2
    before = jnp.where(edge >= 1, 1.0, 0.0).astype(f32)
    after = jnp.where(edge <= SPACE // 2 - 2, 1.0, 0.0).astype(f32)
    outer_weight = jnp.where(core == 0, before, after)
    inner_weight = jnp.where(core == 0, after, before)

    gain = stencil_coeffs[1] / (2.0 * energy_scale)
    level = -(energy_shift + 1.5 * stencil_coeffs[0]) / energy_scale

    def mirrored(position, last):
        return position + core * (last - 2 * position)

    def receive(phase, c):
        own = owns[phase]
        windows = [
            own[mirrored(q, 2), :, lanes_of(c, b * BLOCK, WINDOW)]
            for q in range(PLANES)
            for b in range(PER_CHUNK)
        ]
        flat[lax.rem(c, 2)] = jnp.dot(
            jnp.concatenate(windows, axis=0), band_ref[...], preferred_element_type=f32
        )
        halo(phase, 0, c).wait_recv()
        halo(phase, 3, c).start()

    def stencil(phase, source, c, finish):
        own, rim = owns[phase], rims[phase]
        slot = lax.rem(c, 2)
        for kind in (1, 2, 3):
            halo(phase, kind, c).wait_recv()
        for b in range(PER_CHUNK):
            outside = lanes_of(c, b * BLOCK, BLOCK)
            inside = lanes_of(c, (b + 1) * BLOCK, BLOCK)
            outer = [
                rim[core, mirrored(at, 3), :, outside].astype(f32) * outer_weight
                for at in range(4)
            ]
            middle = [own[mirrored(at, 2), :, inside].astype(f32) for at in range(PLANES)]
            inner = [rim[1 - core, mirrored(at, 3), :, outside].astype(f32) for at in range(4)]
            stack = outer + middle + inner[:3] + [inner[3] * inner_weight]
            for q in range(PLANES):
                p = mirrored(q, 2)
                across = stack[q + 5] + stack[q + 3]
                for offset in range(2, 5):
                    across = across + scaled_coeffs[offset] * (
                        stack[q + 4 + offset] + stack[q + 4 - offset]
                    )
                at = 16 * (q * PER_CHUNK + b)
                across = gain * (across + flat[slot, at : at + 16])
                for half in range(2):
                    lanes = lanes_of(c, half * FOLD + b * BLOCK, BLOCK)
                    centre = source[p, :, lanes]
                    factor = pot_ref[pl.ds(p, 1), lanes] * (1.0 / energy_scale) + level
                    value = centre * factor - across[8 * half : 8 * half + 8]
                    finish(p, b, half, lanes, centre, value)

    def sweep(phase, use):
        receive(phase, 0)

        def step(c, carry):
            @pl.when(c < CHUNKS)
            def _():
                receive(phase, c)

            use(c - 1)
            return carry

        lax.fori_loop(1, CHUNKS + 1, step, 0)


    def first_chunk(c):
        values = []

        def finish(p, b, half, lanes, centre, value):
            first[p, :, lanes] = value
            values.append(value)
            if half == 1:
                own1[p, :, lanes_of(c, (b + 1) * BLOCK, BLOCK)] = jnp.concatenate(
                    values[-2:], axis=0
                ).astype(bf16)

        stencil(0, field, c, finish)
        for kind in range(3):
            halo(1, kind, c).start()

    sweep(0, first_chunk)
    pl.semaphore_wait(hand.at[0], 2)
    greet(hand.at[2], "band", z, BAND, 4)
    pl.semaphore_wait(hand.at[1], 2)
    greet(hand.at[3], "space", s, SPACE, 4)
    fold_edges(first, own1)

    rows = lax.broadcasted_iota(jnp.int32, (FIELDS, BLOCK), 0)
    weight = jnp.zeros((FIELDS, BLOCK), f32)
    for o in range(4):
        weight = jnp.where(lax.rem(rows, 4) == o, occ_ref[o] * (1.0 / ORBITALS), weight)
    sign = jnp.where(rows < 4, 2.0 * bessel_terms[1], -2.0 * bessel_terms[1]).astype(f32)

    def stores(c, half, part):
        lanes = lanes_of(c, half * FOLD)
        return pltpu.make_async_copy(
            prop.at[:, pl.ds(4 * part, 4), lanes],
            prop_hbm.at[part, :, :, lanes],
            store_sem.at[c, half, part],
        )

    def second_chunk(c):
        def finish(p, b, half, lanes, centre, value):
            swapped = jnp.concatenate([centre[4:8], centre[0:4]], axis=0)
            result = (
                (bessel_terms[0] + 2.0 * bessel_terms[2]) * field[p, :, lanes]
                + sign * swapped
                - (4.0 * bessel_terms[2]) * value
            )
            prop[p, :, lanes] = result
            share = jnp.sum(weight * (result * result), axis=0, keepdims=True)
            lines[pl.ds(p * BLOCKS + half * (BLOCKS // 2) + c * PER_CHUNK + b, 1), :] = share

        stencil(1, first, c, finish)
        for half in range(2):
            for part in range(2):
                stores(c, half, part).start()

    sweep(1, second_chunk)
    pl.semaphore_wait(hand.at[2], 2)
    pl.semaphore_wait(hand.at[3], 2)
    greet(hand.at[4], "space", s, SPACE, 8)

    for copy in tables[1:]:
        copy.wait()
    turned = exact_dot(lines[...], forward_ref[0:BLOCK, :])
    stacked = jnp.concatenate(
        [
            jnp.concatenate(
                [
                    turned[p * BLOCKS : (p + 1) * BLOCKS, r * 256 : (r + 1) * 256]
                    for r in range(4)
                ],
                axis=0,
            )
            for p in range(PLANES)
        ],
        axis=1,
    )
    spectral = exact_dot(forward_ref[BLOCK : BLOCK + NY, 0:NY], stacked)
    lane = lax.broadcasted_iota(jnp.int32, (1, 128), 1)
    for p in range(PLANES):
        wide = spectral[:, p * 256 : p * 256 + 128]
        tail = spectral[:, p * 256 + 128 : (p + 1) * 256]
        head = jnp.where(lane < 64, wide[0:48], wide[48:96])
        rest = tail[0:24]
        for quarter in range(1, 4):
            rest = jnp.where(lane >= 32 * quarter, tail[24 * quarter : 24 * quarter + 24], rest)
        for o in range(6):
            modes[o, p] = head[8 * o : 8 * o + 8]
        for o in range(3):
            modes[6 + o, p] = rest[8 * o : 8 * o + 8]


    def share_copy(o, source):
        return pltpu.make_async_remote_copy(
            src_ref=modes.at[o],
            dst_ref=shares.at[source],
            send_sem=share_send.at[o],
            recv_sem=share_recv.at[source],
            device_id={"band": (BAND * o) // OWNERS},
            device_id_type=MESH,
        )

    def by_distance(i, middle):
        return middle + jnp.where(lax.rem(i, 2) == 0, i // 2, -(i + 1) // 2)

    def out_share(i, carry):
        target = lax.rem(z + by_distance(i, BAND // 2), BAND)
        o = (OWNERS * target + BAND - 1) // BAND

        @pl.when((BAND * o) // OWNERS == target)
        def _():
            share_copy(o, z).start()

        return carry

    lax.fori_loop(0, BAND - 1, out_share, 0)
    pl.semaphore_wait(hand.at[4], 2)

    def layer_copy(k):
        return pltpu.make_async_remote_copy(
            src_ref=summed,
            dst_ref=layer.at[SPACE // 2 - k],
            send_sem=layer_send.at[k],
            recv_sem=layer_recv.at[SPACE // 2 - k],
            device_id={"space": lax.rem(s + 2 * k, SPACE)},
            device_id_type=MESH,
        )

    partner_copy = pltpu.make_async_remote_copy(
        src_ref=partial,
        dst_ref=crossed,
        send_sem=cross_sem.at[0],
        recv_sem=cross_sem.at[1],
        device_id={"space": s - outward},
        device_id_type=MESH,
    )

    def band_copy(src, dst, send, recv, k):
        return pltpu.make_async_remote_copy(
            src_ref=src,
            dst_ref=dst.at[owner_index],
            send_sem=send.at[k],
            recv_sem=recv.at[owner_index],
            device_id={"band": lax.rem(z + k, BAND)},
            device_id_type=MESH,
        )

    def keep(values, ref, gathered_ref):
        upper = jnp.concatenate([values[0], values[1]], axis=0).astype(bf16)
        lower = jnp.concatenate([values[2], jnp.zeros((8, 128), f32)], axis=0).astype(bf16)
        for out in (ref, gathered_ref.at[owner_index]):
            out[0] = upper
            out[1] = lower

    @pl.when(is_owner)
    def _():
        def collect(k, total):
            source = lax.rem(z + k, BAND)
            pltpu.make_async_copy(modes.at[0], shares.at[source], share_recv.at[source]).wait()
            return total + shares[source]

        total = lax.fori_loop(1, BAND, collect, modes[owner_index])
        summed[...] = total
        layer[0] = total

        def out_layer(i, carry):
            layer_copy(by_distance(i, SPACE // 4)).start()
            return carry

        lax.fori_loop(0, SPACE // 2 - 1, out_layer, 0)
        keep([total[p] for p in range(PLANES)], dens_own, dens_modes)

        def out_dens(i, carry):
            band_copy(dens_own, dens_modes, dens_send, dens_recv, by_distance(i, BAND // 2)).start()
            return carry

        lax.fori_loop(0, BAND - 1, out_dens, 0)

        def apply(r, total):
            out = list(total)
            for q in range(PLANES):
                value = layer[r, q]
                for p in range(PLANES):
                    at = 6 * r + q - p + 5
                    out[p] = out[p] + green_ref[at] * value
                    out[PLANES + p] = out[PLANES + p] + green_ref[at + 3 * outward] * value
            return tuple(out)

        def collect_layer(r, total):
            pltpu.make_async_copy(summed, layer.at[r], layer_recv.at[r]).wait()
            return apply(r, total)

        zero = jnp.zeros((8, 128), f32)
        result = lax.fori_loop(1, SPACE // 2, collect_layer, apply(0, (zero,) * (2 * PLANES)))
        for p in range(PLANES):
            partial[p] = result[PLANES + p]
        partner_copy.start()
        partner_copy.wait()
        keep([result[p] + crossed[p] for p in range(PLANES)], hart_own, hart_modes)

        def out_hart(i, carry):
            band_copy(hart_own, hart_modes, hart_send, hart_recv, by_distance(i, BAND // 2)).start()
            return carry

        lax.fori_loop(0, BAND - 1, out_hart, 0)

    def back(spec_ref):
        halves = [[spec_ref[o, i].astype(f32) for i in range(2)] for o in range(OWNERS)]
        pieces = []
        for p in range(PLANES):
            at = 8 * (p % 2)
            blocks = [halves[o][p // 2][at : at + 8] for o in range(OWNERS)]
            head = jnp.concatenate(blocks[:6], axis=0)
            rest = jnp.concatenate(blocks[6:], axis=0)
            upper = [jnp.where(lane < 64, head, 0.0), jnp.where(lane >= 64, head, 0.0)]
            lower = [jnp.where(lane // 32 == quarter, rest, 0.0) for quarter in range(4)]
            pieces += [jnp.concatenate(upper, axis=0), jnp.concatenate(lower, axis=0)]
        spread = jnp.concatenate(pieces, axis=1).astype(bf16)
        rows_y = jnp.dot(
            inverse_ref[2048 : 2048 + NY, 0 : 2 * NY],
            jnp.concatenate([spread, spread], axis=0),
            preferred_element_type=f32,
        )
        wide = jnp.concatenate(
            [
                jnp.concatenate(
                    [
                        rows_y[r * BLOCKS : (r + 1) * BLOCKS, p * 256 : (p + 1) * 256]
                        for r in range(4)
                    ],
                    axis=1,
                )
                for p in range(PLANES)
            ],
            axis=0,
        )
        high = wide.astype(bf16)
        low = (wide - high.astype(f32)).astype(bf16)
        z_high = inverse_ref[0:1024]
        return (
            jnp.dot(high, z_high, preferred_element_type=f32)
            + jnp.dot(low, z_high, preferred_element_type=f32)
            + jnp.dot(high, inverse_ref[1024:2048], preferred_element_type=f32)
        )

    def put(out_ref, values):
        for p in range(PLANES):
            for block in range(BLOCKS):
                at = p * BLOCKS + block
                out_ref[p : p + 1, block * BLOCK : (block + 1) * BLOCK] = values[at : at + 1]

    def gathered(dst, recv):
        for o in range(OWNERS):
            @pl.when((BAND * o) // OWNERS != z)
            def _():
                pltpu.make_async_copy(dens_own, dst.at[o], recv.at[o]).wait()

    dens_copy = pltpu.make_async_copy(dens_ref, dens_hbm, table_sem.at[6])
    hart_copy = pltpu.make_async_copy(hart_ref, hart_hbm, table_sem.at[7])
    gathered(dens_modes, dens_recv)
    put(dens_ref, back(dens_modes))
    dens_copy.start()
    gathered(hart_modes, hart_recv)
    put(hart_ref, back(hart_modes))
    hart_copy.start()

    @pl.when(is_owner)
    def _():
        def drain_layer(k, carry):
            layer_copy(k).wait_send()
            return carry

        lax.fori_loop(1, SPACE // 2, drain_layer, 0)

        def drain_band(k, carry):
            band_copy(dens_own, dens_modes, dens_send, dens_recv, k).wait_send()
            band_copy(hart_own, hart_modes, hart_send, hart_recv, k).wait_send()
            return carry

        lax.fori_loop(1, BAND, drain_band, 0)

    for o in range(OWNERS):
        @pl.when((BAND * o) // OWNERS != z)
        def _():
            share_copy(o, z).wait_send()

    def drain(c, carry):
        for phase in range(2):
            for kind in range(4):
                halo(phase, kind, c).wait_send()
        for half in range(2):
            for part in range(2):
                stores(c, half, part).wait()
        return carry

    lax.fori_loop(0, CHUNKS, drain, 0)
    dens_copy.wait()
    hart_copy.wait()


def settle(prop_in, dens_in, hart_in, prop_out, dens_out, hart_out, prop_at, dens_at, hart_at, in_sem, out_sem):
    routes = [(dens_in, dens_at, dens_out), (hart_in, hart_at, hart_out)]
    for part in range(2):
        for p in range(PLANES):
            routes.append((prop_in.at[part, p], prop_at.at[part, p], prop_out.at[part, p]))
    inward = [pltpu.make_async_copy(r[0], r[1], in_sem.at[i]) for i, r in enumerate(routes)]
    outward = [pltpu.make_async_copy(r[1], r[2], out_sem.at[i]) for i, r in enumerate(routes)]
    for copy in inward:
        copy.start()
    for i in range(len(routes)):
        inward[i].wait()
        outward[i].start()
    for copy in outward:
        copy.wait()


def per_device(orbitals, potential, occupations):
    f32 = jnp.float32
    bf16 = jnp.bfloat16
    forward, inverse, green = transform_tables()
    vmem = pltpu.VMEM
    dma = pltpu.SemaphoreType.DMA
    anywhere = pl.BlockSpec(memory_space=pl.ANY)
    raw = pl.pallas_call(
        body,
        out_shape=(
            jax.ShapeDtypeStruct((2, PLANES, 4, CELLS), f32),
            jax.ShapeDtypeStruct((PLANES, CELLS), f32),
            jax.ShapeDtypeStruct((PLANES, CELLS), f32),
        ),
        in_specs=[anywhere] * 7,
        out_specs=(anywhere, anywhere, anywhere),
        scratch_shapes=[
            vmem((PLANES, CELLS), f32),
            pltpu.SMEM((4,), f32),
            vmem((PLANES, CELLS), f32),
            vmem((PLANES, CELLS), f32),
            vmem((2, 16 * PLANES * PER_CHUNK, BLOCK), f32),
            vmem((PLANES, FIELDS, CELLS), f32),
            vmem((PLANES, FIELDS, CELLS), f32),
            vmem((PLANES, FIELDS, CELLS), f32),
            vmem((PLANES, 16, PADDED), bf16),
            vmem((PLANES, 16, PADDED), bf16),
            vmem((2, 4, 16, FOLD), bf16),
            vmem((2, 4, 16, FOLD), bf16),
            vmem((PLANES * BLOCKS, BLOCK), f32),
            vmem((WINDOW, BLOCK), bf16),
            vmem((BLOCK + NY, 1024), f32),
            vmem((2048 + NY, BLOCK), bf16),
            vmem((NX + 5, 8, 128), f32),
            vmem((OWNERS, PLANES, 8, 128), f32),
            vmem((BAND, PLANES, 8, 128), f32),
            vmem((PLANES, 8, 128), f32),
            vmem((SPACE // 2, PLANES, 8, 128), f32),
            vmem((PLANES, 8, 128), f32),
            vmem((PLANES, 8, 128), f32),
            vmem((2, 16, 128), bf16),
            vmem((2, 16, 128), bf16),
            vmem((OWNERS, 2, 16, 128), bf16),
            vmem((OWNERS, 2, 16, 128), bf16),
            dma((CHUNKS, 2, 2)),
            dma((8,)),
            dma((CHUNKS, 2, 2)),
            dma((2, 4, CHUNKS)),
            dma((2, 4, CHUNKS)),
            pltpu.SemaphoreType.REGULAR((5,)),
            dma((OWNERS,)),
            dma((BAND,)),
            dma((SPACE // 2,)),
            dma((SPACE // 2,)),
            dma((2,)),
            dma((BAND,)),
            dma((OWNERS,)),
            dma((BAND,)),
            dma((OWNERS,)),
        ],
        compiler_params=pltpu.CompilerParams(
            collective_id=0, has_side_effects=True, vmem_limit_bytes=62 * 2**20
        ),
    )(
        jnp.transpose(orbitals, (0, 2, 1, 3)),
        potential,
        occupations,
        jnp.asarray(band_matrix()),
        jnp.asarray(forward),
        jnp.asarray(inverse),
        jnp.asarray(green),
    )
    prop, dens, hart = pl.pallas_call(
        settle,
        out_shape=[jax.ShapeDtypeStruct(r.shape, r.dtype) for r in raw],
        in_specs=[anywhere] * 3,
        out_specs=[anywhere] * 3,
        scratch_shapes=[vmem(r.shape, r.dtype) for r in raw] + [dma((8,)), dma((8,))],
        compiler_params=pltpu.CompilerParams(vmem_limit_bytes=62 * 2**20),
    )(*raw)
    return jnp.transpose(prop, (0, 2, 1, 3)), dens, hart


def solution(mesh):
    in_specs = (P(None, "band", "space", None), P("space", None), P("band"))
    out_specs = (P(None, "band", "space", None), P("space", None), P("space", None))
    return jax.shard_map(
        per_device, mesh=mesh, in_specs=in_specs, out_specs=out_specs, check_vma=False
    )
```

```python
import functools
import math

import jax
import jax.numpy as jnp
import ml_dtypes
import numpy as np
from jax import lax
from jax.experimental import pallas as pl
from jax.experimental.pallas import tpu as pltpu
from jax.sharding import PartitionSpec as P

NX = 96
NY = 96
NZ = 96

stencil_coeffs = (-205.0 / 72.0, 8.0 / 5.0, -1.0 / 5.0, 8.0 / 315.0, -1.0 / 560.0)
energy_shift = 6.0
energy_scale = 8.0
bessel_terms = (0.7651976865579666, 0.44005058574493355, 0.11490348493190049)
scaled_coeffs = tuple(c / stencil_coeffs[1] for c in stencil_coeffs)

MESH = pl.DeviceIdType.MESH
PLANES = 3
FIELDS = 8
CELLS = NY * NZ
FOLD = CELLS // 2
BLOCK = 4 * NZ
BLOCKS = CELLS // BLOCK
CHUNKS = 4
CHUNK = FOLD // CHUNKS
PER_CHUNK = CHUNK // BLOCK
WINDOW = 3 * BLOCK
PADDED = FOLD + 2 * BLOCK
SPACE = 32
BAND = 16
OWNERS = 9
ORBITALS = 64


def band_matrix():
    table = np.zeros((WINDOW, BLOCK))
    for cell in range(BLOCK):
        z = cell % NZ
        for offset in range(1, 5):
            c = scaled_coeffs[offset]
            table[BLOCK + cell + offset * NZ, cell] += c
            table[BLOCK + cell - offset * NZ, cell] += c
            if z + offset < NZ:
                table[BLOCK + cell + offset, cell] += c
            if z - offset >= 0:
                table[BLOCK + cell - offset, cell] += c
    return table.astype(ml_dtypes.bfloat16)


def real_basis(length):
    cells = np.arange(length)
    rows = [np.full(length, 1.0 / math.sqrt(length))]
    waves = [0]
    for k in range(1, length // 2):
        phase = 2.0 * math.pi * ((k * cells) % length) / length
        rows.append(math.sqrt(2.0 / length) * np.cos(phase))
        rows.append(math.sqrt(2.0 / length) * np.sin(phase))
        waves += [k, k]
    rows.append(np.where(cells % 2 == 0, 1.0, -1.0) / math.sqrt(length))
    waves.append(length // 2)
    return np.stack(rows), (2.0 * math.pi / length * np.array(waves)) ** 2


def split(table):
    high = table.astype(ml_dtypes.bfloat16)
    low = (table - high.astype(np.float64)).astype(ml_dtypes.bfloat16)
    return high, low


def transform_tables():
    basis, squares = real_basis(NY)
    order = np.array([4 * block + r for r in range(4) for block in range(BLOCKS)])
    forward_y = basis[:, order]
    lanes = np.arange(128)
    forward_z = np.zeros((4, NZ, 4, 128))
    for r in range(4):
        forward_z[r, :, r, :NZ] = basis.T
    forward_z = forward_z.reshape(BLOCK, 512)
    row = np.arange(72)[:, None]
    mode_y = np.where(row < 48, row + 48 * (lanes >= 64), row - 48 + 24 * (lanes // 32))
    mode_z = np.where(row < 48, lanes % 64, 64 + lanes % 32)
    across = squares[mode_y] + squares[mode_z]
    cells = np.arange(NX)
    signed = np.where(cells < NX // 2, cells, cells - NX)
    along = (2.0 * math.pi / NX * signed) ** 2
    total = along[:, None, None] + across
    kernel = np.where(total > 0, 4.0 * math.pi / np.where(total > 0, total, 1.0), 0.0)
    green = np.real(np.fft.ifft(kernel, axis=0))
    green = green[(np.arange(NX + 5) - 5) % NX]
    green = green.reshape(NX + 5, OWNERS, 8, 128).transpose(1, 0, 2, 3)
    f32 = np.float32
    y_high, y_low = split(forward_y.T)
    z_high, z_low = split(forward_z.T)
    return (
        np.concatenate([forward_z, np.pad(forward_y, ((0, 0), (0, 512 - NY)))]).astype(f32),
        np.concatenate([z_high, z_low, np.pad(np.concatenate([y_high, y_low], axis=1), ((0, 0), (0, BLOCK - 2 * NY)))]),
        green.astype(f32),
    )


def exact_dot(a, b):
    return lax.dot_general(
        a,
        b,
        (((1,), (0,)), ((), ())),
        precision=lax.Precision.HIGHEST,
        preferred_element_type=jnp.float32,
    )


def body(
    orb_hbm, pot_hbm, occ_hbm, band_hbm, forward_hbm, inverse_hbm, green_hbm,
    prop_hbm, dens_hbm, hart_hbm,
    pot_ref, occ_ref, dens_ref, hart_ref, flat, field, first, prop, own0, own1, rim0, rim1, lines,
    band_ref, forward_ref, inverse_ref, green_ref,
    modes, shares, summed, layer, partial, crossed, dens_own, hart_own, dens_modes, hart_modes,
    load_sem, table_sem, store_sem, halo_send, halo_recv, hand,
    share_send, share_recv, layer_send, layer_recv, cross_sem,
    dens_send, dens_recv, hart_send, hart_recv,
):
    s = lax.axis_index("space")
    z = lax.axis_index("band")
    core = lax.rem(s, 2)
    f32 = jnp.float32
    bf16 = jnp.bfloat16

    def lanes_of(c, extra=0, size=CHUNK):
        return pl.ds(pl.multiple_of(c * CHUNK + extra, 128), size)

    def load(c, half, part):
        lanes = lanes_of(c, half * FOLD)
        return pltpu.make_async_copy(
            orb_hbm.at[part, :, :, lanes],
            field.at[:, pl.ds(4 * part, 4), lanes],
            load_sem.at[c, half, part],
        )

    barrier = pltpu.get_barrier_semaphore()

    def greet(sem, axis, me, size, offset):
        for step in (offset, size - offset):
            pl.semaphore_signal(
                sem, inc=1, device_id={axis: lax.rem(me + step, size)}, device_id_type=MESH
            )

    for offset in (1, 2):
        greet(barrier, "space", s, SPACE, offset)
        greet(barrier, "band", z, BAND, offset)
    for c in range(CHUNKS):
        for half in range(2):
            for part in range(2):
                load(c, half, part).start()
    owner = (OWNERS * z + BAND - 1) // BAND
    owner_index = jnp.minimum(owner, OWNERS - 1)
    is_owner = (BAND * owner) // OWNERS == z
    pot_copy = pltpu.make_async_copy(pot_hbm, pot_ref, table_sem.at[4])
    pot_copy.start()
    occ_copy = pltpu.make_async_copy(occ_hbm, occ_ref, table_sem.at[5])
    occ_copy.start()
    tables = [
        pltpu.make_async_copy(src, dst, table_sem.at[i])
        for i, (src, dst) in enumerate(
            [
                (band_hbm, band_ref),
                (forward_hbm, forward_ref),
                (inverse_hbm, inverse_ref),
                (green_hbm.at[owner_index], green_ref),
            ]
        )
    ]
    tables[0].start()

    outward = 2 * core - 1
    owns = (own0, own1)
    rims = (rim0, rim1)

    def halo(phase, kind, c):
        own, rim = owns[phase], rims[phase]
        inside = lanes_of(c, BLOCK)
        outside = lanes_of(c)
        if kind == 0:
            src = own.at[:, :, inside]
            dst = rim.at[1 - core, pl.ds(core, 3), :, outside]
            step = outward
        elif kind == 1:
            src = own.at[:, :, inside]
            dst = rim.at[core, pl.ds(1 - core, 3), :, outside]
            step = -outward
        elif kind == 2:
            src = own.at[2 * (1 - core), :, inside]
            dst = rim.at[core, 3 * core, :, outside]
            step = -2 * outward
        else:
            src = rim.at[core, 3 * (1 - core), :, outside]
            dst = rim.at[core, 3 * core, :, outside]
            step = -outward
        return pltpu.make_async_remote_copy(
            src_ref=src,
            dst_ref=dst,
            send_sem=halo_send.at[phase, kind, c],
            recv_sem=halo_recv.at[phase, kind, c],
            device_id={"space": lax.rem(s + step + SPACE, SPACE)},
            device_id_type=MESH,
        )

    def fold_edges(source, own):
        zeros = jnp.zeros((FIELDS, BLOCK), f32)
        for p in range(PLANES):
            own[p, :, 0:BLOCK] = jnp.concatenate(
                [zeros, source[p, :, FOLD - BLOCK : FOLD]], axis=0
            ).astype(bf16)
            own[p, :, PADDED - BLOCK : PADDED] = jnp.concatenate(
                [source[p, :, FOLD : FOLD + BLOCK], zeros], axis=0
            ).astype(bf16)

    def pack(c, carry):
        for half in range(2):
            for part in range(2):
                load(c, half, part).wait()
        for p in range(PLANES):
            own0[p, :, lanes_of(c, BLOCK)] = jnp.concatenate(
                [field[p, :, lanes_of(c)], field[p, :, lanes_of(c, FOLD)]], axis=0
            ).astype(bf16)
        return carry

    lax.fori_loop(0, CHUNKS, pack, 0)
    pl.semaphore_wait(barrier, 8)

    def ship(c, carry):
        for kind in range(3):
            halo(0, kind, c).start()
        return carry

    lax.fori_loop(0, CHUNKS, ship, 0)
    greet(hand.at[0], "band", z, BAND, 2)
    greet(hand.at[1], "space", s, SPACE, 2)
    fold_edges(field, own0)
    for copy in tables[1:]:
        copy.start()
    tables[0].wait()

    pot_copy.wait()
    occ_copy.wait()
    edge = (s - core) // 2
    before = jnp.where(edge >= 1, 1.0, 0.0).astype(f32)
    after = jnp.where(edge <= SPACE // 2 - 2, 1.0, 0.0).astype(f32)
    outer_weight = jnp.where(core == 0, before, after)
    inner_weight = jnp.where(core == 0, after, before)

    gain = stencil_coeffs[1] / (2.0 * energy_scale)
    level = -(energy_shift + 1.5 * stencil_coeffs[0]) / energy_scale

    def mirrored(position, last):
        return position + core * (last - 2 * position)

    def receive(phase, c):
        own = owns[phase]
        windows = [
            own[mirrored(q, 2), :, lanes_of(c, b * BLOCK, WINDOW)]
            for q in range(PLANES)
            for b in range(PER_CHUNK)
        ]
        flat[lax.rem(c, 2)] = jnp.dot(
            jnp.concatenate(windows, axis=0), band_ref[...], preferred_element_type=f32
        )
        halo(phase, 0, c).wait_recv()
        halo(phase, 3, c).start()

    def stencil(phase, source, c, finish):
        own, rim = owns[phase], rims[phase]
        slot = lax.rem(c, 2)
        for kind in (1, 2, 3):
            halo(phase, kind, c).wait_recv()
        for b in range(PER_CHUNK):
            outside = lanes_of(c, b * BLOCK, BLOCK)
            inside = lanes_of(c, (b + 1) * BLOCK, BLOCK)
            outer = [
                rim[core, mirrored(at, 3), :, outside].astype(f32) * outer_weight
                for at in range(4)
            ]
            middle = [own[mirrored(at, 2), :, inside].astype(f32) for at in range(PLANES)]
            inner = [rim[1 - core, mirrored(at, 3), :, outside].astype(f32) for at in range(4)]
            stack = outer + middle + inner[:3] + [inner[3] * inner_weight]
            for q in range(PLANES):
                p = mirrored(q, 2)
                across = stack[q + 5] + stack[q + 3]
                for offset in range(2, 5):
                    across = across + scaled_coeffs[offset] * (
                        stack[q + 4 + offset] + stack[q + 4 - offset]
                    )
                at = 16 * (q * PER_CHUNK + b)
                across = gain * (across + flat[slot, at : at + 16])
                for half in range(2):
                    lanes = lanes_of(c, half * FOLD + b * BLOCK, BLOCK)
                    centre = source[p, :, lanes]
                    factor = pot_ref[pl.ds(p, 1), lanes] * (1.0 / energy_scale) + level
                    value = centre * factor - across[8 * half : 8 * half + 8]
                    finish(p, b, half, lanes, centre, value)

    def sweep(phase, use):
        receive(phase, 0)

        def step(c, carry):
            @pl.when(c < CHUNKS)
            def _():
                receive(phase, c)

            use(c - 1)
            return carry

        lax.fori_loop(1, CHUNKS + 1, step, 0)


    def first_chunk(c):
        values = []

        def finish(p, b, half, lanes, centre, value):
            first[p, :, lanes] = value
            values.append(value)
            if half == 1:
                own1[p, :, lanes_of(c, (b + 1) * BLOCK, BLOCK)] = jnp.concatenate(
                    values[-2:], axis=0
                ).astype(bf16)

        stencil(0, field, c, finish)
        for kind in range(3):
            halo(1, kind, c).start()

    sweep(0, first_chunk)
    pl.semaphore_wait(hand.at[0], 2)
    greet(hand.at[2], "band", z, BAND, 4)
    pl.semaphore_wait(hand.at[1], 2)
    greet(hand.at[3], "space", s, SPACE, 4)
    fold_edges(first, own1)

    rows = lax.broadcasted_iota(jnp.int32, (FIELDS, BLOCK), 0)
    weight = jnp.zeros((FIELDS, BLOCK), f32)
    for o in range(4):
        weight = jnp.where(lax.rem(rows, 4) == o, occ_ref[o] * (1.0 / ORBITALS), weight)
    sign = jnp.where(rows < 4, 2.0 * bessel_terms[1], -2.0 * bessel_terms[1]).astype(f32)

    def stores(c, half, part):
        lanes = lanes_of(c, half * FOLD)
        return pltpu.make_async_copy(
            prop.at[:, pl.ds(4 * part, 4), lanes],
            prop_hbm.at[part, :, :, lanes],
            store_sem.at[c, half, part],
        )

    def second_chunk(c):
        def finish(p, b, half, lanes, centre, value):
            swapped = jnp.concatenate([centre[4:8], centre[0:4]], axis=0)
            result = (
                (bessel_terms[0] + 2.0 * bessel_terms[2]) * field[p, :, lanes]
                + sign * swapped
                - (4.0 * bessel_terms[2]) * value
            )
            prop[p, :, lanes] = result
            share = jnp.sum(weight * (result * result), axis=0, keepdims=True)
            lines[pl.ds(p * BLOCKS + half * (BLOCKS // 2) + c * PER_CHUNK + b, 1), :] = share

        stencil(1, first, c, finish)
        for half in range(2):
            for part in range(2):
                stores(c, half, part).start()

    sweep(1, second_chunk)
    pl.semaphore_wait(hand.at[2], 2)
    pl.semaphore_wait(hand.at[3], 2)
    greet(hand.at[4], "space", s, SPACE, 8)

    for copy in tables[1:]:
        copy.wait()
    turned = exact_dot(lines[...], forward_ref[0:BLOCK, :])
    stacked = jnp.concatenate(
        [
            jnp.concatenate(
                [
                    turned[p * BLOCKS : (p + 1) * BLOCKS, r * 128 : (r + 1) * 128]
                    for r in range(4)
                ],
                axis=0,
            )
            for p in range(PLANES)
        ],
        axis=1,
    )
    spectral = exact_dot(forward_ref[BLOCK : BLOCK + NY, 0:NY], stacked)
    lane = lax.broadcasted_iota(jnp.int32, (1, 128), 1)
    for p in range(PLANES):
        full = spectral[:, p * 128 : (p + 1) * 128]
        head = jnp.where(lane < 64, full[0:48], pltpu.roll(full[48:96], 64, 1))
        rest = pltpu.roll(full[0:24], 64, 1)
        for quarter in range(1, 4):
            piece = full[24 * quarter : 24 * quarter + 24]
            turn = (32 * quarter + 64) % 128
            piece = pltpu.roll(piece, turn, 1) if turn else piece
            rest = jnp.where(lane >= 32 * quarter, piece, rest)
        for o in range(6):
            modes[o, p] = head[8 * o : 8 * o + 8]
        for o in range(3):
            modes[6 + o, p] = rest[8 * o : 8 * o + 8]


    def share_copy(o, source):
        return pltpu.make_async_remote_copy(
            src_ref=modes.at[o],
            dst_ref=shares.at[source],
            send_sem=share_send.at[o],
            recv_sem=share_recv.at[source],
            device_id={"band": (BAND * o) // OWNERS},
            device_id_type=MESH,
        )

    def by_distance(i, middle):
        return middle + jnp.where(lax.rem(i, 2) == 0, i // 2, -(i + 1) // 2)

    def out_share(i, carry):
        target = lax.rem(z + by_distance(i, BAND // 2), BAND)
        o = (OWNERS * target + BAND - 1) // BAND

        @pl.when((BAND * o) // OWNERS == target)
        def _():
            share_copy(o, z).start()

        return carry

    lax.fori_loop(0, BAND - 1, out_share, 0)
    pl.semaphore_wait(hand.at[4], 2)

    def layer_copy(k):
        return pltpu.make_async_remote_copy(
            src_ref=summed,
            dst_ref=layer.at[SPACE // 2 - k],
            send_sem=layer_send.at[k],
            recv_sem=layer_recv.at[SPACE // 2 - k],
            device_id={"space": lax.rem(s + 2 * k, SPACE)},
            device_id_type=MESH,
        )

    partner_copy = pltpu.make_async_remote_copy(
        src_ref=partial,
        dst_ref=crossed,
        send_sem=cross_sem.at[0],
        recv_sem=cross_sem.at[1],
        device_id={"space": s - outward},
        device_id_type=MESH,
    )

    def band_copy(src, dst, send, recv, k):
        return pltpu.make_async_remote_copy(
            src_ref=src,
            dst_ref=dst.at[owner_index],
            send_sem=send.at[k],
            recv_sem=recv.at[owner_index],
            device_id={"band": lax.rem(z + k, BAND)},
            device_id_type=MESH,
        )

    def keep(values, ref, gathered_ref):
        upper = jnp.concatenate([values[0], values[1]], axis=0).astype(bf16)
        lower = jnp.concatenate([values[2], jnp.zeros((8, 128), f32)], axis=0).astype(bf16)
        for out in (ref, gathered_ref.at[owner_index]):
            out[0] = upper
            out[1] = lower

    @pl.when(is_owner)
    def _():
        def collect(k, total):
            source = lax.rem(z + k, BAND)
            pltpu.make_async_copy(modes.at[0], shares.at[source], share_recv.at[source]).wait()
            return total + shares[source]

        total = lax.fori_loop(1, BAND, collect, modes[owner_index])
        summed[...] = total
        layer[0] = total

        def out_layer(i, carry):
            layer_copy(by_distance(i, SPACE // 4)).start()
            return carry

        lax.fori_loop(0, SPACE // 2 - 1, out_layer, 0)
        keep([total[p] for p in range(PLANES)], dens_own, dens_modes)

        def out_dens(i, carry):
            band_copy(dens_own, dens_modes, dens_send, dens_recv, by_distance(i, BAND // 2)).start()
            return carry

        lax.fori_loop(0, BAND - 1, out_dens, 0)

        def apply(r, total):
            out = list(total)
            for q in range(PLANES):
                value = layer[r, q]
                for p in range(PLANES):
                    at = 6 * r + q - p + 5
                    out[p] = out[p] + green_ref[at] * value
                    out[PLANES + p] = out[PLANES + p] + green_ref[at + 3 * outward] * value
            return tuple(out)

        def collect_layer(r, total):
            pltpu.make_async_copy(summed, layer.at[r], layer_recv.at[r]).wait()
            return apply(r, total)

        zero = jnp.zeros((8, 128), f32)
        result = lax.fori_loop(1, SPACE // 2, collect_layer, apply(0, (zero,) * (2 * PLANES)))
        for p in range(PLANES):
            partial[p] = result[PLANES + p]
        partner_copy.start()
        partner_copy.wait()
        keep([result[p] + crossed[p] for p in range(PLANES)], hart_own, hart_modes)

        def out_hart(i, carry):
            band_copy(hart_own, hart_modes, hart_send, hart_recv, by_distance(i, BAND // 2)).start()
            return carry

        lax.fori_loop(0, BAND - 1, out_hart, 0)

    def back(spec_ref):
        halves = [[spec_ref[o, i].astype(f32) for i in range(2)] for o in range(OWNERS)]
        pieces = []
        for p in range(PLANES):
            at = 8 * (p % 2)
            blocks = [halves[o][p // 2][at : at + 8] for o in range(OWNERS)]
            head = jnp.concatenate(blocks[:6], axis=0)
            rest = jnp.concatenate(blocks[6:], axis=0)
            upper = jnp.concatenate([head, pltpu.roll(head, 64, 1)], axis=0)
            lower = jnp.concatenate(
                [pltpu.roll(rest, 64, 1), pltpu.roll(rest, 32, 1), rest, pltpu.roll(rest, 96, 1)],
                axis=0,
            )
            pieces.append(jnp.where(lane < 64, upper, jnp.where(lane < NZ, lower, 0.0)))
        spread = jnp.concatenate(pieces, axis=1).astype(bf16)
        rows_y = jnp.dot(
            inverse_ref[1024 : 1024 + NY, 0 : 2 * NY],
            jnp.concatenate([spread, spread], axis=0),
            preferred_element_type=f32,
        )
        wide = jnp.concatenate(
            [
                jnp.concatenate(
                    [
                        rows_y[r * BLOCKS : (r + 1) * BLOCKS, p * 128 : (p + 1) * 128]
                        for r in range(4)
                    ],
                    axis=1,
                )
                for p in range(PLANES)
            ],
            axis=0,
        )
        high = wide.astype(bf16)
        low = (wide - high.astype(f32)).astype(bf16)
        z_high = inverse_ref[0:512]
        return (
            jnp.dot(high, z_high, preferred_element_type=f32)
            + jnp.dot(low, z_high, preferred_element_type=f32)
            + jnp.dot(high, inverse_ref[512:1024], preferred_element_type=f32)
        )

    def put(out_ref, values):
        for p in range(PLANES):
            for block in range(BLOCKS):
                at = p * BLOCKS + block
                out_ref[p : p + 1, block * BLOCK : (block + 1) * BLOCK] = values[at : at + 1]

    def gathered(dst, recv):
        for o in range(OWNERS):
            @pl.when((BAND * o) // OWNERS != z)
            def _():
                pltpu.make_async_copy(dens_own, dst.at[o], recv.at[o]).wait()

    dens_copy = pltpu.make_async_copy(dens_ref, dens_hbm, table_sem.at[6])
    hart_copy = pltpu.make_async_copy(hart_ref, hart_hbm, table_sem.at[7])
    gathered(dens_modes, dens_recv)
    put(dens_ref, back(dens_modes))
    dens_copy.start()

    @pl.when(is_owner)
    def _():
        def drain_layer(k, carry):
            layer_copy(k).wait_send()
            return carry

        lax.fori_loop(1, SPACE // 2, drain_layer, 0)

        def drain_dens(k, carry):
            band_copy(dens_own, dens_modes, dens_send, dens_recv, k).wait_send()
            return carry

        lax.fori_loop(1, BAND, drain_dens, 0)

    for o in range(OWNERS):
        @pl.when((BAND * o) // OWNERS != z)
        def _():
            share_copy(o, z).wait_send()

    def drain(c, carry):
        for phase in range(2):
            for kind in range(4):
                halo(phase, kind, c).wait_send()
        for half in range(2):
            for part in range(2):
                stores(c, half, part).wait()
        return carry

    lax.fori_loop(0, CHUNKS, drain, 0)
    dens_copy.wait()
    gathered(hart_modes, hart_recv)
    put(hart_ref, back(hart_modes))
    hart_copy.start()

    @pl.when(is_owner)
    def _():
        def drain_hart(k, carry):
            band_copy(hart_own, hart_modes, hart_send, hart_recv, k).wait_send()
            return carry

        lax.fori_loop(1, BAND, drain_hart, 0)

    hart_copy.wait()


def settle(prop_in, dens_in, hart_in, prop_out, dens_out, hart_out, prop_at, dens_at, hart_at, in_sem, out_sem):
    routes = [(dens_in, dens_at, dens_out), (hart_in, hart_at, hart_out)]
    for part in range(2):
        for p in range(PLANES):
            routes.append((prop_in.at[part, p], prop_at.at[part, p], prop_out.at[part, p]))
    inward = [pltpu.make_async_copy(r[0], r[1], in_sem.at[i]) for i, r in enumerate(routes)]
    outward = [pltpu.make_async_copy(r[1], r[2], out_sem.at[i]) for i, r in enumerate(routes)]
    for copy in inward:
        copy.start()
    for i in range(len(routes)):
        inward[i].wait()
        outward[i].start()
    for copy in outward:
        copy.wait()


def per_device(orbitals, potential, occupations):
    f32 = jnp.float32
    bf16 = jnp.bfloat16
    forward, inverse, green = transform_tables()
    vmem = pltpu.VMEM
    dma = pltpu.SemaphoreType.DMA
    anywhere = pl.BlockSpec(memory_space=pl.ANY)
    raw = pl.pallas_call(
        body,
        out_shape=(
            jax.ShapeDtypeStruct((2, PLANES, 4, CELLS), f32),
            jax.ShapeDtypeStruct((PLANES, CELLS), f32),
            jax.ShapeDtypeStruct((PLANES, CELLS), f32),
        ),
        in_specs=[anywhere] * 7,
        out_specs=(anywhere, anywhere, anywhere),
        scratch_shapes=[
            vmem((PLANES, CELLS), f32),
            pltpu.SMEM((4,), f32),
            vmem((PLANES, CELLS), f32),
            vmem((PLANES, CELLS), f32),
            vmem((2, 16 * PLANES * PER_CHUNK, BLOCK), f32),
            vmem((PLANES, FIELDS, CELLS), f32),
            vmem((PLANES, FIELDS, CELLS), f32),
            vmem((PLANES, FIELDS, CELLS), f32),
            vmem((PLANES, 16, PADDED), bf16),
            vmem((PLANES, 16, PADDED), bf16),
            vmem((2, 4, 16, FOLD), bf16),
            vmem((2, 4, 16, FOLD), bf16),
            vmem((PLANES * BLOCKS, BLOCK), f32),
            vmem((WINDOW, BLOCK), bf16),
            vmem((BLOCK + NY, 512), f32),
            vmem((1024 + NY, BLOCK), bf16),
            vmem((NX + 5, 8, 128), f32),
            vmem((OWNERS, PLANES, 8, 128), f32),
            vmem((BAND, PLANES, 8, 128), f32),
            vmem((PLANES, 8, 128), f32),
            vmem((SPACE // 2, PLANES, 8, 128), f32),
            vmem((PLANES, 8, 128), f32),
            vmem((PLANES, 8, 128), f32),
            vmem((2, 16, 128), bf16),
            vmem((2, 16, 128), bf16),
            vmem((OWNERS, 2, 16, 128), bf16),
            vmem((OWNERS, 2, 16, 128), bf16),
            dma((CHUNKS, 2, 2)),
            dma((8,)),
            dma((CHUNKS, 2, 2)),
            dma((2, 4, CHUNKS)),
            dma((2, 4, CHUNKS)),
            pltpu.SemaphoreType.REGULAR((5,)),
            dma((OWNERS,)),
            dma((BAND,)),
            dma((SPACE // 2,)),
            dma((SPACE // 2,)),
            dma((2,)),
            dma((BAND,)),
            dma((OWNERS,)),
            dma((BAND,)),
            dma((OWNERS,)),
        ],
        compiler_params=pltpu.CompilerParams(
            collective_id=0, has_side_effects=True, vmem_limit_bytes=62 * 2**20
        ),
    )(
        jnp.transpose(orbitals, (0, 2, 1, 3)),
        potential,
        occupations,
        jnp.asarray(band_matrix()),
        jnp.asarray(forward),
        jnp.asarray(inverse),
        jnp.asarray(green),
    )
    prop, dens, hart = pl.pallas_call(
        settle,
        out_shape=[jax.ShapeDtypeStruct(r.shape, r.dtype) for r in raw],
        in_specs=[anywhere] * 3,
        out_specs=[anywhere] * 3,
        scratch_shapes=[vmem(r.shape, r.dtype) for r in raw] + [dma((8,)), dma((8,))],
        compiler_params=pltpu.CompilerParams(vmem_limit_bytes=62 * 2**20),
    )(*raw)
    return jnp.transpose(prop, (0, 2, 1, 3)), dens, hart


def solution(mesh):
    in_specs = (P(None, "band", "space", None), P("space", None), P("band"))
    out_specs = (P(None, "band", "space", None), P("space", None), P("space", None))
    return jax.shard_map(
        per_device, mesh=mesh, in_specs=in_specs, out_specs=out_specs, check_vma=False
    )
```

```python
import functools
import math

import jax
import jax.numpy as jnp
import ml_dtypes
import numpy as np
from jax import lax
from jax.experimental import pallas as pl
from jax.experimental.pallas import tpu as pltpu
from jax.sharding import PartitionSpec as P

NX = 96
NY = 96
NZ = 96

stencil_coeffs = (-205.0 / 72.0, 8.0 / 5.0, -1.0 / 5.0, 8.0 / 315.0, -1.0 / 560.0)
energy_shift = 6.0
energy_scale = 8.0
bessel_terms = (0.7651976865579666, 0.44005058574493355, 0.11490348493190049)
scaled_coeffs = tuple(c / stencil_coeffs[1] for c in stencil_coeffs)

MESH = pl.DeviceIdType.MESH
PLANES = 3
FIELDS = 8
CELLS = NY * NZ
FOLD = CELLS // 2
BLOCK = 4 * NZ
BLOCKS = CELLS // BLOCK
CHUNKS = 6
CHUNK = FOLD // CHUNKS
PER_CHUNK = CHUNK // BLOCK
WINDOW = 3 * BLOCK
PADDED = FOLD + 2 * BLOCK
SPACE = 32
BAND = 16
OWNERS = 9
ORBITALS = 64


def band_matrix():
    table = np.zeros((WINDOW, BLOCK))
    for cell in range(BLOCK):
        z = cell % NZ
        for offset in range(1, 5):
            c = scaled_coeffs[offset]
            table[BLOCK + cell + offset * NZ, cell] += c
            table[BLOCK + cell - offset * NZ, cell] += c
            if z + offset < NZ:
                table[BLOCK + cell + offset, cell] += c
            if z - offset >= 0:
                table[BLOCK + cell - offset, cell] += c
    return table.astype(ml_dtypes.bfloat16)


def real_basis(length):
    cells = np.arange(length)
    rows = [np.full(length, 1.0 / math.sqrt(length))]
    waves = [0]
    for k in range(1, length // 2):
        phase = 2.0 * math.pi * ((k * cells) % length) / length
        rows.append(math.sqrt(2.0 / length) * np.cos(phase))
        rows.append(math.sqrt(2.0 / length) * np.sin(phase))
        waves += [k, k]
    rows.append(np.where(cells % 2 == 0, 1.0, -1.0) / math.sqrt(length))
    waves.append(length // 2)
    return np.stack(rows), (2.0 * math.pi / length * np.array(waves)) ** 2


def split(table):
    high = table.astype(ml_dtypes.bfloat16)
    low = (table - high.astype(np.float64)).astype(ml_dtypes.bfloat16)
    return high, low


def transform_tables():
    basis, squares = real_basis(NY)
    order = np.array([4 * block + r for r in range(4) for block in range(BLOCKS)])
    forward_y = basis[:, order]
    lanes = np.arange(128)
    forward_z = np.zeros((4, NZ, 4, 128))
    for r in range(4):
        forward_z[r, :, r, :NZ] = basis.T
    forward_z = forward_z.reshape(BLOCK, 512)
    row = np.arange(72)[:, None]
    mode_y = np.where(row < 48, row + 48 * (lanes >= 64), row - 48 + 24 * (lanes // 32))
    mode_z = np.where(row < 48, lanes % 64, 64 + lanes % 32)
    across = squares[mode_y] + squares[mode_z]
    cells = np.arange(NX)
    signed = np.where(cells < NX // 2, cells, cells - NX)
    along = (2.0 * math.pi / NX * signed) ** 2
    total = along[:, None, None] + across
    kernel = np.where(total > 0, 4.0 * math.pi / np.where(total > 0, total, 1.0), 0.0)
    green = np.real(np.fft.ifft(kernel, axis=0))
    green = green[(np.arange(NX + 5) - 5) % NX]
    green = green.reshape(NX + 5, OWNERS, 8, 128).transpose(1, 0, 2, 3)
    f32 = np.float32
    y_high, y_low = split(forward_y.T)
    z_high, z_low = split(forward_z.T)
    return (
        np.concatenate([forward_z, np.pad(forward_y, ((0, 0), (0, 512 - NY)))]).astype(f32),
        np.concatenate([z_high, z_low, np.pad(np.concatenate([y_high, y_low], axis=1), ((0, 0), (0, BLOCK - 2 * NY)))]),
        green.astype(f32),
    )


def exact_dot(a, b):
    return lax.dot_general(
        a,
        b,
        (((1,), (0,)), ((), ())),
        precision=lax.Precision.HIGHEST,
        preferred_element_type=jnp.float32,
    )


def body(
    orb_hbm, pot_hbm, occ_hbm, band_hbm, forward_hbm, inverse_hbm, green_hbm,
    prop_hbm, dens_hbm, hart_hbm,
    pot_ref, occ_ref, dens_ref, hart_ref, flat, field, first, prop, own0, own1, rim0, rim1, lines,
    band_ref, forward_ref, inverse_ref, green_ref,
    modes, shares, summed, layer, partial, crossed, dens_own, hart_own, dens_modes, hart_modes,
    load_sem, table_sem, store_sem, halo_send, halo_recv, hand,
    share_send, share_recv, layer_send, layer_recv, cross_sem,
    dens_send, dens_recv, hart_send, hart_recv,
):
    s = lax.axis_index("space")
    z = lax.axis_index("band")
    core = lax.rem(s, 2)
    f32 = jnp.float32
    bf16 = jnp.bfloat16

    def lanes_of(c, extra=0, size=CHUNK):
        return pl.ds(pl.multiple_of(c * CHUNK + extra, 128), size)

    def load(c, half, part):
        lanes = lanes_of(c, half * FOLD)
        return pltpu.make_async_copy(
            orb_hbm.at[part, :, :, lanes],
            field.at[:, pl.ds(4 * part, 4), lanes],
            load_sem.at[c, half, part],
        )

    barrier = pltpu.get_barrier_semaphore()

    def greet(sem, axis, me, size, offset):
        for step in (offset, size - offset):
            pl.semaphore_signal(
                sem, inc=1, device_id={axis: lax.rem(me + step, size)}, device_id_type=MESH
            )

    for offset in (1, 2):
        greet(barrier, "space", s, SPACE, offset)
        greet(barrier, "band", z, BAND, offset)
    for c in range(CHUNKS):
        for half in range(2):
            for part in range(2):
                load(c, half, part).start()
    owner = (OWNERS * z + BAND - 1) // BAND
    owner_index = jnp.minimum(owner, OWNERS - 1)
    is_owner = (BAND * owner) // OWNERS == z
    pot_copy = pltpu.make_async_copy(pot_hbm, pot_ref, table_sem.at[4])
    pot_copy.start()
    occ_copy = pltpu.make_async_copy(occ_hbm, occ_ref, table_sem.at[5])
    occ_copy.start()
    tables = [
        pltpu.make_async_copy(src, dst, table_sem.at[i])
        for i, (src, dst) in enumerate(
            [
                (band_hbm, band_ref),
                (forward_hbm, forward_ref),
                (inverse_hbm, inverse_ref),
                (green_hbm.at[owner_index], green_ref),
            ]
        )
    ]
    tables[0].start()

    outward = 2 * core - 1
    owns = (own0, own1)
    rims = (rim0, rim1)

    def halo(phase, kind, c):
        own, rim = owns[phase], rims[phase]
        inside = lanes_of(c, BLOCK)
        outside = lanes_of(c)
        if kind == 0:
            src = own.at[:, :, inside]
            dst = rim.at[1 - core, pl.ds(core, 3), :, outside]
            step = outward
        elif kind == 1:
            src = own.at[:, :, inside]
            dst = rim.at[core, pl.ds(1 - core, 3), :, outside]
            step = -outward
        elif kind == 2:
            src = own.at[2 * (1 - core), :, inside]
            dst = rim.at[core, 3 * core, :, outside]
            step = -2 * outward
        else:
            src = rim.at[core, 3 * (1 - core), :, outside]
            dst = rim.at[core, 3 * core, :, outside]
            step = -outward
        return pltpu.make_async_remote_copy(
            src_ref=src,
            dst_ref=dst,
            send_sem=halo_send.at[phase, kind, c],
            recv_sem=halo_recv.at[phase, kind, c],
            device_id={"space": lax.rem(s + step + SPACE, SPACE)},
            device_id_type=MESH,
        )

    def fold_edges(source, own):
        zeros = jnp.zeros((FIELDS, BLOCK), f32)
        for p in range(PLANES):
            own[p, :, 0:BLOCK] = jnp.concatenate(
                [zeros, source[p, :, FOLD - BLOCK : FOLD]], axis=0
            ).astype(bf16)
            own[p, :, PADDED - BLOCK : PADDED] = jnp.concatenate(
                [source[p, :, FOLD : FOLD + BLOCK], zeros], axis=0
            ).astype(bf16)

    def pack(c, carry):
        for half in range(2):
            for part in range(2):
                load(c, half, part).wait()
        for p in range(PLANES):
            own0[p, :, lanes_of(c, BLOCK)] = jnp.concatenate(
                [field[p, :, lanes_of(c)], field[p, :, lanes_of(c, FOLD)]], axis=0
            ).astype(bf16)
        return carry

    lax.fori_loop(0, CHUNKS, pack, 0)
    pl.semaphore_wait(barrier, 8)

    def ship(c, carry):
        for kind in range(3):
            halo(0, kind, c).start()
        return carry

    lax.fori_loop(0, CHUNKS, ship, 0)
    greet(hand.at[0], "band", z, BAND, 2)
    greet(hand.at[1], "space", s, SPACE, 2)
    fold_edges(field, own0)
    for copy in tables[1:]:
        copy.start()
    tables[0].wait()

    pot_copy.wait()
    occ_copy.wait()
    edge = (s - core) // 2
    before = jnp.where(edge >= 1, 1.0, 0.0).astype(f32)
    after = jnp.where(edge <= SPACE // 2 - 2, 1.0, 0.0).astype(f32)
    outer_weight = jnp.where(core == 0, before, after)
    inner_weight = jnp.where(core == 0, after, before)

    gain = stencil_coeffs[1] / (2.0 * energy_scale)
    level = -(energy_shift + 1.5 * stencil_coeffs[0]) / energy_scale

    def mirrored(position, last):
        return position + core * (last - 2 * position)

    def receive(phase, c):
        own = owns[phase]
        windows = [
            own[mirrored(q, 2), :, lanes_of(c, b * BLOCK, WINDOW)]
            for q in range(PLANES)
            for b in range(PER_CHUNK)
        ]
        flat[lax.rem(c, 2)] = jnp.dot(
            jnp.concatenate(windows, axis=0), band_ref[...], preferred_element_type=f32
        )
        halo(phase, 0, c).wait_recv()
        halo(phase, 3, c).start()

    def stencil(phase, source, c, finish):
        own, rim = owns[phase], rims[phase]
        slot = lax.rem(c, 2)
        for kind in (1, 2, 3):
            halo(phase, kind, c).wait_recv()
        for b in range(PER_CHUNK):
            outside = lanes_of(c, b * BLOCK, BLOCK)
            inside = lanes_of(c, (b + 1) * BLOCK, BLOCK)
            outer = [
                rim[core, mirrored(at, 3), :, outside].astype(f32) * outer_weight
                for at in range(4)
            ]
            middle = [own[mirrored(at, 2), :, inside].astype(f32) for at in range(PLANES)]
            inner = [rim[1 - core, mirrored(at, 3), :, outside].astype(f32) for at in range(4)]
            stack = outer + middle + inner[:3] + [inner[3] * inner_weight]
            for q in range(PLANES):
                p = mirrored(q, 2)
                across = stack[q + 5] + stack[q + 3]
                for offset in range(2, 5):
                    across = across + scaled_coeffs[offset] * (
                        stack[q + 4 + offset] + stack[q + 4 - offset]
                    )
                at = 16 * (q * PER_CHUNK + b)
                across = gain * (across + flat[slot, at : at + 16])
                for half in range(2):
                    lanes = lanes_of(c, half * FOLD + b * BLOCK, BLOCK)
                    centre = source[p, :, lanes]
                    factor = pot_ref[pl.ds(p, 1), lanes] * (1.0 / energy_scale) + level
                    value = centre * factor - across[8 * half : 8 * half + 8]
                    finish(p, b, half, lanes, centre, value)

    def sweep(phase, use):
        receive(phase, 0)

        def step(c, carry):
            @pl.when(c < CHUNKS)
            def _():
                receive(phase, c)

            use(c - 1)
            return carry

        lax.fori_loop(1, CHUNKS + 1, step, 0)


    def first_chunk(c):
        values = []

        def finish(p, b, half, lanes, centre, value):
            first[p, :, lanes] = value
            values.append(value)
            if half == 1:
                own1[p, :, lanes_of(c, (b + 1) * BLOCK, BLOCK)] = jnp.concatenate(
                    values[-2:], axis=0
                ).astype(bf16)

        stencil(0, field, c, finish)
        for kind in range(3):
            halo(1, kind, c).start()

    sweep(0, first_chunk)
    pl.semaphore_wait(hand.at[0], 2)
    greet(hand.at[2], "band", z, BAND, 4)
    pl.semaphore_wait(hand.at[1], 2)
    greet(hand.at[3], "space", s, SPACE, 4)
    fold_edges(first, own1)

    rows = lax.broadcasted_iota(jnp.int32, (FIELDS, BLOCK), 0)
    weight = jnp.zeros((FIELDS, BLOCK), f32)
    for o in range(4):
        weight = jnp.where(lax.rem(rows, 4) == o, occ_ref[o] * (1.0 / ORBITALS), weight)
    sign = jnp.where(rows < 4, 2.0 * bessel_terms[1], -2.0 * bessel_terms[1]).astype(f32)

    def stores(c, half, part):
        lanes = lanes_of(c, half * FOLD)
        return pltpu.make_async_copy(
            prop.at[:, pl.ds(4 * part, 4), lanes],
            prop_hbm.at[part, :, :, lanes],
            store_sem.at[c, half, part],
        )

    def second_chunk(c):
        def finish(p, b, half, lanes, centre, value):
            swapped = jnp.concatenate([centre[4:8], centre[0:4]], axis=0)
            result = (
                (bessel_terms[0] + 2.0 * bessel_terms[2]) * field[p, :, lanes]
                + sign * swapped
                - (4.0 * bessel_terms[2]) * value
            )
            prop[p, :, lanes] = result
            share = jnp.sum(weight * (result * result), axis=0, keepdims=True)
            lines[pl.ds(p * BLOCKS + half * (BLOCKS // 2) + c * PER_CHUNK + b, 1), :] = share

        stencil(1, first, c, finish)
        for half in range(2):
            for part in range(2):
                stores(c, half, part).start()

    sweep(1, second_chunk)
    pl.semaphore_wait(hand.at[2], 2)
    pl.semaphore_wait(hand.at[3], 2)
    greet(hand.at[4], "space", s, SPACE, 8)

    for copy in tables[1:]:
        copy.wait()
    turned = exact_dot(lines[...], forward_ref[0:BLOCK, :])
    stacked = jnp.concatenate(
        [
            jnp.concatenate(
                [
                    turned[p * BLOCKS : (p + 1) * BLOCKS, r * 128 : (r + 1) * 128]
                    for r in range(4)
                ],
                axis=0,
            )
            for p in range(PLANES)
        ],
        axis=1,
    )
    spectral = exact_dot(forward_ref[BLOCK : BLOCK + NY, 0:NY], stacked)
    lane = lax.broadcasted_iota(jnp.int32, (1, 128), 1)
    for p in range(PLANES):
        full = spectral[:, p * 128 : (p + 1) * 128]
        head = jnp.where(lane < 64, full[0:48], pltpu.roll(full[48:96], 64, 1))
        rest = pltpu.roll(full[0:24], 64, 1)
        for quarter in range(1, 4):
            piece = full[24 * quarter : 24 * quarter + 24]
            turn = (32 * quarter + 64) % 128
            piece = pltpu.roll(piece, turn, 1) if turn else piece
            rest = jnp.where(lane >= 32 * quarter, piece, rest)
        for o in range(6):
            modes[o, p] = head[8 * o : 8 * o + 8]
        for o in range(3):
            modes[6 + o, p] = rest[8 * o : 8 * o + 8]


    def share_copy(o, source):
        return pltpu.make_async_remote_copy(
            src_ref=modes.at[o],
            dst_ref=shares.at[source],
            send_sem=share_send.at[o],
            recv_sem=share_recv.at[source],
            device_id={"band": (BAND * o) // OWNERS},
            device_id_type=MESH,
        )

    def by_distance(i, middle):
        return middle + jnp.where(lax.rem(i, 2) == 0, i // 2, -(i + 1) // 2)

    def out_share(i, carry):
        target = lax.rem(z + by_distance(i, BAND // 2), BAND)
        o = (OWNERS * target + BAND - 1) // BAND

        @pl.when((BAND * o) // OWNERS == target)
        def _():
            share_copy(o, z).start()

        return carry

    lax.fori_loop(0, BAND - 1, out_share, 0)
    pl.semaphore_wait(hand.at[4], 2)

    def layer_copy(k):
        return pltpu.make_async_remote_copy(
            src_ref=summed,
            dst_ref=layer.at[SPACE // 2 - k],
            send_sem=layer_send.at[k],
            recv_sem=layer_recv.at[SPACE // 2 - k],
            device_id={"space": lax.rem(s + 2 * k, SPACE)},
            device_id_type=MESH,
        )

    partner_copy = pltpu.make_async_remote_copy(
        src_ref=partial,
        dst_ref=crossed,
        send_sem=cross_sem.at[0],
        recv_sem=cross_sem.at[1],
        device_id={"space": s - outward},
        device_id_type=MESH,
    )

    def band_copy(src, dst, send, recv, k):
        return pltpu.make_async_remote_copy(
            src_ref=src,
            dst_ref=dst.at[owner_index],
            send_sem=send.at[k],
            recv_sem=recv.at[owner_index],
            device_id={"band": lax.rem(z + k, BAND)},
            device_id_type=MESH,
        )

    def keep(values, ref, gathered_ref):
        upper = jnp.concatenate([values[0], values[1]], axis=0).astype(bf16)
        lower = jnp.concatenate([values[2], jnp.zeros((8, 128), f32)], axis=0).astype(bf16)
        for out in (ref, gathered_ref.at[owner_index]):
            out[0] = upper
            out[1] = lower

    @pl.when(is_owner)
    def _():
        def collect(k, total):
            source = lax.rem(z + k, BAND)
            pltpu.make_async_copy(modes.at[0], shares.at[source], share_recv.at[source]).wait()
            return total + shares[source]

        total = lax.fori_loop(1, BAND, collect, modes[owner_index])
        summed[...] = total
        layer[0] = total

        def out_layer(i, carry):
            layer_copy(by_distance(i, SPACE // 4)).start()
            return carry

        lax.fori_loop(0, SPACE // 2 - 1, out_layer, 0)
        keep([total[p] for p in range(PLANES)], dens_own, dens_modes)

        def out_dens(i, carry):
            band_copy(dens_own, dens_modes, dens_send, dens_recv, by_distance(i, BAND // 2)).start()
            return carry

        lax.fori_loop(0, BAND - 1, out_dens, 0)

        def apply(r, total):
            out = list(total)
            for q in range(PLANES):
                value = layer[r, q]
                for p in range(PLANES):
                    at = 6 * r + q - p + 5
                    out[p] = out[p] + green_ref[at] * value
                    out[PLANES + p] = out[PLANES + p] + green_ref[at + 3 * outward] * value
            return tuple(out)

        def collect_layer(r, total):
            pltpu.make_async_copy(summed, layer.at[r], layer_recv.at[r]).wait()
            return apply(r, total)

        zero = jnp.zeros((8, 128), f32)
        result = lax.fori_loop(1, SPACE // 2, collect_layer, apply(0, (zero,) * (2 * PLANES)))
        for p in range(PLANES):
            partial[p] = result[PLANES + p]
        partner_copy.start()
        partner_copy.wait()
        keep([result[p] + crossed[p] for p in range(PLANES)], hart_own, hart_modes)

        def out_hart(i, carry):
            band_copy(hart_own, hart_modes, hart_send, hart_recv, by_distance(i, BAND // 2)).start()
            return carry

        lax.fori_loop(0, BAND - 1, out_hart, 0)

    def back(spec_ref):
        halves = [[spec_ref[o, i].astype(f32) for i in range(2)] for o in range(OWNERS)]
        pieces = []
        for p in range(PLANES):
            at = 8 * (p % 2)
            blocks = [halves[o][p // 2][at : at + 8] for o in range(OWNERS)]
            head = jnp.concatenate(blocks[:6], axis=0)
            rest = jnp.concatenate(blocks[6:], axis=0)
            upper = jnp.concatenate([head, pltpu.roll(head, 64, 1)], axis=0)
            lower = jnp.concatenate(
                [pltpu.roll(rest, 64, 1), pltpu.roll(rest, 32, 1), rest, pltpu.roll(rest, 96, 1)],
                axis=0,
            )
            pieces.append(jnp.where(lane < 64, upper, jnp.where(lane < NZ, lower, 0.0)))
        spread = jnp.concatenate(pieces, axis=1).astype(bf16)
        rows_y = jnp.dot(
            inverse_ref[1024 : 1024 + NY, 0 : 2 * NY],
            jnp.concatenate([spread, spread], axis=0),
            preferred_element_type=f32,
        )
        wide = jnp.concatenate(
            [
                jnp.concatenate(
                    [
                        rows_y[r * BLOCKS : (r + 1) * BLOCKS, p * 128 : (p + 1) * 128]
                        for r in range(4)
                    ],
                    axis=1,
                )
                for p in range(PLANES)
            ],
            axis=0,
        )
        high = wide.astype(bf16)
        low = (wide - high.astype(f32)).astype(bf16)
        z_high = inverse_ref[0:512]
        return (
            jnp.dot(high, z_high, preferred_element_type=f32)
            + jnp.dot(low, z_high, preferred_element_type=f32)
            + jnp.dot(high, inverse_ref[512:1024], preferred_element_type=f32)
        )

    def put(out_ref, values):
        for p in range(PLANES):
            for block in range(BLOCKS):
                at = p * BLOCKS + block
                out_ref[p : p + 1, block * BLOCK : (block + 1) * BLOCK] = values[at : at + 1]

    def gathered(dst, recv):
        for o in range(OWNERS):
            @pl.when((BAND * o) // OWNERS != z)
            def _():
                pltpu.make_async_copy(dens_own, dst.at[o], recv.at[o]).wait()

    dens_copy = pltpu.make_async_copy(dens_ref, dens_hbm, table_sem.at[6])
    hart_copy = pltpu.make_async_copy(hart_ref, hart_hbm, table_sem.at[7])
    gathered(dens_modes, dens_recv)
    put(dens_ref, back(dens_modes))
    dens_copy.start()

    @pl.when(is_owner)
    def _():
        def drain_layer(k, carry):
            layer_copy(k).wait_send()
            return carry

        lax.fori_loop(1, SPACE // 2, drain_layer, 0)

        def drain_dens(k, carry):
            band_copy(dens_own, dens_modes, dens_send, dens_recv, k).wait_send()
            return carry

        lax.fori_loop(1, BAND, drain_dens, 0)

    for o in range(OWNERS):
        @pl.when((BAND * o) // OWNERS != z)
        def _():
            share_copy(o, z).wait_send()

    def drain(c, carry):
        for phase in range(2):
            for kind in range(4):
                halo(phase, kind, c).wait_send()
        for half in range(2):
            for part in range(2):
                stores(c, half, part).wait()
        return carry

    lax.fori_loop(0, CHUNKS, drain, 0)
    dens_copy.wait()
    gathered(hart_modes, hart_recv)
    put(hart_ref, back(hart_modes))
    hart_copy.start()

    @pl.when(is_owner)
    def _():
        def drain_hart(k, carry):
            band_copy(hart_own, hart_modes, hart_send, hart_recv, k).wait_send()
            return carry

        lax.fori_loop(1, BAND, drain_hart, 0)

    hart_copy.wait()


def settle(prop_in, dens_in, hart_in, prop_out, dens_out, hart_out, prop_at, dens_at, hart_at, in_sem, out_sem):
    routes = [(dens_in, dens_at, dens_out), (hart_in, hart_at, hart_out)]
    for part in range(2):
        for p in range(PLANES):
            routes.append((prop_in.at[part, p], prop_at.at[part, p], prop_out.at[part, p]))
    inward = [pltpu.make_async_copy(r[0], r[1], in_sem.at[i]) for i, r in enumerate(routes)]
    outward = [pltpu.make_async_copy(r[1], r[2], out_sem.at[i]) for i, r in enumerate(routes)]
    for copy in inward:
        copy.start()
    for i in range(len(routes)):
        inward[i].wait()
        outward[i].start()
    for copy in outward:
        copy.wait()


def per_device(orbitals, potential, occupations):
    f32 = jnp.float32
    bf16 = jnp.bfloat16
    forward, inverse, green = transform_tables()
    vmem = pltpu.VMEM
    dma = pltpu.SemaphoreType.DMA
    anywhere = pl.BlockSpec(memory_space=pl.ANY)
    raw = pl.pallas_call(
        body,
        out_shape=(
            jax.ShapeDtypeStruct((2, PLANES, 4, CELLS), f32),
            jax.ShapeDtypeStruct((PLANES, CELLS), f32),
            jax.ShapeDtypeStruct((PLANES, CELLS), f32),
        ),
        in_specs=[anywhere] * 7,
        out_specs=(anywhere, anywhere, anywhere),
        scratch_shapes=[
            vmem((PLANES, CELLS), f32),
            pltpu.SMEM((4,), f32),
            vmem((PLANES, CELLS), f32),
            vmem((PLANES, CELLS), f32),
            vmem((2, 16 * PLANES * PER_CHUNK, BLOCK), f32),
            vmem((PLANES, FIELDS, CELLS), f32),
            vmem((PLANES, FIELDS, CELLS), f32),
            vmem((PLANES, FIELDS, CELLS), f32),
            vmem((PLANES, 16, PADDED), bf16),
            vmem((PLANES, 16, PADDED), bf16),
            vmem((2, 4, 16, FOLD), bf16),
            vmem((2, 4, 16, FOLD), bf16),
            vmem((PLANES * BLOCKS, BLOCK), f32),
            vmem((WINDOW, BLOCK), bf16),
            vmem((BLOCK + NY, 512), f32),
            vmem((1024 + NY, BLOCK), bf16),
            vmem((NX + 5, 8, 128), f32),
            vmem((OWNERS, PLANES, 8, 128), f32),
            vmem((BAND, PLANES, 8, 128), f32),
            vmem((PLANES, 8, 128), f32),
            vmem((SPACE // 2, PLANES, 8, 128), f32),
            vmem((PLANES, 8, 128), f32),
            vmem((PLANES, 8, 128), f32),
            vmem((2, 16, 128), bf16),
            vmem((2, 16, 128), bf16),
            vmem((OWNERS, 2, 16, 128), bf16),
            vmem((OWNERS, 2, 16, 128), bf16),
            dma((CHUNKS, 2, 2)),
            dma((8,)),
            dma((CHUNKS, 2, 2)),
            dma((2, 4, CHUNKS)),
            dma((2, 4, CHUNKS)),
            pltpu.SemaphoreType.REGULAR((5,)),
            dma((OWNERS,)),
            dma((BAND,)),
            dma((SPACE // 2,)),
            dma((SPACE // 2,)),
            dma((2,)),
            dma((BAND,)),
            dma((OWNERS,)),
            dma((BAND,)),
            dma((OWNERS,)),
        ],
        compiler_params=pltpu.CompilerParams(
            collective_id=0, has_side_effects=True, vmem_limit_bytes=62 * 2**20
        ),
    )(
        jnp.transpose(orbitals, (0, 2, 1, 3)),
        potential,
        occupations,
        jnp.asarray(band_matrix()),
        jnp.asarray(forward),
        jnp.asarray(inverse),
        jnp.asarray(green),
    )
    prop, dens, hart = pl.pallas_call(
        settle,
        out_shape=[jax.ShapeDtypeStruct(r.shape, r.dtype) for r in raw],
        in_specs=[anywhere] * 3,
        out_specs=[anywhere] * 3,
        scratch_shapes=[vmem(r.shape, r.dtype) for r in raw] + [dma((8,)), dma((8,))],
        compiler_params=pltpu.CompilerParams(vmem_limit_bytes=62 * 2**20),
    )(*raw)
    return jnp.transpose(prop, (0, 2, 1, 3)), dens, hart


def solution(mesh):
    in_specs = (P(None, "band", "space", None), P("space", None), P("band"))
    out_specs = (P(None, "band", "space", None), P("space", None), P("space", None))
    return jax.shard_map(
        per_device, mesh=mesh, in_specs=in_specs, out_specs=out_specs, check_vma=False
    )
```

```python
import functools
import math

import jax
import jax.numpy as jnp
import ml_dtypes
import numpy as np
from jax import lax
from jax.experimental import pallas as pl
from jax.experimental.pallas import tpu as pltpu
from jax.sharding import PartitionSpec as P

NX = 96
NY = 96
NZ = 96

stencil_coeffs = (-205.0 / 72.0, 8.0 / 5.0, -1.0 / 5.0, 8.0 / 315.0, -1.0 / 560.0)
energy_shift = 6.0
energy_scale = 8.0
bessel_terms = (0.7651976865579666, 0.44005058574493355, 0.11490348493190049)
scaled_coeffs = tuple(c / stencil_coeffs[1] for c in stencil_coeffs)

MESH = pl.DeviceIdType.MESH
PLANES = 3
FIELDS = 8
CELLS = NY * NZ
FOLD = CELLS // 2
BLOCK = 4 * NZ
BLOCKS = CELLS // BLOCK
CHUNKS = 4
CHUNK = FOLD // CHUNKS
PER_CHUNK = CHUNK // BLOCK
WINDOW = 3 * BLOCK
PADDED = FOLD + 2 * BLOCK
SPACE = 32
BAND = 16
OWNERS = 9
ORBITALS = 64


def band_matrix():
    table = np.zeros((WINDOW, BLOCK))
    for cell in range(BLOCK):
        z = cell % NZ
        for offset in range(1, 5):
            c = scaled_coeffs[offset]
            table[BLOCK + cell + offset * NZ, cell] += c
            table[BLOCK + cell - offset * NZ, cell] += c
            if z + offset < NZ:
                table[BLOCK + cell + offset, cell] += c
            if z - offset >= 0:
                table[BLOCK + cell - offset, cell] += c
    return table.astype(ml_dtypes.bfloat16)


def real_basis(length):
    cells = np.arange(length)
    rows = [np.full(length, 1.0 / math.sqrt(length))]
    waves = [0]
    for k in range(1, length // 2):
        phase = 2.0 * math.pi * ((k * cells) % length) / length
        rows.append(math.sqrt(2.0 / length) * np.cos(phase))
        rows.append(math.sqrt(2.0 / length) * np.sin(phase))
        waves += [k, k]
    rows.append(np.where(cells % 2 == 0, 1.0, -1.0) / math.sqrt(length))
    waves.append(length // 2)
    return np.stack(rows), (2.0 * math.pi / length * np.array(waves)) ** 2


def split(table):
    high = table.astype(ml_dtypes.bfloat16)
    low = (table - high.astype(np.float64)).astype(ml_dtypes.bfloat16)
    return high, low


def transform_tables():
    basis, squares = real_basis(NY)
    order = np.array([4 * block + r for r in range(4) for block in range(BLOCKS)])
    forward_y = basis[:, order]
    lanes = np.arange(128)
    forward_z = np.zeros((4, NZ, 4, 128))
    for r in range(4):
        forward_z[r, :, r, :NZ] = basis.T
    forward_z = forward_z.reshape(BLOCK, 512)
    row = np.arange(72)[:, None]
    mode_y = np.where(row < 48, row + 48 * (lanes >= 64), row - 48 + 24 * (lanes // 32))
    mode_z = np.where(row < 48, lanes % 64, 64 + lanes % 32)
    across = squares[mode_y] + squares[mode_z]
    cells = np.arange(NX)
    signed = np.where(cells < NX // 2, cells, cells - NX)
    along = (2.0 * math.pi / NX * signed) ** 2
    total = along[:, None, None] + across
    kernel = np.where(total > 0, 4.0 * math.pi / np.where(total > 0, total, 1.0), 0.0)
    green = np.real(np.fft.ifft(kernel, axis=0))
    green = green[(np.arange(NX + 5) - 5) % NX]
    green = green.reshape(NX + 5, OWNERS, 8, 128).transpose(1, 0, 2, 3)
    f32 = np.float32
    forward = np.concatenate([forward_z, np.pad(forward_y, ((0, 0), (0, 512 - NY)))])
    f_high, f_middle = split(forward)
    f_low = split(forward - f_high.astype(np.float64))[1]
    y_high, y_low = split(forward_y.T)
    z_high, z_low = split(forward_z.T)
    return (
        np.stack([f_high, f_middle, f_low]),
        np.concatenate([z_high, z_low, np.pad(np.concatenate([y_high, y_low], axis=1), ((0, 0), (0, BLOCK - 2 * NY)))]),
        green.astype(f32),
    )


def thirds(values):
    f32, bf16 = jnp.float32, jnp.bfloat16
    high = values.astype(bf16)
    rest = values - high.astype(f32)
    middle = rest.astype(bf16)
    return high, middle, (rest - middle.astype(f32)).astype(bf16)


def exact_dot(a, b):
    def one(i, j):
        return jnp.dot(a[i], b[j], preferred_element_type=jnp.float32)

    small = (one(0, 2) + one(2, 0)) + one(1, 1)
    return (small + (one(0, 1) + one(1, 0))) + one(0, 0)


def body(
    orb_hbm, pot_hbm, occ_hbm, band_hbm, forward_hbm, inverse_hbm, green_hbm,
    prop_hbm, dens_hbm, hart_hbm,
    pot_ref, occ_ref, dens_ref, hart_ref, flat, field, first, prop, own0, own1, rim0, rim1, lines,
    band_ref, forward_ref, inverse_ref, green_ref,
    modes, shares, summed, layer, partial, crossed, dens_own, hart_own, dens_modes, hart_modes,
    load_sem, table_sem, store_sem, halo_send, halo_recv, hand,
    share_send, share_recv, layer_send, layer_recv, cross_sem,
    dens_send, dens_recv, hart_send, hart_recv,
):
    s = lax.axis_index("space")
    z = lax.axis_index("band")
    core = lax.rem(s, 2)
    f32 = jnp.float32
    bf16 = jnp.bfloat16

    def lanes_of(c, extra=0, size=CHUNK):
        return pl.ds(pl.multiple_of(c * CHUNK + extra, 128), size)

    def load(c, half, part):
        lanes = lanes_of(c, half * FOLD)
        return pltpu.make_async_copy(
            orb_hbm.at[part, :, :, lanes],
            field.at[:, pl.ds(4 * part, 4), lanes],
            load_sem.at[c, half, part],
        )

    barrier = pltpu.get_barrier_semaphore()

    def greet(sem, axis, me, size, offset):
        for step in (offset, size - offset):
            pl.semaphore_signal(
                sem, inc=1, device_id={axis: lax.rem(me + step, size)}, device_id_type=MESH
            )

    for offset in (1, 2):
        greet(barrier, "space", s, SPACE, offset)
        greet(barrier, "band", z, BAND, offset)
    for c in range(CHUNKS):
        for half in range(2):
            for part in range(2):
                load(c, half, part).start()
    owner = (OWNERS * z + BAND - 1) // BAND
    owner_index = jnp.minimum(owner, OWNERS - 1)
    is_owner = (BAND * owner) // OWNERS == z
    pot_copy = pltpu.make_async_copy(pot_hbm, pot_ref, table_sem.at[4])
    pot_copy.start()
    occ_copy = pltpu.make_async_copy(occ_hbm, occ_ref, table_sem.at[5])
    occ_copy.start()
    tables = [
        pltpu.make_async_copy(src, dst, table_sem.at[i])
        for i, (src, dst) in enumerate(
            [
                (band_hbm, band_ref),
                (forward_hbm, forward_ref),
                (inverse_hbm, inverse_ref),
                (green_hbm.at[owner_index], green_ref),
            ]
        )
    ]
    tables[0].start()

    outward = 2 * core - 1
    owns = (own0, own1)
    rims = (rim0, rim1)

    def halo(phase, kind, c):
        own, rim = owns[phase], rims[phase]
        inside = lanes_of(c, BLOCK)
        outside = lanes_of(c)
        if kind == 0:
            src = own.at[:, :, inside]
            dst = rim.at[1 - core, pl.ds(core, 3), :, outside]
            step = outward
        elif kind == 1:
            src = own.at[:, :, inside]
            dst = rim.at[core, pl.ds(1 - core, 3), :, outside]
            step = -outward
        elif kind == 2:
            src = own.at[2 * (1 - core), :, inside]
            dst = rim.at[core, 3 * core, :, outside]
            step = -2 * outward
        else:
            src = rim.at[core, 3 * (1 - core), :, outside]
            dst = rim.at[core, 3 * core, :, outside]
            step = -outward
        return pltpu.make_async_remote_copy(
            src_ref=src,
            dst_ref=dst,
            send_sem=halo_send.at[phase, kind, c],
            recv_sem=halo_recv.at[phase, kind, c],
            device_id={"space": lax.rem(s + step + SPACE, SPACE)},
            device_id_type=MESH,
        )

    def fold_edges(source, own):
        zeros = jnp.zeros((FIELDS, BLOCK), f32)
        for p in range(PLANES):
            own[p, :, 0:BLOCK] = jnp.concatenate(
                [zeros, source[p, :, FOLD - BLOCK : FOLD]], axis=0
            ).astype(bf16)
            own[p, :, PADDED - BLOCK : PADDED] = jnp.concatenate(
                [source[p, :, FOLD : FOLD + BLOCK], zeros], axis=0
            ).astype(bf16)

    def pack(c, carry):
        for half in range(2):
            for part in range(2):
                load(c, half, part).wait()
        for p in range(PLANES):
            own0[p, :, lanes_of(c, BLOCK)] = jnp.concatenate(
                [field[p, :, lanes_of(c)], field[p, :, lanes_of(c, FOLD)]], axis=0
            ).astype(bf16)
        return carry

    lax.fori_loop(0, CHUNKS, pack, 0)
    pl.semaphore_wait(barrier, 8)

    def ship(c, carry):
        for kind in range(3):
            halo(0, kind, c).start()
        return carry

    lax.fori_loop(0, CHUNKS, ship, 0)
    greet(hand.at[0], "band", z, BAND, 2)
    greet(hand.at[1], "space", s, SPACE, 2)
    fold_edges(field, own0)
    for copy in tables[1:]:
        copy.start()
    tables[0].wait()

    pot_copy.wait()
    occ_copy.wait()
    edge = (s - core) // 2
    before = jnp.where(edge >= 1, 1.0, 0.0).astype(f32)
    after = jnp.where(edge <= SPACE // 2 - 2, 1.0, 0.0).astype(f32)
    outer_weight = jnp.where(core == 0, before, after)
    inner_weight = jnp.where(core == 0, after, before)

    gain = stencil_coeffs[1] / (2.0 * energy_scale)
    level = -(energy_shift + 1.5 * stencil_coeffs[0]) / energy_scale

    def mirrored(position, last):
        return position + core * (last - 2 * position)

    def receive(phase, c):
        own = owns[phase]
        windows = [
            own[mirrored(q, 2), :, lanes_of(c, b * BLOCK, WINDOW)]
            for q in range(PLANES)
            for b in range(PER_CHUNK)
        ]
        flat[lax.rem(c, 2)] = jnp.dot(
            jnp.concatenate(windows, axis=0), band_ref[...], preferred_element_type=f32
        )
        halo(phase, 0, c).wait_recv()
        halo(phase, 3, c).start()

    def stencil(phase, source, c, finish):
        own, rim = owns[phase], rims[phase]
        slot = lax.rem(c, 2)
        for kind in (1, 2, 3):
            halo(phase, kind, c).wait_recv()
        for b in range(PER_CHUNK):
            outside = lanes_of(c, b * BLOCK, BLOCK)
            inside = lanes_of(c, (b + 1) * BLOCK, BLOCK)
            outer = [
                rim[core, mirrored(at, 3), :, outside].astype(f32) * outer_weight
                for at in range(4)
            ]
            middle = [own[mirrored(at, 2), :, inside].astype(f32) for at in range(PLANES)]
            inner = [rim[1 - core, mirrored(at, 3), :, outside].astype(f32) for at in range(4)]
            stack = outer + middle + inner[:3] + [inner[3] * inner_weight]
            for q in range(PLANES):
                p = mirrored(q, 2)
                across = stack[q + 5] + stack[q + 3]
                for offset in range(2, 5):
                    across = across + scaled_coeffs[offset] * (
                        stack[q + 4 + offset] + stack[q + 4 - offset]
                    )
                at = 16 * (q * PER_CHUNK + b)
                across = gain * (across + flat[slot, at : at + 16])
                for half in range(2):
                    lanes = lanes_of(c, half * FOLD + b * BLOCK, BLOCK)
                    centre = source[p, :, lanes]
                    factor = pot_ref[pl.ds(p, 1), lanes] * (1.0 / energy_scale) + level
                    value = centre * factor - across[8 * half : 8 * half + 8]
                    finish(p, b, half, lanes, centre, value)

    def sweep(phase, use):
        receive(phase, 0)

        def step(c, carry):
            @pl.when(c < CHUNKS)
            def _():
                receive(phase, c)

            use(c - 1)
            return carry

        lax.fori_loop(1, CHUNKS + 1, step, 0)


    def first_chunk(c):
        values = []

        def finish(p, b, half, lanes, centre, value):
            first[p, :, lanes] = value
            values.append(value)
            if half == 1:
                own1[p, :, lanes_of(c, (b + 1) * BLOCK, BLOCK)] = jnp.concatenate(
                    values[-2:], axis=0
                ).astype(bf16)

        stencil(0, field, c, finish)
        for kind in range(3):
            halo(1, kind, c).start()

    sweep(0, first_chunk)
    pl.semaphore_wait(hand.at[0], 2)
    greet(hand.at[2], "band", z, BAND, 4)
    pl.semaphore_wait(hand.at[1], 2)
    greet(hand.at[3], "space", s, SPACE, 4)
    fold_edges(first, own1)

    rows = lax.broadcasted_iota(jnp.int32, (FIELDS, BLOCK), 0)
    weight = jnp.zeros((FIELDS, BLOCK), f32)
    for o in range(4):
        weight = jnp.where(lax.rem(rows, 4) == o, occ_ref[o] * (1.0 / ORBITALS), weight)
    sign = jnp.where(rows < 4, 2.0 * bessel_terms[1], -2.0 * bessel_terms[1]).astype(f32)

    def stores(c, half, part):
        lanes = lanes_of(c, half * FOLD)
        return pltpu.make_async_copy(
            prop.at[:, pl.ds(4 * part, 4), lanes],
            prop_hbm.at[part, :, :, lanes],
            store_sem.at[c, half, part],
        )

    def second_chunk(c):
        def finish(p, b, half, lanes, centre, value):
            swapped = jnp.concatenate([centre[4:8], centre[0:4]], axis=0)
            result = (
                (bessel_terms[0] + 2.0 * bessel_terms[2]) * field[p, :, lanes]
                + sign * swapped
                - (4.0 * bessel_terms[2]) * value
            )
            prop[p, :, lanes] = result
            share = jnp.sum(weight * (result * result), axis=0, keepdims=True)
            lines[pl.ds(p * BLOCKS + half * (BLOCKS // 2) + c * PER_CHUNK + b, 1), :] = share

        stencil(1, first, c, finish)
        for half in range(2):
            for part in range(2):
                stores(c, half, part).start()

    sweep(1, second_chunk)
    pl.semaphore_wait(hand.at[2], 2)
    pl.semaphore_wait(hand.at[3], 2)
    greet(hand.at[4], "space", s, SPACE, 8)

    for copy in tables[1:]:
        copy.wait()
    turned = exact_dot(thirds(lines[...]), [forward_ref[i, 0:BLOCK, :] for i in range(3)])
    stacked = jnp.concatenate(
        [
            jnp.concatenate(
                [
                    turned[p * BLOCKS : (p + 1) * BLOCKS, r * 128 : (r + 1) * 128]
                    for r in range(4)
                ],
                axis=0,
            )
            for p in range(PLANES)
        ],
        axis=1,
    )
    spectral = exact_dot(
        [forward_ref[i, BLOCK : BLOCK + NY, 0:NY] for i in range(3)], thirds(stacked)
    )
    lane = lax.broadcasted_iota(jnp.int32, (1, 128), 1)
    for p in range(PLANES):
        full = spectral[:, p * 128 : (p + 1) * 128]
        head = jnp.where(lane < 64, full[0:48], pltpu.roll(full[48:96], 64, 1))
        rest = pltpu.roll(full[0:24], 64, 1)
        for quarter in range(1, 4):
            piece = full[24 * quarter : 24 * quarter + 24]
            turn = (32 * quarter + 64) % 128
            piece = pltpu.roll(piece, turn, 1) if turn else piece
            rest = jnp.where(lane >= 32 * quarter, piece, rest)
        for o in range(6):
            modes[o, p] = head[8 * o : 8 * o + 8]
        for o in range(3):
            modes[6 + o, p] = rest[8 * o : 8 * o + 8]


    def share_copy(o, source):
        return pltpu.make_async_remote_copy(
            src_ref=modes.at[o],
            dst_ref=shares.at[source],
            send_sem=share_send.at[o],
            recv_sem=share_recv.at[source],
            device_id={"band": (BAND * o) // OWNERS},
            device_id_type=MESH,
        )

    def by_distance(i, middle):
        return middle + jnp.where(lax.rem(i, 2) == 0, i // 2, -(i + 1) // 2)

    def out_share(i, carry):
        target = lax.rem(z + by_distance(i, BAND // 2), BAND)
        o = (OWNERS * target + BAND - 1) // BAND

        @pl.when((BAND * o) // OWNERS == target)
        def _():
            share_copy(o, z).start()

        return carry

    lax.fori_loop(0, BAND - 1, out_share, 0)
    pl.semaphore_wait(hand.at[4], 2)

    def layer_copy(k):
        return pltpu.make_async_remote_copy(
            src_ref=summed,
            dst_ref=layer.at[SPACE // 2 - k],
            send_sem=layer_send.at[k],
            recv_sem=layer_recv.at[SPACE // 2 - k],
            device_id={"space": lax.rem(s + 2 * k, SPACE)},
            device_id_type=MESH,
        )

    partner_copy = pltpu.make_async_remote_copy(
        src_ref=partial,
        dst_ref=crossed,
        send_sem=cross_sem.at[0],
        recv_sem=cross_sem.at[1],
        device_id={"space": s - outward},
        device_id_type=MESH,
    )

    def band_copy(src, dst, send, recv, k):
        return pltpu.make_async_remote_copy(
            src_ref=src,
            dst_ref=dst.at[owner_index],
            send_sem=send.at[k],
            recv_sem=recv.at[owner_index],
            device_id={"band": lax.rem(z + k, BAND)},
            device_id_type=MESH,
        )

    def keep(values, ref, gathered_ref):
        upper = jnp.concatenate([values[0], values[1]], axis=0).astype(bf16)
        lower = jnp.concatenate([values[2], jnp.zeros((8, 128), f32)], axis=0).astype(bf16)
        for out in (ref, gathered_ref.at[owner_index]):
            out[0] = upper
            out[1] = lower

    @pl.when(is_owner)
    def _():
        def collect(k, total):
            source = lax.rem(z + k, BAND)
            pltpu.make_async_copy(modes.at[0], shares.at[source], share_recv.at[source]).wait()
            return total + shares[source]

        total = lax.fori_loop(1, BAND, collect, modes[owner_index])
        summed[...] = total
        layer[0] = total

        def out_layer(i, carry):
            layer_copy(by_distance(i, SPACE // 4)).start()
            return carry

        lax.fori_loop(0, SPACE // 2 - 1, out_layer, 0)
        keep([total[p] for p in range(PLANES)], dens_own, dens_modes)

        def out_dens(i, carry):
            band_copy(dens_own, dens_modes, dens_send, dens_recv, by_distance(i, BAND // 2)).start()
            return carry

        lax.fori_loop(0, BAND - 1, out_dens, 0)

        def apply(r, total):
            out = list(total)
            for q in range(PLANES):
                value = layer[r, q]
                for p in range(PLANES):
                    at = 6 * r + q - p + 5
                    out[p] = out[p] + green_ref[at] * value
                    out[PLANES + p] = out[PLANES + p] + green_ref[at + 3 * outward] * value
            return tuple(out)

        def collect_layer(r, total):
            pltpu.make_async_copy(summed, layer.at[r], layer_recv.at[r]).wait()
            return apply(r, total)

        zero = jnp.zeros((8, 128), f32)
        result = lax.fori_loop(1, SPACE // 2, collect_layer, apply(0, (zero,) * (2 * PLANES)))
        for p in range(PLANES):
            partial[p] = result[PLANES + p]
        partner_copy.start()
        partner_copy.wait()
        keep([result[p] + crossed[p] for p in range(PLANES)], hart_own, hart_modes)

        def out_hart(i, carry):
            band_copy(hart_own, hart_modes, hart_send, hart_recv, by_distance(i, BAND // 2)).start()
            return carry

        lax.fori_loop(0, BAND - 1, out_hart, 0)

    def back(spec_ref):
        halves = [[spec_ref[o, i].astype(f32) for i in range(2)] for o in range(OWNERS)]
        pieces = []
        for p in range(PLANES):
            at = 8 * (p % 2)
            blocks = [halves[o][p // 2][at : at + 8] for o in range(OWNERS)]
            head = jnp.concatenate(blocks[:6], axis=0)
            rest = jnp.concatenate(blocks[6:], axis=0)
            upper = jnp.concatenate([head, pltpu.roll(head, 64, 1)], axis=0)
            lower = jnp.concatenate(
                [pltpu.roll(rest, 64, 1), pltpu.roll(rest, 32, 1), rest, pltpu.roll(rest, 96, 1)],
                axis=0,
            )
            pieces.append(jnp.where(lane < 64, upper, jnp.where(lane < NZ, lower, 0.0)))
        spread = jnp.concatenate(pieces, axis=1).astype(bf16)
        rows_y = jnp.dot(
            inverse_ref[1024 : 1024 + NY, 0 : 2 * NY],
            jnp.concatenate([spread, spread], axis=0),
            preferred_element_type=f32,
        )
        wide = jnp.concatenate(
            [
                jnp.concatenate(
                    [
                        rows_y[r * BLOCKS : (r + 1) * BLOCKS, p * 128 : (p + 1) * 128]
                        for r in range(4)
                    ],
                    axis=1,
                )
                for p in range(PLANES)
            ],
            axis=0,
        )
        high = wide.astype(bf16)
        low = (wide - high.astype(f32)).astype(bf16)
        z_high = inverse_ref[0:512]
        return (
            jnp.dot(high, z_high, preferred_element_type=f32)
            + jnp.dot(low, z_high, preferred_element_type=f32)
            + jnp.dot(high, inverse_ref[512:1024], preferred_element_type=f32)
        )

    def put(out_ref, values):
        for p in range(PLANES):
            for block in range(BLOCKS):
                at = p * BLOCKS + block
                out_ref[p : p + 1, block * BLOCK : (block + 1) * BLOCK] = values[at : at + 1]

    def gathered(dst, recv):
        for o in range(OWNERS):
            @pl.when((BAND * o) // OWNERS != z)
            def _():
                pltpu.make_async_copy(dens_own, dst.at[o], recv.at[o]).wait()

    dens_copy = pltpu.make_async_copy(dens_ref, dens_hbm, table_sem.at[6])
    hart_copy = pltpu.make_async_copy(hart_ref, hart_hbm, table_sem.at[7])
    gathered(dens_modes, dens_recv)
    put(dens_ref, back(dens_modes))
    dens_copy.start()

    @pl.when(is_owner)
    def _():
        def drain_layer(k, carry):
            layer_copy(k).wait_send()
            return carry

        lax.fori_loop(1, SPACE // 2, drain_layer, 0)

        def drain_dens(k, carry):
            band_copy(dens_own, dens_modes, dens_send, dens_recv, k).wait_send()
            return carry

        lax.fori_loop(1, BAND, drain_dens, 0)

    for o in range(OWNERS):
        @pl.when((BAND * o) // OWNERS != z)
        def _():
            share_copy(o, z).wait_send()

    def drain(c, carry):
        for phase in range(2):
            for kind in range(4):
                halo(phase, kind, c).wait_send()
        for half in range(2):
            for part in range(2):
                stores(c, half, part).wait()
        return carry

    lax.fori_loop(0, CHUNKS, drain, 0)
    dens_copy.wait()
    gathered(hart_modes, hart_recv)
    put(hart_ref, back(hart_modes))
    hart_copy.start()

    @pl.when(is_owner)
    def _():
        def drain_hart(k, carry):
            band_copy(hart_own, hart_modes, hart_send, hart_recv, k).wait_send()
            return carry

        lax.fori_loop(1, BAND, drain_hart, 0)

    hart_copy.wait()


def settle(prop_in, dens_in, hart_in, prop_out, dens_out, hart_out, prop_at, dens_at, hart_at, in_sem, out_sem):
    routes = [(dens_in, dens_at, dens_out), (hart_in, hart_at, hart_out)]
    for part in range(2):
        for p in range(PLANES):
            routes.append((prop_in.at[part, p], prop_at.at[part, p], prop_out.at[part, p]))
    inward = [pltpu.make_async_copy(r[0], r[1], in_sem.at[i]) for i, r in enumerate(routes)]
    outward = [pltpu.make_async_copy(r[1], r[2], out_sem.at[i]) for i, r in enumerate(routes)]
    for copy in inward:
        copy.start()
    for i in range(len(routes)):
        inward[i].wait()
        outward[i].start()
    for copy in outward:
        copy.wait()


def per_device(orbitals, potential, occupations):
    f32 = jnp.float32
    bf16 = jnp.bfloat16
    forward, inverse, green = transform_tables()
    vmem = pltpu.VMEM
    dma = pltpu.SemaphoreType.DMA
    anywhere = pl.BlockSpec(memory_space=pl.ANY)
    raw = pl.pallas_call(
        body,
        out_shape=(
            jax.ShapeDtypeStruct((2, PLANES, 4, CELLS), f32),
            jax.ShapeDtypeStruct((PLANES, CELLS), f32),
            jax.ShapeDtypeStruct((PLANES, CELLS), f32),
        ),
        in_specs=[anywhere] * 7,
        out_specs=(anywhere, anywhere, anywhere),
        scratch_shapes=[
            vmem((PLANES, CELLS), f32),
            pltpu.SMEM((4,), f32),
            vmem((PLANES, CELLS), f32),
            vmem((PLANES, CELLS), f32),
            vmem((2, 16 * PLANES * PER_CHUNK, BLOCK), f32),
            vmem((PLANES, FIELDS, CELLS), f32),
            vmem((PLANES, FIELDS, CELLS), f32),
            vmem((PLANES, FIELDS, CELLS), f32),
            vmem((PLANES, 16, PADDED), bf16),
            vmem((PLANES, 16, PADDED), bf16),
            vmem((2, 4, 16, FOLD), bf16),
            vmem((2, 4, 16, FOLD), bf16),
            vmem((PLANES * BLOCKS, BLOCK), f32),
            vmem((WINDOW, BLOCK), bf16),
            vmem((3, BLOCK + NY, 512), bf16),
            vmem((1024 + NY, BLOCK), bf16),
            vmem((NX + 5, 8, 128), f32),
            vmem((OWNERS, PLANES, 8, 128), f32),
            vmem((BAND, PLANES, 8, 128), f32),
            vmem((PLANES, 8, 128), f32),
            vmem((SPACE // 2, PLANES, 8, 128), f32),
            vmem((PLANES, 8, 128), f32),
            vmem((PLANES, 8, 128), f32),
            vmem((2, 16, 128), bf16),
            vmem((2, 16, 128), bf16),
            vmem((OWNERS, 2, 16, 128), bf16),
            vmem((OWNERS, 2, 16, 128), bf16),
            dma((CHUNKS, 2, 2)),
            dma((8,)),
            dma((CHUNKS, 2, 2)),
            dma((2, 4, CHUNKS)),
            dma((2, 4, CHUNKS)),
            pltpu.SemaphoreType.REGULAR((5,)),
            dma((OWNERS,)),
            dma((BAND,)),
            dma((SPACE // 2,)),
            dma((SPACE // 2,)),
            dma((2,)),
            dma((BAND,)),
            dma((OWNERS,)),
            dma((BAND,)),
            dma((OWNERS,)),
        ],
        compiler_params=pltpu.CompilerParams(
            collective_id=0, has_side_effects=True, vmem_limit_bytes=62 * 2**20
        ),
    )(
        jnp.transpose(orbitals, (0, 2, 1, 3)),
        potential,
        occupations,
        jnp.asarray(band_matrix()),
        jnp.asarray(forward),
        jnp.asarray(inverse),
        jnp.asarray(green),
    )
    prop, dens, hart = pl.pallas_call(
        settle,
        out_shape=[jax.ShapeDtypeStruct(r.shape, r.dtype) for r in raw],
        in_specs=[anywhere] * 3,
        out_specs=[anywhere] * 3,
        scratch_shapes=[vmem(r.shape, r.dtype) for r in raw] + [dma((8,)), dma((8,))],
        compiler_params=pltpu.CompilerParams(vmem_limit_bytes=62 * 2**20),
    )(*raw)
    return jnp.transpose(prop, (0, 2, 1, 3)), dens, hart


def solution(mesh):
    in_specs = (P(None, "band", "space", None), P("space", None), P("band"))
    out_specs = (P(None, "band", "space", None), P("space", None), P("space", None))
    return jax.shard_map(
        per_device, mesh=mesh, in_specs=in_specs, out_specs=out_specs, check_vma=False
    )
```

```python
import functools
import math

import jax
import jax.numpy as jnp
import ml_dtypes
import numpy as np
from jax import lax
from jax.experimental import pallas as pl
from jax.experimental.pallas import tpu as pltpu
from jax.sharding import PartitionSpec as P

NX = 96
NY = 96
NZ = 96

stencil_coeffs = (-205.0 / 72.0, 8.0 / 5.0, -1.0 / 5.0, 8.0 / 315.0, -1.0 / 560.0)
energy_shift = 6.0
energy_scale = 8.0
bessel_terms = (0.7651976865579666, 0.44005058574493355, 0.11490348493190049)
scaled_coeffs = tuple(c / stencil_coeffs[1] for c in stencil_coeffs)

MESH = pl.DeviceIdType.MESH
PLANES = 3
FIELDS = 8
CELLS = NY * NZ
FOLD = CELLS // 2
BLOCK = 4 * NZ
BLOCKS = CELLS // BLOCK
CHUNKS = 4
CHUNK = FOLD // CHUNKS
PER_CHUNK = CHUNK // BLOCK
WINDOW = 3 * BLOCK
PADDED = FOLD + 2 * BLOCK
SPACE = 32
BAND = 16
OWNERS = 9
ORBITALS = 64


def band_matrix():
    table = np.zeros((WINDOW, BLOCK))
    for cell in range(BLOCK):
        z = cell % NZ
        for offset in range(1, 5):
            c = scaled_coeffs[offset]
            table[BLOCK + cell + offset * NZ, cell] += c
            table[BLOCK + cell - offset * NZ, cell] += c
            if z + offset < NZ:
                table[BLOCK + cell + offset, cell] += c
            if z - offset >= 0:
                table[BLOCK + cell - offset, cell] += c
    return table.astype(ml_dtypes.bfloat16)


def real_basis(length):
    cells = np.arange(length)
    rows = [np.full(length, 1.0 / math.sqrt(length))]
    waves = [0]
    for k in range(1, length // 2):
        phase = 2.0 * math.pi * ((k * cells) % length) / length
        rows.append(math.sqrt(2.0 / length) * np.cos(phase))
        rows.append(math.sqrt(2.0 / length) * np.sin(phase))
        waves += [k, k]
    rows.append(np.where(cells % 2 == 0, 1.0, -1.0) / math.sqrt(length))
    waves.append(length // 2)
    return np.stack(rows), (2.0 * math.pi / length * np.array(waves)) ** 2


def split(table):
    high = table.astype(ml_dtypes.bfloat16)
    low = (table - high.astype(np.float64)).astype(ml_dtypes.bfloat16)
    return high, low


def transform_tables():
    basis, squares = real_basis(NY)
    order = np.array([4 * block + r for r in range(4) for block in range(BLOCKS)])
    forward_y = basis[:, order]
    lanes = np.arange(128)
    forward_z = np.zeros((4, NZ, 4, 128))
    for r in range(4):
        forward_z[r, :, r, :NZ] = basis.T
    forward_z = forward_z.reshape(BLOCK, 512)
    row = np.arange(72)[:, None]
    mode_y = np.where(row < 48, row + 48 * (lanes >= 64), row - 48 + 24 * (lanes // 32))
    mode_z = np.where(row < 48, lanes % 64, 64 + lanes % 32)
    across = squares[mode_y] + squares[mode_z]
    cells = np.arange(NX)
    signed = np.where(cells < NX // 2, cells, cells - NX)
    along = (2.0 * math.pi / NX * signed) ** 2
    total = along[:, None, None] + across
    kernel = np.where(total > 0, 4.0 * math.pi / np.where(total > 0, total, 1.0), 0.0)
    green = np.real(np.fft.ifft(kernel, axis=0))
    green = green[(np.arange(NX + 5) - 5) % NX]
    green = green.reshape(NX + 5, OWNERS, 8, 128).transpose(1, 0, 2, 3)
    f32 = np.float32
    y_high, y_low = split(forward_y.T)
    z_high, z_low = split(forward_z.T)
    return (
        np.concatenate([forward_z, np.pad(forward_y, ((0, 0), (0, 512 - NY)))]).astype(f32),
        np.concatenate([z_high, z_low, np.pad(np.concatenate([y_high, y_low], axis=1), ((0, 0), (0, BLOCK - 2 * NY)))]),
        green.astype(f32),
    )


def exact_dot(a, b):
    return lax.dot_general(
        a,
        b,
        (((1,), (0,)), ((), ())),
        precision=lax.Precision.HIGHEST,
        preferred_element_type=jnp.float32,
    )


def body(
    orb_hbm, pot_hbm, occ_hbm, band_hbm, forward_hbm, inverse_hbm, green_hbm,
    prop_hbm, dens_hbm, hart_hbm,
    pot_ref, occ_ref, dens_ref, hart_ref, flat, field, first, prop, own0, own1, rim0, rim1, lines,
    band_ref, forward_ref, inverse_ref, green_ref,
    modes, shares, summed, layer, partial, crossed, dens_own, hart_own, dens_modes, hart_modes,
    load_sem, table_sem, store_sem, halo_send, halo_recv, hand,
    share_send, share_recv, layer_send, layer_recv, cross_sem,
    dens_send, dens_recv, hart_send, hart_recv,
):
    s = lax.axis_index("space")
    z = lax.axis_index("band")
    core = lax.rem(s, 2)
    f32 = jnp.float32
    bf16 = jnp.bfloat16

    def lanes_of(c, extra=0, size=CHUNK):
        return pl.ds(pl.multiple_of(c * CHUNK + extra, 128), size)

    def load(c, half, part):
        lanes = lanes_of(c, half * FOLD)
        return pltpu.make_async_copy(
            orb_hbm.at[part, :, :, lanes],
            field.at[:, pl.ds(4 * part, 4), lanes],
            load_sem.at[c, half, part],
        )

    barrier = pltpu.get_barrier_semaphore()

    def greet(sem, axis, me, size, offset):
        for step in (offset, size - offset):
            pl.semaphore_signal(
                sem, inc=1, device_id={axis: lax.rem(me + step, size)}, device_id_type=MESH
            )

    for offset in (1, 2):
        greet(barrier, "space", s, SPACE, offset)
        greet(barrier, "band", z, BAND, offset)
    for c in range(CHUNKS):
        for half in range(2):
            for part in range(2):
                load(c, half, part).start()
    owner = (OWNERS * z + BAND - 1) // BAND
    owner_index = jnp.minimum(owner, OWNERS - 1)
    is_owner = (BAND * owner) // OWNERS == z
    pot_copy = pltpu.make_async_copy(pot_hbm, pot_ref, table_sem.at[4])
    pot_copy.start()
    occ_copy = pltpu.make_async_copy(occ_hbm, occ_ref, table_sem.at[5])
    occ_copy.start()
    tables = [
        pltpu.make_async_copy(src, dst, table_sem.at[i])
        for i, (src, dst) in enumerate(
            [
                (band_hbm, band_ref),
                (forward_hbm, forward_ref),
                (inverse_hbm, inverse_ref),
                (green_hbm.at[owner_index], green_ref),
            ]
        )
    ]
    tables[0].start()

    outward = 2 * core - 1
    owns = (own0, own1)
    rims = (rim0, rim1)

    def halo(phase, kind, c):
        own, rim = owns[phase], rims[phase]
        inside = lanes_of(c, BLOCK)
        outside = lanes_of(c)
        if kind == 0:
            src = own.at[:, :, inside]
            dst = rim.at[1 - core, pl.ds(core, 3), :, outside]
            step = outward
        elif kind == 1:
            src = own.at[:, :, inside]
            dst = rim.at[core, pl.ds(1 - core, 3), :, outside]
            step = -outward
        elif kind == 2:
            src = own.at[2 * (1 - core), :, inside]
            dst = rim.at[core, 3 * core, :, outside]
            step = -2 * outward
        else:
            src = rim.at[core, 3 * (1 - core), :, outside]
            dst = rim.at[core, 3 * core, :, outside]
            step = -outward
        return pltpu.make_async_remote_copy(
            src_ref=src,
            dst_ref=dst,
            send_sem=halo_send.at[phase, kind, c],
            recv_sem=halo_recv.at[phase, kind, c],
            device_id={"space": lax.rem(s + step + SPACE, SPACE)},
            device_id_type=MESH,
        )

    def fold_edges(source, own):
        zeros = jnp.zeros((FIELDS, BLOCK), f32)
        for p in range(PLANES):
            own[p, :, 0:BLOCK] = jnp.concatenate(
                [zeros, source[p, :, FOLD - BLOCK : FOLD]], axis=0
            ).astype(bf16)
            own[p, :, PADDED - BLOCK : PADDED] = jnp.concatenate(
                [source[p, :, FOLD : FOLD + BLOCK], zeros], axis=0
            ).astype(bf16)

    def pack(c, carry):
        for half in range(2):
            for part in range(2):
                load(c, half, part).wait()
        for p in range(PLANES):
            own0[p, :, lanes_of(c, BLOCK)] = jnp.concatenate(
                [field[p, :, lanes_of(c)], field[p, :, lanes_of(c, FOLD)]], axis=0
            ).astype(bf16)
        return carry

    lax.fori_loop(0, CHUNKS, pack, 0)
    pl.semaphore_wait(barrier, 8)

    def ship(c, carry):
        for kind in (0, 2, 1):
            halo(0, kind, c).start()
        return carry

    lax.fori_loop(0, CHUNKS, ship, 0)
    greet(hand.at[0], "band", z, BAND, 2)
    greet(hand.at[1], "space", s, SPACE, 2)
    fold_edges(field, own0)
    for copy in tables[1:]:
        copy.start()
    tables[0].wait()

    pot_copy.wait()
    occ_copy.wait()
    edge = (s - core) // 2
    before = jnp.where(edge >= 1, 1.0, 0.0).astype(f32)
    after = jnp.where(edge <= SPACE // 2 - 2, 1.0, 0.0).astype(f32)
    outer_weight = jnp.where(core == 0, before, after)
    inner_weight = jnp.where(core == 0, after, before)

    gain = stencil_coeffs[1] / (2.0 * energy_scale)
    level = -(energy_shift + 1.5 * stencil_coeffs[0]) / energy_scale

    def mirrored(position, last):
        return position + core * (last - 2 * position)

    def receive(phase, c):
        own = owns[phase]
        windows = [
            own[mirrored(q, 2), :, lanes_of(c, b * BLOCK, WINDOW)]
            for q in range(PLANES)
            for b in range(PER_CHUNK)
        ]
        flat[lax.rem(c, 2)] = jnp.dot(
            jnp.concatenate(windows, axis=0), band_ref[...], preferred_element_type=f32
        )
        halo(phase, 0, c).wait_recv()
        halo(phase, 3, c).start()

    def stencil(phase, source, c, finish):
        own, rim = owns[phase], rims[phase]
        slot = lax.rem(c, 2)
        for kind in (1, 2, 3):
            halo(phase, kind, c).wait_recv()
        for b in range(PER_CHUNK):
            outside = lanes_of(c, b * BLOCK, BLOCK)
            inside = lanes_of(c, (b + 1) * BLOCK, BLOCK)
            outer = [
                rim[core, mirrored(at, 3), :, outside].astype(f32) * outer_weight
                for at in range(4)
            ]
            middle = [own[mirrored(at, 2), :, inside].astype(f32) for at in range(PLANES)]
            inner = [rim[1 - core, mirrored(at, 3), :, outside].astype(f32) for at in range(4)]
            stack = outer + middle + inner[:3] + [inner[3] * inner_weight]
            for q in range(PLANES):
                p = mirrored(q, 2)
                across = stack[q + 5] + stack[q + 3]
                for offset in range(2, 5):
                    across = across + scaled_coeffs[offset] * (
                        stack[q + 4 + offset] + stack[q + 4 - offset]
                    )
                at = 16 * (q * PER_CHUNK + b)
                across = gain * (across + flat[slot, at : at + 16])
                for half in range(2):
                    lanes = lanes_of(c, half * FOLD + b * BLOCK, BLOCK)
                    centre = source[p, :, lanes]
                    factor = pot_ref[pl.ds(p, 1), lanes] * (1.0 / energy_scale) + level
                    value = centre * factor - across[8 * half : 8 * half + 8]
                    finish(p, b, half, lanes, centre, value)

    def sweep(phase, use):
        receive(phase, 0)

        def step(c, carry):
            @pl.when(c < CHUNKS)
            def _():
                receive(phase, c)

            use(c - 1)
            return carry

        lax.fori_loop(1, CHUNKS + 1, step, 0)


    def first_chunk(c):
        values = []

        def finish(p, b, half, lanes, centre, value):
            first[p, :, lanes] = value
            values.append(value)
            if half == 1:
                own1[p, :, lanes_of(c, (b + 1) * BLOCK, BLOCK)] = jnp.concatenate(
                    values[-2:], axis=0
                ).astype(bf16)

        stencil(0, field, c, finish)
        for kind in (0, 2, 1):
            halo(1, kind, c).start()

    sweep(0, first_chunk)
    pl.semaphore_wait(hand.at[0], 2)
    greet(hand.at[2], "band", z, BAND, 4)
    pl.semaphore_wait(hand.at[1], 2)
    greet(hand.at[3], "space", s, SPACE, 4)
    fold_edges(first, own1)

    rows = lax.broadcasted_iota(jnp.int32, (FIELDS, BLOCK), 0)
    weight = jnp.zeros((FIELDS, BLOCK), f32)
    for o in range(4):
        weight = jnp.where(lax.rem(rows, 4) == o, occ_ref[o] * (1.0 / ORBITALS), weight)
    sign = jnp.where(rows < 4, 2.0 * bessel_terms[1], -2.0 * bessel_terms[1]).astype(f32)

    def stores(c, half, part):
        lanes = lanes_of(c, half * FOLD)
        return pltpu.make_async_copy(
            prop.at[:, pl.ds(4 * part, 4), lanes],
            prop_hbm.at[part, :, :, lanes],
            store_sem.at[c, half, part],
        )

    def second_chunk(c):
        def finish(p, b, half, lanes, centre, value):
            swapped = jnp.concatenate([centre[4:8], centre[0:4]], axis=0)
            result = (
                (bessel_terms[0] + 2.0 * bessel_terms[2]) * field[p, :, lanes]
                + sign * swapped
                - (4.0 * bessel_terms[2]) * value
            )
            prop[p, :, lanes] = result
            share = jnp.sum(weight * (result * result), axis=0, keepdims=True)
            lines[pl.ds(p * BLOCKS + half * (BLOCKS // 2) + c * PER_CHUNK + b, 1), :] = share

        stencil(1, first, c, finish)
        for half in range(2):
            for part in range(2):
                stores(c, half, part).start()

    sweep(1, second_chunk)
    pl.semaphore_wait(hand.at[2], 2)
    pl.semaphore_wait(hand.at[3], 2)
    greet(hand.at[4], "space", s, SPACE, 8)

    for copy in tables[1:]:
        copy.wait()
    turned = exact_dot(lines[...], forward_ref[0:BLOCK, :])
    stacked = jnp.concatenate(
        [
            jnp.concatenate(
                [
                    turned[p * BLOCKS : (p + 1) * BLOCKS, r * 128 : (r + 1) * 128]
                    for r in range(4)
                ],
                axis=0,
            )
            for p in range(PLANES)
        ],
        axis=1,
    )
    spectral = exact_dot(forward_ref[BLOCK : BLOCK + NY, 0:NY], stacked)
    lane = lax.broadcasted_iota(jnp.int32, (1, 128), 1)
    for p in range(PLANES):
        full = spectral[:, p * 128 : (p + 1) * 128]
        head = jnp.where(lane < 64, full[0:48], pltpu.roll(full[48:96], 64, 1))
        rest = pltpu.roll(full[0:24], 64, 1)
        for quarter in range(1, 4):
            piece = full[24 * quarter : 24 * quarter + 24]
            turn = (32 * quarter + 64) % 128
            piece = pltpu.roll(piece, turn, 1) if turn else piece
            rest = jnp.where(lane >= 32 * quarter, piece, rest)
        for o in range(6):
            modes[o, p] = head[8 * o : 8 * o + 8]
        for o in range(3):
            modes[6 + o, p] = rest[8 * o : 8 * o + 8]


    def share_copy(o, source):
        return pltpu.make_async_remote_copy(
            src_ref=modes.at[o],
            dst_ref=shares.at[source],
            send_sem=share_send.at[o],
            recv_sem=share_recv.at[source],
            device_id={"band": (BAND * o) // OWNERS},
            device_id_type=MESH,
        )

    def by_distance(i, middle):
        return middle + jnp.where(lax.rem(i, 2) == 0, i // 2, -(i + 1) // 2)

    def out_share(i, carry):
        target = lax.rem(z + by_distance(i, BAND // 2), BAND)
        o = (OWNERS * target + BAND - 1) // BAND

        @pl.when((BAND * o) // OWNERS == target)
        def _():
            share_copy(o, z).start()

        return carry

    lax.fori_loop(0, BAND - 1, out_share, 0)
    pl.semaphore_wait(hand.at[4], 2)

    def layer_copy(k):
        return pltpu.make_async_remote_copy(
            src_ref=summed,
            dst_ref=layer.at[SPACE // 2 - k],
            send_sem=layer_send.at[k],
            recv_sem=layer_recv.at[SPACE // 2 - k],
            device_id={"space": lax.rem(s + 2 * k, SPACE)},
            device_id_type=MESH,
        )

    partner_copy = pltpu.make_async_remote_copy(
        src_ref=partial,
        dst_ref=crossed,
        send_sem=cross_sem.at[0],
        recv_sem=cross_sem.at[1],
        device_id={"space": s - outward},
        device_id_type=MESH,
    )

    def band_copy(src, dst, send, recv, k):
        return pltpu.make_async_remote_copy(
            src_ref=src,
            dst_ref=dst.at[owner_index],
            send_sem=send.at[k],
            recv_sem=recv.at[owner_index],
            device_id={"band": lax.rem(z + k, BAND)},
            device_id_type=MESH,
        )

    def keep(values, ref, gathered_ref):
        upper = jnp.concatenate([values[0], values[1]], axis=0).astype(bf16)
        lower = jnp.concatenate([values[2], jnp.zeros((8, 128), f32)], axis=0).astype(bf16)
        for out in (ref, gathered_ref.at[owner_index]):
            out[0] = upper
            out[1] = lower

    @pl.when(is_owner)
    def _():
        def collect(k, total):
            source = lax.rem(z + k, BAND)
            pltpu.make_async_copy(modes.at[0], shares.at[source], share_recv.at[source]).wait()
            return total + shares[source]

        total = lax.fori_loop(1, BAND, collect, modes[owner_index])
        summed[...] = total
        layer[0] = total

        def out_layer(i, carry):
            layer_copy(by_distance(i, SPACE // 4)).start()
            return carry

        lax.fori_loop(0, SPACE // 2 - 1, out_layer, 0)
        keep([total[p] for p in range(PLANES)], dens_own, dens_modes)

        def out_dens(i, carry):
            band_copy(dens_own, dens_modes, dens_send, dens_recv, by_distance(i, BAND // 2)).start()
            return carry

        lax.fori_loop(0, BAND - 1, out_dens, 0)

        def apply(r, total):
            out = list(total)
            for q in range(PLANES):
                value = layer[r, q]
                for p in range(PLANES):
                    at = 6 * r + q - p + 5
                    out[p] = out[p] + green_ref[at] * value
                    out[PLANES + p] = out[PLANES + p] + green_ref[at + 3 * outward] * value
            return tuple(out)

        def collect_layer(r, total):
            pltpu.make_async_copy(summed, layer.at[r], layer_recv.at[r]).wait()
            return apply(r, total)

        zero = jnp.zeros((8, 128), f32)
        result = lax.fori_loop(1, SPACE // 2, collect_layer, apply(0, (zero,) * (2 * PLANES)))
        for p in range(PLANES):
            partial[p] = result[PLANES + p]
        partner_copy.start()
        partner_copy.wait()
        keep([result[p] + crossed[p] for p in range(PLANES)], hart_own, hart_modes)

        def out_hart(i, carry):
            band_copy(hart_own, hart_modes, hart_send, hart_recv, by_distance(i, BAND // 2)).start()
            return carry

        lax.fori_loop(0, BAND - 1, out_hart, 0)

    def back(spec_ref):
        halves = [[spec_ref[o, i].astype(f32) for i in range(2)] for o in range(OWNERS)]
        pieces = []
        for p in range(PLANES):
            at = 8 * (p % 2)
            blocks = [halves[o][p // 2][at : at + 8] for o in range(OWNERS)]
            head = jnp.concatenate(blocks[:6], axis=0)
            rest = jnp.concatenate(blocks[6:], axis=0)
            upper = jnp.concatenate([head, pltpu.roll(head, 64, 1)], axis=0)
            lower = jnp.concatenate(
                [pltpu.roll(rest, 64, 1), pltpu.roll(rest, 32, 1), rest, pltpu.roll(rest, 96, 1)],
                axis=0,
            )
            pieces.append(jnp.where(lane < 64, upper, jnp.where(lane < NZ, lower, 0.0)))
        spread = jnp.concatenate(pieces, axis=1).astype(bf16)
        rows_y = jnp.dot(
            inverse_ref[1024 : 1024 + NY, 0 : 2 * NY],
            jnp.concatenate([spread, spread], axis=0),
            preferred_element_type=f32,
        )
        wide = jnp.concatenate(
            [
                jnp.concatenate(
                    [
                        rows_y[r * BLOCKS : (r + 1) * BLOCKS, p * 128 : (p + 1) * 128]
                        for r in range(4)
                    ],
                    axis=1,
                )
                for p in range(PLANES)
            ],
            axis=0,
        )
        high = wide.astype(bf16)
        low = (wide - high.astype(f32)).astype(bf16)
        z_high = inverse_ref[0:512]
        return (
            jnp.dot(high, z_high, preferred_element_type=f32)
            + jnp.dot(low, z_high, preferred_element_type=f32)
            + jnp.dot(high, inverse_ref[512:1024], preferred_element_type=f32)
        )

    def put(out_ref, values):
        for p in range(PLANES):
            for block in range(BLOCKS):
                at = p * BLOCKS + block
                out_ref[p : p + 1, block * BLOCK : (block + 1) * BLOCK] = values[at : at + 1]

    def gathered(dst, recv):
        for o in range(OWNERS):
            @pl.when((BAND * o) // OWNERS != z)
            def _():
                pltpu.make_async_copy(dens_own, dst.at[o], recv.at[o]).wait()

    dens_copy = pltpu.make_async_copy(dens_ref, dens_hbm, table_sem.at[6])
    hart_copy = pltpu.make_async_copy(hart_ref, hart_hbm, table_sem.at[7])
    gathered(dens_modes, dens_recv)
    put(dens_ref, back(dens_modes))
    dens_copy.start()

    @pl.when(is_owner)
    def _():
        def drain_layer(k, carry):
            layer_copy(k).wait_send()
            return carry

        lax.fori_loop(1, SPACE // 2, drain_layer, 0)

        def drain_dens(k, carry):
            band_copy(dens_own, dens_modes, dens_send, dens_recv, k).wait_send()
            return carry

        lax.fori_loop(1, BAND, drain_dens, 0)

    for o in range(OWNERS):
        @pl.when((BAND * o) // OWNERS != z)
        def _():
            share_copy(o, z).wait_send()

    def drain(c, carry):
        for phase in range(2):
            for kind in range(4):
                halo(phase, kind, c).wait_send()
        for half in range(2):
            for part in range(2):
                stores(c, half, part).wait()
        return carry

    lax.fori_loop(0, CHUNKS, drain, 0)
    dens_copy.wait()
    gathered(hart_modes, hart_recv)
    put(hart_ref, back(hart_modes))
    hart_copy.start()

    @pl.when(is_owner)
    def _():
        def drain_hart(k, carry):
            band_copy(hart_own, hart_modes, hart_send, hart_recv, k).wait_send()
            return carry

        lax.fori_loop(1, BAND, drain_hart, 0)

    hart_copy.wait()


def settle(prop_in, dens_in, hart_in, prop_out, dens_out, hart_out, prop_at, dens_at, hart_at, in_sem, out_sem):
    routes = [(dens_in, dens_at, dens_out), (hart_in, hart_at, hart_out)]
    for part in range(2):
        for p in range(PLANES):
            routes.append((prop_in.at[part, p], prop_at.at[part, p], prop_out.at[part, p]))
    inward = [pltpu.make_async_copy(r[0], r[1], in_sem.at[i]) for i, r in enumerate(routes)]
    outward = [pltpu.make_async_copy(r[1], r[2], out_sem.at[i]) for i, r in enumerate(routes)]
    for copy in inward:
        copy.start()
    for i in range(len(routes)):
        inward[i].wait()
        outward[i].start()
    for copy in outward:
        copy.wait()


def per_device(orbitals, potential, occupations):
    f32 = jnp.float32
    bf16 = jnp.bfloat16
    forward, inverse, green = transform_tables()
    vmem = pltpu.VMEM
    dma = pltpu.SemaphoreType.DMA
    anywhere = pl.BlockSpec(memory_space=pl.ANY)
    raw = pl.pallas_call(
        body,
        out_shape=(
            jax.ShapeDtypeStruct((2, PLANES, 4, CELLS), f32),
            jax.ShapeDtypeStruct((PLANES, CELLS), f32),
            jax.ShapeDtypeStruct((PLANES, CELLS), f32),
        ),
        in_specs=[anywhere] * 7,
        out_specs=(anywhere, anywhere, anywhere),
        scratch_shapes=[
            vmem((PLANES, CELLS), f32),
            pltpu.SMEM((4,), f32),
            vmem((PLANES, CELLS), f32),
            vmem((PLANES, CELLS), f32),
            vmem((2, 16 * PLANES * PER_CHUNK, BLOCK), f32),
            vmem((PLANES, FIELDS, CELLS), f32),
            vmem((PLANES, FIELDS, CELLS), f32),
            vmem((PLANES, FIELDS, CELLS), f32),
            vmem((PLANES, 16, PADDED), bf16),
            vmem((PLANES, 16, PADDED), bf16),
            vmem((2, 4, 16, FOLD), bf16),
            vmem((2, 4, 16, FOLD), bf16),
            vmem((PLANES * BLOCKS, BLOCK), f32),
            vmem((WINDOW, BLOCK), bf16),
            vmem((BLOCK + NY, 512), f32),
            vmem((1024 + NY, BLOCK), bf16),
            vmem((NX + 5, 8, 128), f32),
            vmem((OWNERS, PLANES, 8, 128), f32),
            vmem((BAND, PLANES, 8, 128), f32),
            vmem((PLANES, 8, 128), f32),
            vmem((SPACE // 2, PLANES, 8, 128), f32),
            vmem((PLANES, 8, 128), f32),
            vmem((PLANES, 8, 128), f32),
            vmem((2, 16, 128), bf16),
            vmem((2, 16, 128), bf16),
            vmem((OWNERS, 2, 16, 128), bf16),
            vmem((OWNERS, 2, 16, 128), bf16),
            dma((CHUNKS, 2, 2)),
            dma((8,)),
            dma((CHUNKS, 2, 2)),
            dma((2, 4, CHUNKS)),
            dma((2, 4, CHUNKS)),
            pltpu.SemaphoreType.REGULAR((5,)),
            dma((OWNERS,)),
            dma((BAND,)),
            dma((SPACE // 2,)),
            dma((SPACE // 2,)),
            dma((2,)),
            dma((BAND,)),
            dma((OWNERS,)),
            dma((BAND,)),
            dma((OWNERS,)),
        ],
        compiler_params=pltpu.CompilerParams(
            collective_id=0, has_side_effects=True, vmem_limit_bytes=62 * 2**20
        ),
    )(
        jnp.transpose(orbitals, (0, 2, 1, 3)),
        potential,
        occupations,
        jnp.asarray(band_matrix()),
        jnp.asarray(forward),
        jnp.asarray(inverse),
        jnp.asarray(green),
    )
    prop, dens, hart = pl.pallas_call(
        settle,
        out_shape=[jax.ShapeDtypeStruct(r.shape, r.dtype) for r in raw],
        in_specs=[anywhere] * 3,
        out_specs=[anywhere] * 3,
        scratch_shapes=[vmem(r.shape, r.dtype) for r in raw] + [dma((8,)), dma((8,))],
        compiler_params=pltpu.CompilerParams(vmem_limit_bytes=62 * 2**20),
    )(*raw)
    return jnp.transpose(prop, (0, 2, 1, 3)), dens, hart


def solution(mesh):
    in_specs = (P(None, "band", "space", None), P("space", None), P("band"))
    out_specs = (P(None, "band", "space", None), P("space", None), P("space", None))
    return jax.shard_map(
        per_device, mesh=mesh, in_specs=in_specs, out_specs=out_specs, check_vma=False
    )
```
